32 devices in a mesh: parts: 2 (over y), row: 8 (over z, x), col: 2 (over core).
Axes of the slice: x: 2, y: 2, z: 4, core: 2. Of those that a mesh axis runs over, the one named last changes fastest.
Arguments:
- values: bfloat16 [16, 46, 128, 128], P(('parts', 'row'), 'col'), parts along dimension 0, as said below
- block_rows: int32 [16, 46], P(('parts', 'row'), 'col'), parts along dimension 0, may hold values from 0 to 23, as said below
- block_cols: int32 [16, 46], P(('parts', 'row'), 'col'), parts along dimension 0, may hold values from 0 to 23, as said below
- counts: int32 [16, 2], P(('parts', 'row'), 'col'), parts along dimension 0, may hold values from 1 to 23, as said below
Outputs:
- product: float32 [16, 46, 128, 128], P(('parts', 'row'), 'col'), parts along dimension 0
The draws below stay inside these ranges and needn't reach their ends.
There are 2 independent parts, one for each index of `parts`. The reference program is written for one: setup_inputs(seed, part) draws one part's arguments, and reference() takes and returns one part's arrays. A program takes and returns all parts, laid end to end along the dimension named above; each array names one. Nothing has to cross between parts.
Inputs may be any that keep to these rules, and one draw needn't show every extreme that they name: `block_rows`: slots below a device's count hold global block rows of that device's panel, rows 3 r to 3 r + 2; later slots hold 0. `block_cols`: slots below a device's count hold block columns whose parity is the device's col index and whose cyclic distance from the slot's row is at most 7; no position appears twice; the stored pattern and X are symmetric (block (J, I) is the transpose of block (I, J)); later slots hold 0. `counts`: the number of used slots of each device; some device is full. `values`: blocks in unused slots are zero.
All inputs are finite; a program needn't handle non-finite values.
Results may differ from the reference program's by a relative error of at most 0.0003.
Values may be sent and summed in bfloat16 or wider, within the bound.
No kernel may reach another device: no remote copies, remote signals or barrier semaphores. Data moves between devices by JAX's collectives and lax.ppermute only.
A program may use at most 128 MiB of HBM per device.

```python
import jax
import jax.numpy as jnp
from jax import lax

BLK = 128
BR = 3
HB = 7
SLOTS = 23
N_ROW = 8
N_COL = 2


def pattern_lists(key):
    nblocks = BR * N_ROW
    coins = jax.random.randint(jax.random.fold_in(key, 11), (nblocks, HB), 0, 10)
    panel_full = 2 * jax.random.randint(jax.random.fold_in(key, 12), (), 0, N_ROW // 2)
    offsets = jnp.arange(-HB, HB + 1, dtype=jnp.int32)
    row_ids = jnp.arange(nblocks, dtype=jnp.int32)[:, None]
    col_ids = (row_ids + offsets[None, :]) % nblocks
    low_ids = jnp.where(offsets[None, :] > 0, row_ids, col_ids)
    distance = jnp.abs(offsets)[None, :] + 0 * row_ids
    chosen = coins[low_ids, jnp.clip(distance - 1, 0, HB - 1)] < 7
    forced = (row_ids // BR == panel_full) & (col_ids % 2 == 1) | (col_ids // BR == panel_full) & (row_ids % 2 == 1)
    present = (distance == 0) | chosen | forced
    width_all = BR * (2 * HB + 1)
    present = present.reshape(N_ROW, 1, width_all)
    rows_all = jnp.broadcast_to(row_ids, (nblocks, 2 * HB + 1)).reshape(N_ROW, 1, width_all)
    cols_all = col_ids.reshape(N_ROW, 1, width_all)
    parity = jnp.arange(N_COL, dtype=jnp.int32)[None, :, None]
    keep_mask = present & (cols_all % 2 == parity)
    places = jnp.cumsum(keep_mask.astype(jnp.int32), axis=-1) - 1
    places = jnp.where(keep_mask, places, SLOTS)
    rows_all = jnp.broadcast_to(rows_all, keep_mask.shape)
    cols_all = jnp.broadcast_to(cols_all, keep_mask.shape)

    def pack_one(place_vec, entry_vec):
        return jnp.zeros((SLOTS,), jnp.int32).at[place_vec].set(entry_vec, mode='drop')
    packer = jax.vmap(jax.vmap(pack_one))
    out_rows = packer(places, rows_all).reshape(N_ROW, N_COL * SLOTS)
    out_cols = packer(places, cols_all).reshape(N_ROW, N_COL * SLOTS)
    out_counts = jnp.sum(keep_mask.astype(jnp.int32), axis=-1)
    return (out_rows, out_cols, out_counts)


def draw_block_rows(key, part):
    lists = pattern_lists(key)
    return lists[0].astype(jnp.int32)


def draw_block_cols(key, part):
    lists = pattern_lists(key)
    return lists[1].astype(jnp.int32)


def draw_counts(key, part):
    lists = pattern_lists(key)
    return lists[2].astype(jnp.int32)


def draw_values(key, part):
    lists = pattern_lists(key)
    key = jax.random.fold_in(key, 4)
    nblocks = BR * N_ROW
    flat_rows = lists[0].reshape(-1)
    flat_cols = lists[1].reshape(-1)
    slot_ids = jnp.arange(N_COL * SLOTS, dtype=jnp.int32)
    valid = ((slot_ids % SLOTS)[None, :] < jnp.repeat(lists[2], SLOTS, axis=1)).reshape(-1)
    pair_ids = jnp.minimum(flat_rows, flat_cols) * nblocks + jnp.maximum(flat_rows, flat_cols)
    sub_keys = jax.vmap(lambda pair: jax.random.fold_in(key, pair))(pair_ids)
    noise = jax.vmap(lambda sub: jax.random.normal(sub, (BLK, BLK), jnp.float32))(sub_keys)
    flipped = jnp.swapaxes(noise, 1, 2)
    eye_block = jnp.eye(BLK, dtype=jnp.float32)[None]
    upper = (flat_rows < flat_cols)[:, None, None]
    lower = (flat_rows > flat_cols)[:, None, None]
    diagonal = 0.7071 * (noise + flipped) + 3.3 * eye_block
    blocks = jnp.where(upper, noise, jnp.where(lower, flipped, diagonal)) * 0.15
    blocks = jnp.where(valid[:, None, None], blocks, 0.0)
    return blocks.reshape(N_ROW, N_COL * SLOTS, BLK, BLK).astype(jnp.bfloat16)


def setup_inputs(seed: int = 0, part: int = 0) -> dict:
    key_of = jax.random.split(jax.random.key(seed), 5)
    part_keys = jax.random.split(jax.random.fold_in(key_of[4], part), 5)
    values = draw_values(jax.random.fold_in(jax.random.fold_in(key_of[4], part), 71), part)
    block_rows = draw_block_rows(jax.random.fold_in(jax.random.fold_in(key_of[4], part), 71), part)
    block_cols = draw_block_cols(jax.random.fold_in(jax.random.fold_in(key_of[4], part), 71), part)
    counts = draw_counts(jax.random.fold_in(jax.random.fold_in(key_of[4], part), 71), part)
    return {"values": values, "block_rows": block_rows, "block_cols": block_cols, "counts": counts}


def reference(values, block_rows, block_cols, counts):
    nblocks = BR * N_ROW
    flat_rows = block_rows.reshape(-1).astype(jnp.int32)
    flat_cols = block_cols.reshape(-1).astype(jnp.int32)
    slot_ids = jnp.arange(N_COL * SLOTS, dtype=jnp.int32)
    limits = jnp.repeat(counts, SLOTS, axis=1)
    valid = ((slot_ids % SLOTS)[None, :] < limits).reshape(-1)
    blocks = values.reshape(-1, BLK, BLK)
    total_slots = blocks.shape[0]
    target_ids = jnp.where(valid, flat_rows * nblocks + flat_cols, nblocks * nblocks)
    table_flat = jnp.full((nblocks * nblocks,), -1, jnp.int32)
    table_flat = table_flat.at[target_ids].set(jnp.arange(total_slots, dtype=jnp.int32), mode="drop")
    table_full = table_flat.reshape(nblocks, nblocks)
    safe_rows = jnp.where(valid, flat_rows, 0)
    safe_cols = jnp.where(valid, flat_cols, 0)

    def one_offset(running, offset):
        middle = (safe_rows + offset) % nblocks
        left_idx = table_full[safe_rows, middle]
        right_idx = table_full[middle, safe_cols]
        keep_mask = (left_idx >= 0) & (right_idx >= 0) & valid
        left_blocks = jnp.where(keep_mask[:, None, None], blocks[jnp.maximum(left_idx, 0)].astype(jnp.float32), jnp.float32(0.0))
        right_blocks = jnp.where(keep_mask[:, None, None], blocks[jnp.maximum(right_idx, 0)].astype(jnp.float32), jnp.float32(0.0))
        return running + jnp.einsum("sab,sbc->sac", left_blocks, right_blocks), None

    start = jnp.zeros((total_slots, BLK, BLK), jnp.float32)
    running, unused = lax.scan(one_offset, start, jnp.arange(-HB, HB + 1, dtype=jnp.int32))
    return running.reshape(values.shape)
```

```python
import functools

import jax
import jax.numpy as jnp
from jax import lax
from jax.experimental import pallas as pl
from jax.experimental.pallas import tpu as pltpu
from jax.sharding import PartitionSpec as P

BLK = 128
BR = 3
HB = 7
WIDTH = 2 * HB + 1
LOW, HIGH = -HB, BR - 1 + HB
NCOL = 9

CROSS = {
    (1, 0): [(3, -4), (3, -2), (5, -2), (4, -2)],
    (1, 1): [(3, -3)],
    (-1, 0): [(-1, 6), (-1, 4), (-3, 4)],
    (-1, 1): [(-1, 5), (-1, 3)],
}
SIZES = {1: 12, -1: 12, 2: 5, -2: 5, 3: 1, -3: 1}


def sent_positions(distance, parity):
    rows = [3 * distance + i for i in range(BR)]
    found = []
    for k in rows:
        for j in range(LOW, HIGH + 1):
            if j % 2 != parity or not LOW <= k <= HIGH:
                continue
            if (distance > 0 and j >= k) or (distance < 0 and j <= k):
                found.append((k, j))
    found += CROSS.get((distance, parity), [])
    return found


def own_parity():
    return (lax.axis_index("row") + lax.axis_index("col")) % 2


def first_column(parity):
    return LOW if parity == 1 else LOW + 1


def slot_position(rows_ref, cols_ref, slot, panel, nblocks):
    row = rows_ref[0, slot] - panel * BR
    band = cols_ref[0, slot] - rows_ref[0, slot] + HB
    band = jnp.where(band < 0, band + nblocks, band)
    band = jnp.where(band >= nblocks, band - nblocks, band)
    return row, band


def pack_kernel(nblocks, slots, rows_ref, cols_ref, counts_ref, values_ref, *rest):
    out_refs = dict(zip((1, -1, 2, -2, 3, -3), rest[:6]))
    left_ref, held, table, sem = rest[6:]
    panel = lax.axis_index("row")
    parity = own_parity()
    load = pltpu.make_async_copy(values_ref.at[0], held.at[pl.ds(0, slots)], sem)
    load.start()
    held[slots] = jnp.zeros((BLK, BLK), held.dtype)
    for i in range(BR * WIDTH + 1):
        table[i] = slots
    count = counts_ref[0, 0]
    for m in range(slots):
        row, band = slot_position(rows_ref, cols_ref, m, panel, nblocks)
        table[jnp.where(m < count, row * WIDTH + band, BR * WIDTH)] = m
    load.wait()

    for mine in (0, 1):

        @pl.when(parity == mine)
        def _(mine=mine):
            for distance, ref in out_refs.items():
                wanted = sent_positions(distance, (mine + distance) % 2)
                for n in range(SIZES[distance]):
                    if n < len(wanted):
                        k, j = wanted[n]
                        at = (k - 3 * distance) * WIDTH + j - k + HB
                        ref[n] = held[table[at]]
                    else:
                        ref[n] = jnp.zeros((BLK, BLK), ref.dtype)
            for i in range(BR):
                for n in range(NCOL):
                    j = first_column(mine) + 2 * n
                    rows, cols = pl.ds(i * BLK, BLK), pl.ds(n * BLK, BLK)
                    if abs(j - i) <= HB:
                        left_ref[rows, cols] = held[table[i * WIDTH + j - i + HB]]
                    else:
                        left_ref[rows, cols] = jnp.zeros((BLK, BLK), left_ref.dtype)


def find_block(parity, k, j):
    if abs(k - j) > HB:
        return None
    if 0 <= k < BR:
        return ("left", parity == j % 2), (k, (j - first_column(j % 2)) // 2), False
    if 0 <= j < BR:
        return ("left", parity == k % 2), (j, (k - first_column(k % 2)) // 2), True
    for a, b, flip in ((k, j, False), (j, k, True)):
        for distance in SIZES:
            wanted = sent_positions(distance, b % 2)
            if (a, b) in wanted:
                return (distance, parity == b % 2), wanted.index((a, b)), flip
    raise AssertionError((k, j))


def multiply_kernel(nblocks, slots, rows_ref, cols_ref, counts_ref, *rest):
    names = [("left", True), ("left", False)]
    names += [(d, own) for own in (True, False) for d in (1, -1, 2, -2)]
    names += [(3, True), (-3, True)]
    refs = dict(zip(names, rest[: len(names)]))
    out_ref, right, made, sems = rest[len(names) :]
    panel = lax.axis_index("row")
    parity = own_parity()
    zero = jnp.zeros((BLK, BLK), right.dtype)
    made[BR * NCOL] = jnp.zeros((BLK, BLK), made.dtype)

    def read(source, place):
        if source[0] == "left":
            i, n = place
            return refs[source][pl.ds(i * BLK, BLK), pl.ds(n * BLK, BLK)]
        return refs[source][place]

    def one_parity(mine):
        columns = [j for j in range(LOW, HIGH + 1) if j % 2 == mine]
        for pair in range(0, len(columns), 2):
            js = columns[pair : pair + 2]
            total = None
            for own in (True, False):
                kind = mine if own else 1 - mine
                ks = [
                    k
                    for k in range(max(LOW, js[0] - HB), min(HIGH, js[-1] + HB) + 1)
                    if k % 2 == kind
                ]
                side = 0 if own else 1
                for x, k in enumerate(ks):
                    for y, j in enumerate(js):
                        found = find_block(mine, k, j)
                        if found is None:
                            block = zero
                        else:
                            source, place, flip = found
                            block = read(source, place)
                            block = block.T if flip else block
                        right[pair // 2, side, pl.ds(x * BLK, BLK), pl.ds(y * BLK, BLK)] = block
                n0 = (ks[0] - first_column(kind)) // 2
                part = jnp.dot(
                    refs[("left", own)][:, pl.ds(n0 * BLK, len(ks) * BLK)],
                    right[pair // 2, side, pl.ds(0, len(ks) * BLK), pl.ds(0, len(js) * BLK)],
                    preferred_element_type=jnp.float32,
                )
                total = part if total is None else total + part
            for i in range(BR):
                for y in range(len(js)):
                    made[i * NCOL + pair + y] = total[i * BLK : (i + 1) * BLK, y * BLK : (y + 1) * BLK]

    for mine in (0, 1):
        pl.when(parity == mine)(functools.partial(one_parity, mine))

    count = counts_ref[0, 0]
    copies = []
    for m in range(slots):
        row, band = slot_position(rows_ref, cols_ref, m, panel, nblocks)
        at = jnp.where(m < count, row * NCOL + (row + band) // 2, BR * NCOL)
        copy = pltpu.make_async_copy(made.at[at], out_ref.at[0, m], sems.at[m])
        copy.start()
        copies.append(copy)
    for copy in copies:
        copy.wait()


def local(values, block_rows, block_cols, counts):
    slots = values.shape[1]
    row_count, col_count = lax.axis_size("row"), lax.axis_size("col")
    nblocks = BR * row_count
    smem = pl.BlockSpec(memory_space=pltpu.SMEM)
    vmem = pl.BlockSpec(memory_space=pltpu.VMEM)
    hbm = pl.BlockSpec(memory_space=pl.ANY)
    order = (1, -1, 2, -2, 3, -3)
    packed = pl.pallas_call(
        functools.partial(pack_kernel, nblocks, slots),
        out_shape=[jax.ShapeDtypeStruct((SIZES[d], BLK, BLK), values.dtype) for d in order]
        + [jax.ShapeDtypeStruct((BR * BLK, NCOL * BLK), values.dtype)],
        in_specs=[smem, smem, smem, hbm],
        out_specs=[vmem] * 7,
        scratch_shapes=[
            pltpu.VMEM((slots + 1, BLK, BLK), values.dtype),
            pltpu.SMEM((BR * WIDTH + 1,), jnp.int32),
            pltpu.SemaphoreType.DMA,
        ],
        name="pack",
    )(block_rows, block_cols, counts, values)
    messages, left = dict(zip(order, packed[:6])), packed[6]

    def towards(distance):
        pairs = []
        for r in range(row_count):
            for c in range(col_count):
                if abs(distance) == 3 and (r + c) % 2 == 0:
                    continue
                pairs.append((((r + distance) % row_count) * col_count + c, r * col_count + c))
        return lax.ppermute(messages[distance], ("row", "col"), pairs)

    def swapped(block):
        return lax.ppermute(block, "col", [(0, 1), (1, 0)])

    got = {d: towards(d) for d in order}
    other = {d: swapped(got[d]) for d in (1, -1, 2, -2)}
    left_other = swapped(left)
    return pl.pallas_call(
        functools.partial(multiply_kernel, nblocks, slots),
        out_shape=jax.ShapeDtypeStruct(values.shape, jnp.float32),
        in_specs=[smem, smem, smem] + [vmem] * 12,
        out_specs=hbm,
        scratch_shapes=[
            pltpu.VMEM((5, 2, 8 * BLK, 2 * BLK), values.dtype),
            pltpu.VMEM((BR * NCOL + 1, BLK, BLK), jnp.float32),
            pltpu.SemaphoreType.DMA((slots,)),
        ],
        compiler_params=pltpu.CompilerParams(vmem_limit_bytes=32 * 2**20),
        name="multiply",
    )(
        block_rows, block_cols, counts, left, left_other,
        *[got[d] for d in (1, -1, 2, -2)], *[other[d] for d in (1, -1, 2, -2)], got[3], got[-3],
    )


def solution(mesh):
    return jax.shard_map(
        local,
        mesh=mesh,
        in_specs=(
            P(("parts", "row"), "col", None, None),
            P(("parts", "row"), "col"),
            P(("parts", "row"), "col"),
            P(("parts", "row"), "col"),
        ),
        out_specs=P(("parts", "row"), "col", None, None),
        check_vma=False,
    )
```

```python
import functools

import jax
import jax.numpy as jnp
from jax import lax
from jax.experimental import pallas as pl
from jax.experimental.pallas import tpu as pltpu
from jax.sharding import PartitionSpec as P

BLK = 128
BR = 3
HB = 7
WIDTH = 2 * HB + 1
LOW, HIGH = -HB, BR - 1 + HB
NCOL = 9
INNER = 6

CROSS = {
    (1, 0): [(3, -4), (3, -2), (5, -2), (4, -2)],
    (1, 1): [(3, -3), (4, -3)],
    (-1, 0): [(-1, 6), (-1, 4)],
    (-1, 1): [(-1, 5), (-1, 3)],
}
SIZES = {-1: 12, 1: 12, -2: 5, 2: 5, -3: 1, 3: 1}
STAGED = 17
VMEM_LIMIT = 12 * 2**20


def sent_positions(distance, parity):
    rows = [3 * distance + i for i in range(BR)]
    found = []
    for k in rows:
        for j in range(LOW, HIGH + 1):
            if j % 2 != parity or not LOW <= k <= HIGH:
                continue
            if (distance > 0 and j >= k) or (distance < 0 and j <= k):
                found.append((k, j))
    found += CROSS.get((distance, parity), [])
    assert len(found) <= SIZES[distance]
    return found


def staged_positions(parity):
    found = []
    for distance in SIZES:
        for n, (k, j) in enumerate(sent_positions(distance, parity)):
            if k % 2 != parity:
                found.append((distance, n, (k, j)))
    assert len(found) <= STAGED
    return found


def columns_of(parity):
    return [j for j in range(LOW, HIGH + 1) if j % 2 == parity]


def own_parity():
    return (lax.axis_index("row") + lax.axis_index("col")) % 2


def for_own_parity(body):
    parity = own_parity()
    for mine in (0, 1):
        pl.when(parity == mine)(functools.partial(body, mine))


def slot_position(rows_ref, cols_ref, slot, panel, nblocks):
    row = rows_ref[0, slot] - panel * BR
    band = cols_ref[0, slot] - rows_ref[0, slot] + HB
    band = jnp.where(band < 0, band + nblocks, band)
    band = jnp.where(band >= nblocks, band - nblocks, band)
    return row, band


def index_copies(hbm_refs, smem_refs, sems):
    return [pltpu.make_async_copy(a, b, sems.at[i]) for i, (a, b) in enumerate(zip(hbm_refs, smem_refs))]


def load_slots(nblocks, slots, index_refs, values_ref, held, table, index, sems, value_sem):
    load = pltpu.make_async_copy(values_ref.at[0], held.at[pl.ds(0, slots)], value_sem)
    load.start()
    copies = index_copies(index_refs, index, sems)
    for copy in copies:
        copy.start()
    held[slots] = jnp.zeros((BLK, BLK), held.dtype)
    for i in range(BR * WIDTH + 1):
        table[i] = slots
    for copy in copies:
        copy.wait()
    panel = lax.axis_index("row")
    for m in reversed(range(slots)):
        row, band = slot_position(*index, m, panel, nblocks)
        table[jnp.where(row >= 0, row * WIDTH + band, BR * WIDTH)] = m
    load.wait()


def pack_kernel(nblocks, slots, rows_ref, cols_ref, values_ref, *rest):
    out_refs = dict(zip(SIZES, rest[:6]))
    left_ref, held, table, *index, sems, value_sem = rest[6:]
    load_slots(nblocks, slots, (rows_ref, cols_ref), values_ref, held, table, index, sems, value_sem)

    @for_own_parity
    def _(mine):
        for distance, ref in out_refs.items():
            wanted = sent_positions(distance, (mine + distance) % 2)
            for n in range(SIZES[distance]):
                if n < len(wanted):
                    k, j = wanted[n]
                    ref[n] = held[table[(k - 3 * distance) * WIDTH + j - k + HB]]
                else:
                    ref[n] = jnp.zeros((BLK, BLK), ref.dtype)
        columns = columns_of(mine)
        for i in range(BR):
            for n in range(NCOL):
                rows, cols = pl.ds(i * BLK, BLK), pl.ds(n * BLK, BLK)
                if n < len(columns) and abs(columns[n] - i) <= HB:
                    left_ref[rows, cols] = held[table[i * WIDTH + columns[n] - i + HB]]
                else:
                    left_ref[rows, cols] = jnp.zeros((BLK, BLK), left_ref.dtype)


def find_block(parity, k, j):
    if abs(k - j) > HB:
        return None
    if 0 <= k < BR:
        return ("left", parity == j % 2), (k, columns_of(j % 2).index(j)), False
    if 0 <= j < BR:
        return ("left", parity == k % 2), (j, columns_of(k % 2).index(k)), True
    for a, b, flip in ((k, j, False), (j, k, True)):
        for distance in SIZES:
            wanted = sent_positions(distance, b % 2)
            if (a, b) in wanted:
                if b % 2 == parity:
                    return distance, wanted.index((a, b)), flip
                staged = [position for _, _, position in staged_positions(1 - parity)]
                return "staged", staged.index((a, b)), flip
    raise AssertionError((k, j))


def columns_product(refs, right, parity, js):
    total = None
    for own in (True, False):
        kind = parity if own else 1 - parity
        ks = [k for k in columns_of(kind) if js[0] - HB <= k <= js[-1] + HB]
        for x, k in enumerate(ks):
            for y, j in enumerate(js):
                found = find_block(parity, k, j)
                if found is None:
                    block = jnp.zeros((BLK, BLK), right.dtype)
                else:
                    source, place, flip = found
                    if isinstance(place, tuple):
                        block = refs[source][pl.ds(place[0] * BLK, BLK), pl.ds(place[1] * BLK, BLK)]
                    else:
                        block = refs[source][place]
                    block = block.T if flip else block
                right[0 if own else 1, pl.ds(x * BLK, BLK), pl.ds(y * BLK, BLK)] = block
        start = columns_of(kind).index(ks[0])
        part = jnp.dot(
            refs[("left", own)][:, pl.ds(start * BLK, len(ks) * BLK)],
            right[0 if own else 1, pl.ds(0, len(ks) * BLK), pl.ds(0, len(js) * BLK)],
            preferred_element_type=jnp.float32,
        )
        total = part if total is None else total + part
    return total


def inner_kernel(left_ref, left_other_ref, made_ref, right):
    refs = {("left", True): left_ref, ("left", False): left_other_ref}

    @for_own_parity
    def _(mine):
        js = [j for j in columns_of(mine) if 0 <= j < BR]
        total = columns_product(refs, right, mine, js)
        for i in range(BR):
            for y in range(len(js)):
                made_ref[i * 2 + y] = total[i * BLK : (i + 1) * BLK, y * BLK : (y + 1) * BLK]
        if len(js) == 1:
            for i in range(BR):
                made_ref[i * 2 + 1] = jnp.zeros((BLK, BLK), made_ref.dtype)


def stage_kernel(*refs):
    got = dict(zip(SIZES, refs[:4]))
    out_ref = refs[4]

    @for_own_parity
    def _(mine):
        staged = staged_positions(mine)
        for n in range(STAGED):
            if n < len(staged):
                distance, place, _ = staged[n]
                out_ref[n] = got[distance][place]
            else:
                out_ref[n] = jnp.zeros((BLK, BLK), out_ref.dtype)


def multiply_kernel(nblocks, slots, rows_ref, cols_ref, counts_ref, *rest):
    names = [("left", True), ("left", False), *SIZES, "staged"]
    refs = dict(zip(names, rest[: len(names)]))
    inner_ref, out_ref, right, made, zero, slot_of, *index, sems, out_sems = rest[len(names) :]
    copies = index_copies((rows_ref, cols_ref), index, sems)
    for copy in copies:
        copy.start()
    zero[...] = jnp.zeros((BLK, BLK), zero.dtype)
    for i in range(BR * NCOL + 1):
        slot_of[i] = -1
    for copy in copies:
        copy.wait()
    panel = lax.axis_index("row")
    count = counts_ref[0, 0]
    for m in range(slots):
        row, band = slot_position(*index, m, panel, nblocks)
        slot_of[jnp.where(m < count, row * NCOL + (row + band) // 2, BR * NCOL)] = m

        @pl.when(m >= count)
        def _(m=m):
            pltpu.make_async_copy(zero, out_ref.at[0, m], out_sems.at[m]).start()

    def store(block, place):
        slot = slot_of[place]

        @pl.when(slot >= 0)
        def _():
            pltpu.make_async_copy(block, out_ref.at[0, slot], out_sems.at[slot]).start()

    @for_own_parity
    def _(mine):
        columns = columns_of(mine)
        inner = [j for j in columns if 0 <= j < BR]
        for i in range(BR):
            for y, j in enumerate(inner):
                store(inner_ref.at[i * 2 + y], i * NCOL + columns.index(j))
        outer = [j for j in columns if j not in inner]
        for pair in range(0, len(outer), 2):
            js = outer[pair : pair + 2]
            total = columns_product(refs, right.at[pair // 2], mine, js)
            for i in range(BR):
                for y, j in enumerate(js):
                    if abs(i - j) <= HB:
                        place = i * NCOL + columns.index(j)
                        made[place] = total[i * BLK : (i + 1) * BLK, y * BLK : (y + 1) * BLK]
                        store(made.at[place], place)

    for m in range(slots):
        pltpu.make_async_copy(zero, out_ref.at[0, m], out_sems.at[m]).wait()


def local(values, block_rows, block_cols, counts):
    slots = values.shape[1]
    row_count, col_count = lax.axis_size("row"), lax.axis_size("col")
    nblocks = BR * row_count
    smem = pl.BlockSpec(memory_space=pltpu.SMEM)
    vmem = pl.BlockSpec(memory_space=pltpu.VMEM)
    hbm = pl.BlockSpec(memory_space=pltpu.HBM)
    params = pltpu.CompilerParams(vmem_limit_bytes=VMEM_LIMIT)
    values, *places = (pltpu.with_memory_space_constraint(x, pltpu.HBM) for x in (values, block_rows, block_cols))
    index_scratch = [
        pltpu.SMEM((1, slots), jnp.int32),
        pltpu.SMEM((1, slots), jnp.int32),
        pltpu.SemaphoreType.DMA((2,)),
    ]
    def blocks(count, dtype=values.dtype):
        return jax.ShapeDtypeStruct((count, BLK, BLK), dtype)

    def cost(flops, nbytes):
        return pl.CostEstimate(flops=flops, bytes_accessed=nbytes, transcendentals=0)

    *packed, left = pl.pallas_call(
        functools.partial(pack_kernel, nblocks, slots),
        out_shape=[blocks(n) for n in SIZES.values()]
        + [jax.ShapeDtypeStruct((BR * BLK, NCOL * BLK), values.dtype)],
        in_specs=[hbm] * 3,
        out_specs=[vmem] * 7,
        scratch_shapes=[
            pltpu.VMEM((slots + 1, BLK, BLK), values.dtype),
            pltpu.SMEM((BR * WIDTH + 1,), jnp.int32),
            *index_scratch,
            pltpu.SemaphoreType.DMA,
        ],
        compiler_params=params,
        name="pack",
    )(*places, values)
    def towards(distance, message):
        pairs = []
        for r in range(row_count):
            for c in range(col_count):
                if abs(distance) == 3 and (r + c) % 2 == 0:
                    continue
                pairs.append((((r + distance) % row_count) * col_count + c, r * col_count + c))
        return lax.ppermute(message, ("row", "col"), pairs)

    def swapped(block):
        return lax.ppermute(block, "col", [(0, 1), (1, 0)])

    got = [towards(distance, message) for distance, message in zip(SIZES, packed)]
    left_other = swapped(left)
    inner = pl.pallas_call(
        inner_kernel,
        out_shape=blocks(INNER, jnp.float32),
        in_specs=[vmem] * 2,
        out_specs=vmem,
        scratch_shapes=[pltpu.VMEM((2, 9 * BLK, 2 * BLK), values.dtype)],
        compiler_params=params,
        cost_estimate=cost(2 * 3 * 2 * 17 * BLK**3, 4 * values.size * 2),
        name="inner",
    )(left, left_other)
    got = list(lax.optimization_barrier((*got, inner)))
    inner = got.pop()
    staged = swapped(
        pl.pallas_call(
            stage_kernel,
            out_shape=blocks(STAGED),
            in_specs=[vmem] * 4,
            out_specs=vmem,
            compiler_params=params,
            name="stage",
        )(*got[:4])
    )
    return pl.pallas_call(
        functools.partial(multiply_kernel, nblocks, slots),
        out_shape=jax.ShapeDtypeStruct(values.shape, jnp.float32),
        in_specs=[hbm] * 2 + [smem] + [vmem] * 10,
        out_specs=hbm,
        scratch_shapes=[
            pltpu.VMEM((4, 2, 9 * BLK, 2 * BLK), values.dtype),
            pltpu.VMEM((BR * NCOL, BLK, BLK), jnp.float32),
            pltpu.VMEM((BLK, BLK), jnp.float32),
            pltpu.SMEM((BR * NCOL + 1,), jnp.int32),
            *index_scratch,
            pltpu.SemaphoreType.DMA((slots,)),
        ],
        compiler_params=params,
        name="multiply",
    )(*places, counts, left, left_other, *got, staged, inner)


def solution(mesh):
    return jax.shard_map(
        local,
        mesh=mesh,
        in_specs=(
            P(("parts", "row"), "col", None, None),
            P(("parts", "row"), "col"),
            P(("parts", "row"), "col"),
            P(("parts", "row"), "col"),
        ),
        out_specs=P(("parts", "row"), "col", None, None),
        check_vma=False,
    )
```

```python
import functools

import jax
import jax.numpy as jnp
from jax import lax
from jax.experimental import pallas as pl
from jax.experimental.pallas import tpu as pltpu
from jax.sharding import PartitionSpec as P

BLK = 128
BR = 3
HB = 7
WIDTH = 2 * HB + 1
LOW, HIGH = -HB, BR - 1 + HB
NCOL = 9
INNER = 6
PLACES = 32
VMEM_LIMIT = 12 * 2**20

DISTANCES = {"a": 1, "b": -1, "c": -2, "d": 2, "e": None}
SENT = {
    ("a", 1): [(3, 3), (5, 5), (3, 5), (3, 7), (4, 7), (5, 7), (3, 9), (4, 9), (5, 9), (3, -3), (3, -1), (4, -3), (5, -1)],
    ("a", 0): [(4, 4), (3, 4), (5, 4), (3, 6), (4, 6), (5, 6), (3, 8), (4, 8), (5, 8), (3, -2), (4, -2), (5, -2), (3, -4)],
    ("b", 1): [(-1, -1), (-3, -3), (-1, -3), (-1, -7), (-2, -7), (-3, -7)],
    ("b", 0): [(-2, -2), (-1, -2), (-3, -2), (-1, 4), (-1, -4), (-1, -6)],
    ("c", 1): [(-5, -5), (-4, -7), (-5, -7), (-6, -7), (-4, -3), (-5, -1), (-5, -3), (-6, -3)],
    ("c", 0): [(-4, -4), (-6, -6), (-4, -6), (-4, -2), (-5, -2), (-6, -2), (-5, -4), (-5, -6)],
    ("d", 1): [(6, 9), (7, 7), (7, 9), (8, 9), (6, -1)],
    ("d", 0): [(6, 6), (6, 8), (8, 8), (7, 6), (7, 8)],
    ("e", 1): [(9, 9)],
    ("e", 0): [(-7, -7)],
}
SIZES = {name: len(SENT[name, 1]) for name in DISTANCES}
STAGED = {
    parity: [
        (name, n, (k, j))
        for name in DISTANCES
        for n, (k, j) in enumerate(SENT[name, parity])
        if k % 2 != j % 2 or (k, j) == (-7, -7)
    ]
    for parity in (0, 1)
}
STAGED_SIZE = max(len(found) for found in STAGED.values())


def columns_of(parity):
    return [j for j in range(LOW, HIGH + 1) if j % 2 == parity]


def own_parity():
    return (lax.axis_index("row") + lax.axis_index("col")) % 2


def for_own_parity(body):
    parity = own_parity()
    for mine in (0, 1):
        pl.when(parity == mine)(functools.partial(body, mine))


def slot_position(rows_ref, cols_ref, slot, nblocks):
    panel = lax.axis_index("row")
    row = rows_ref[0, slot] - panel * BR
    band = cols_ref[0, slot] - rows_ref[0, slot] + HB
    band = jnp.where(band < 0, band + nblocks, band)
    band = jnp.where(band >= nblocks, band - nblocks, band)
    odd = panel % 2 == 1
    return row, jnp.where(odd, BR - 1 - row, row), jnp.where(odd, WIDTH - 1 - band, band)


def index_copies(hbm_refs, smem_refs, sems):
    return [pltpu.make_async_copy(a, b, sems.at[i]) for i, (a, b) in enumerate(zip(hbm_refs, smem_refs))]


def pack_kernel(nblocks, slots, rows_ref, cols_ref, values_ref, *rest):
    out_refs = dict(zip("abcd", rest[:4]))
    left_ref, held, table, *index, sems, value_sem = rest[4:]
    load = pltpu.make_async_copy(values_ref.at[0], held.at[pl.ds(0, slots)], value_sem)
    load.start()
    copies = index_copies((rows_ref, cols_ref), index, sems)
    for copy in copies:
        copy.start()
    held[slots] = jnp.zeros((BLK, BLK), held.dtype)
    for i in range(BR * WIDTH + 1):
        table[i] = slots
    for copy in copies:
        copy.wait()
    for m in reversed(range(slots)):
        real_row, row, band = slot_position(*index, m, nblocks)
        table[jnp.where(real_row >= 0, row * WIDTH + band, BR * WIDTH)] = m
    load.wait()

    @for_own_parity
    def _(mine):
        for name, ref in out_refs.items():
            distance = DISTANCES[name]
            for n, (k, j) in enumerate(SENT[name, (mine + distance) % 2]):
                at = (k - BR * distance) * WIDTH + j - k + HB
                if distance % 2 == 1:
                    at = BR * WIDTH - 1 - at
                ref[n] = held[table[at]]
        columns = columns_of(mine)
        for i in range(BR):
            for n in range(NCOL):
                rows, cols = pl.ds(i * BLK, BLK), pl.ds(n * BLK, BLK)
                if n < len(columns) and abs(columns[n] - i) <= HB:
                    left_ref[rows, cols] = held[table[i * WIDTH + columns[n] - i + HB]]
                else:
                    left_ref[rows, cols] = jnp.zeros((BLK, BLK), left_ref.dtype)


def find_block(parity, k, j):
    if abs(k - j) > HB:
        return None
    if 0 <= k < BR:
        return ("left", parity == j % 2), (k, columns_of(j % 2).index(j)), False
    if 0 <= j < BR:
        return ("left", parity == k % 2), (j, columns_of(k % 2).index(k)), True
    for a, b, flip in ((k, j, False), (j, k, True)):
        for name in DISTANCES:
            if (a, b) in SENT[name, parity]:
                return name, SENT[name, parity].index((a, b)), flip
        staged = [position for _, _, position in STAGED[1 - parity]]
        if (a, b) in staged:
            return "staged", staged.index((a, b)), flip
    raise AssertionError((k, j))


def columns_product(refs, right, parity, js, wanted):
    total = None
    for own in (True, False):
        kind = parity if own else 1 - parity
        found = {}
        for k in columns_of(kind):
            for j in js:
                place = find_block(parity, k, j)
                if place is not None and wanted(place[0]):
                    found[k, j] = place
        if not found:
            continue
        first, last = min(k for k, _ in found), max(k for k, _ in found)
        ks = [k for k in columns_of(kind) if first <= k <= last]
        side = right.at[0 if own else 1]
        for x, k in enumerate(ks):
            for y, j in enumerate(js):
                if (k, j) in found:
                    source, place, flip = found[k, j]
                    if isinstance(place, tuple):
                        block = refs[source][pl.ds(place[0] * BLK, BLK), pl.ds(place[1] * BLK, BLK)]
                    else:
                        block = refs[source][place]
                    block = block.T if flip else block
                else:
                    block = jnp.zeros((BLK, BLK), right.dtype)
                side[pl.ds(x * BLK, BLK), pl.ds(y * BLK, BLK)] = block
        start = columns_of(kind).index(first)
        part = jnp.dot(
            refs["left", own][:, pl.ds(start * BLK, len(ks) * BLK)],
            side[pl.ds(0, len(ks) * BLK), pl.ds(0, len(js) * BLK)],
            preferred_element_type=jnp.float32,
        )
        total = part if total is None else total + part
    return total


def block_of(total, i, y):
    return total[i * BLK : (i + 1) * BLK, y * BLK : (y + 1) * BLK]


def outer_pairs(parity):
    outer = [j for j in columns_of(parity) if not 0 <= j < BR]
    return [outer[n : n + 2] for n in range(0, len(outer), 2)]


def inner_kernel(nblocks, slots, rows_ref, cols_ref, counts_ref, left_ref, left_other_ref, *rest):
    made_ref, message_ref, table_ref, right, table, *index, sems, table_sem = rest
    copies = index_copies((rows_ref, cols_ref), index, sems)
    for copy in copies:
        copy.start()
    refs = {("left", True): left_ref, ("left", False): left_other_ref}

    @for_own_parity
    def _(mine):
        js = [j for j in columns_of(mine) if 0 <= j < BR]
        total = columns_product(refs, right, mine, js, lambda source: True)
        for i in range(BR):
            for y in range(2):
                made_ref[i * 2 + y] = block_of(total, i, y) if y < len(js) else jnp.zeros((BLK, BLK), made_ref.dtype)
        i = 2 if mine == 0 else 0
        n = columns_of(0).index(i)
        message_ref[0] = refs["left", mine == 0][pl.ds(i * BLK, BLK), pl.ds(n * BLK, BLK)]

    for i in range(BR * NCOL + 1):
        table[0, i] = -1
    for copy in copies:
        copy.wait()
    count = counts_ref[0, 0]
    for m in range(slots):
        _, row, band = slot_position(*index, m, nblocks)
        place = jnp.where(m < count, row * NCOL + (row + band) // 2, BR * NCOL)
        table[0, place] = m
        table[0, PLACES + m] = place
    copy = pltpu.make_async_copy(table, table_ref, table_sem)
    copy.start()
    copy.wait()


def stage_kernel(*refs):
    got = dict(zip(DISTANCES, refs))
    out_ref = refs[-1]

    @for_own_parity
    def _(mine):
        for n, (name, place, _) in enumerate(STAGED[mine]):
            out_ref[n] = got[name][place]
        for n in range(len(STAGED[mine]), STAGED_SIZE):
            out_ref[n] = jnp.zeros((BLK, BLK), out_ref.dtype)


def outer_kernel(left_ref, left_other_ref, *rest):
    refs = {("left", True): left_ref, ("left", False): left_other_ref, **dict(zip(DISTANCES, rest))}
    out_ref, right = rest[len(DISTANCES) :]

    @for_own_parity
    def _(mine):
        for pair, js in enumerate(outer_pairs(mine)):
            total = columns_product(refs, right.at[pair], mine, js, lambda source: source != "staged")
            for i in range(BR):
                for y, j in enumerate(js):
                    if abs(i - j) <= HB:
                        out_ref[i * NCOL + columns_of(mine).index(j)] = block_of(total, i, y)


def multiply_kernel(slots, left_ref, left_other_ref, staged_ref, outer_ref, inner_ref, table_ref, out_ref, *rest):
    right, made, zero, table, table_sem, out_sems = rest
    refs = {("left", True): left_ref, ("left", False): left_other_ref, "staged": staged_ref}
    load = pltpu.make_async_copy(table_ref, table, table_sem)
    load.start()
    zero[...] = jnp.zeros((BLK, BLK), zero.dtype)
    load.wait()

    def store(block, place):
        slot = table[0, place]

        @pl.when(slot >= 0)
        def _():
            pltpu.make_async_copy(block, out_ref.at[0, slot], out_sems.at[slot]).start()

    @for_own_parity
    def _(mine):
        columns = columns_of(mine)
        for pair, js in enumerate(outer_pairs(mine)):
            total = columns_product(refs, right.at[pair], mine, js, lambda source: source == "staged")
            for i in range(BR):
                for y, j in enumerate(js):
                    if abs(i - j) <= HB:
                        place = i * NCOL + columns.index(j)
                        made[place] = outer_ref[place] + block_of(total, i, y)
                        store(made.at[place], place)
        for i in range(BR):
            for y, j in enumerate(j for j in columns if 0 <= j < BR):
                store(inner_ref.at[i * 2 + y], i * NCOL + columns.index(j))

    for m in range(slots):

        @pl.when(table[0, PLACES + m] == BR * NCOL)
        def _(m=m):
            pltpu.make_async_copy(zero, out_ref.at[0, m], out_sems.at[m]).start()

    for m in range(slots):
        pltpu.make_async_copy(zero, out_ref.at[0, m], out_sems.at[m]).wait()


def local(values, block_rows, block_cols, counts):
    slots = values.shape[1]
    row_count, col_count = lax.axis_size("row"), lax.axis_size("col")
    nblocks = BR * row_count
    smem = pl.BlockSpec(memory_space=pltpu.SMEM)
    vmem = pl.BlockSpec(memory_space=pltpu.VMEM)
    hbm = pl.BlockSpec(memory_space=pltpu.HBM)
    params = pltpu.CompilerParams(vmem_limit_bytes=VMEM_LIMIT)
    values, *places = (pltpu.with_memory_space_constraint(x, pltpu.HBM) for x in (values, block_rows, block_cols))
    index_scratch = [
        pltpu.SMEM((1, slots), jnp.int32),
        pltpu.SMEM((1, slots), jnp.int32),
        pltpu.SemaphoreType.DMA((2,)),
    ]
    table_shape = (1, BLK)

    def blocks(count, dtype=values.dtype):
        return jax.ShapeDtypeStruct((count, BLK, BLK), dtype)

    def cost(products, nbytes):
        return pl.CostEstimate(flops=2 * products * BLK**3, bytes_accessed=nbytes, transcendentals=0)

    def right_scratch(pairs):
        return pltpu.VMEM((pairs, 2, NCOL * BLK, 2 * BLK), values.dtype)

    *packed, left = pl.pallas_call(
        functools.partial(pack_kernel, nblocks, slots),
        out_shape=[blocks(SIZES[name]) for name in "abcd"]
        + [jax.ShapeDtypeStruct((BR * BLK, NCOL * BLK), values.dtype)],
        in_specs=[hbm] * 3,
        out_specs=[vmem] * 5,
        scratch_shapes=[
            pltpu.VMEM((slots + 1, BLK, BLK), values.dtype),
            pltpu.SMEM((BR * WIDTH + 1,), jnp.int32),
            *index_scratch,
            pltpu.SemaphoreType.DMA,
        ],
        compiler_params=params,
        name="pack",
    )(*places, values)

    def towards(name, message):
        pairs = []
        for r in range(row_count):
            for c in range(col_count):
                distance = DISTANCES[name] or (3 if (r + c) % 2 == 1 else -3)
                source = (r - distance if r % 2 == 1 else r + distance) % row_count
                pairs.append((source * col_count + c, r * col_count + c))
        return lax.ppermute(message, ("row", "col"), pairs)

    def swapped(block):
        return lax.ppermute(block, "col", [(0, 1), (1, 0)])

    left_other = swapped(left)
    got = [towards(name, message) for name, message in zip("abcd", packed)]
    inner, message, table = pl.pallas_call(
        functools.partial(inner_kernel, nblocks, slots),
        out_shape=[blocks(INNER, jnp.float32), blocks(1), jax.ShapeDtypeStruct(table_shape, jnp.int32)],
        in_specs=[hbm] * 2 + [smem] + [vmem] * 2,
        out_specs=[vmem] * 3,
        scratch_shapes=[
            pltpu.VMEM((2, NCOL * BLK, 2 * BLK), values.dtype),
            pltpu.SMEM(table_shape, jnp.int32),
            *index_scratch,
            pltpu.SemaphoreType.DMA,
        ],
        compiler_params=params,
        cost_estimate=cost(3 * 2 * 17, 4 * values.size),
        name="inner",
    )(*places, counts, left, left_other)
    got.append(towards("e", message))
    staged = swapped(
        pl.pallas_call(
            stage_kernel,
            out_shape=blocks(STAGED_SIZE),
            in_specs=[vmem] * 5,
            out_specs=vmem,
            compiler_params=params,
            name="stage",
        )(*got)
    )
    outer = pl.pallas_call(
        outer_kernel,
        out_shape=blocks(BR * NCOL, jnp.float32),
        in_specs=[vmem] * 7,
        out_specs=vmem,
        scratch_shapes=[right_scratch(4)],
        compiler_params=params,
        cost_estimate=cost(3 * 2 * 56, 10 * values.size),
        name="outer",
    )(left, left_other, *got)
    return pl.pallas_call(
        functools.partial(multiply_kernel, slots),
        out_shape=jax.ShapeDtypeStruct(values.shape, jnp.float32),
        in_specs=[vmem] * 6,
        out_specs=hbm,
        scratch_shapes=[
            right_scratch(4),
            pltpu.VMEM((BR * NCOL, BLK, BLK), jnp.float32),
            pltpu.VMEM((BLK, BLK), jnp.float32),
            pltpu.SMEM(table_shape, jnp.int32),
            pltpu.SemaphoreType.DMA,
            pltpu.SemaphoreType.DMA((slots,)),
        ],
        compiler_params=params,
        name="multiply",
    )(left, left_other, staged, outer, inner, table)


def solution(mesh):
    return jax.shard_map(
        local,
        mesh=mesh,
        in_specs=(
            P(("parts", "row"), "col", None, None),
            P(("parts", "row"), "col"),
            P(("parts", "row"), "col"),
            P(("parts", "row"), "col"),
        ),
        out_specs=P(("parts", "row"), "col", None, None),
        check_vma=False,
    )
```

```python
import functools

import jax
import jax.numpy as jnp
from jax import lax
from jax.experimental import pallas as pl
from jax.experimental.pallas import tpu as pltpu
from jax.sharding import PartitionSpec as P

BLK = 128
BR = 3
HB = 7
WIDTH = 2 * HB + 1
LOW, HIGH = -HB, BR - 1 + HB
NCOL = 9
INNER = 6
PLACES = 32
VMEM_LIMIT = 12 * 2**20

DISTANCES = {"a": 1, "b": -1, "c": -2, "d": 2, "e": None}
SENT = {
    ("a", 1): [(3, 3), (5, 5), (3, 5), (3, 9), (4, 9), (5, 9), (3, -3), (3, -1), (4, -3), (4, -1), (5, -1)],
    ("a", 0): [(4, 4), (3, 4), (5, 4), (3, 6), (4, 6), (5, 6), (3, 8), (5, 8), (3, -2), (5, -2), (3, -4)],
    ("b", 1): [(-1, -1), (-3, -3), (-1, -3), (-1, -7), (-2, -7), (-3, -7), (-2, -5)],
    ("b", 0): [(-2, -2), (-1, -2), (-3, -2), (-2, 4), (-1, -4), (-1, -6), (-3, -6)],
    ("c", 1): [(-5, -5), (-4, -7), (-5, -7), (-6, -7), (-5, -1), (-5, -3), (-4, -3)],
    ("c", 0): [(-4, -4), (-6, -6), (-4, -6), (-5, -4), (-5, -6), (-4, -2), (-6, -2)],
    ("d", 1): [(7, 7), (6, 9), (7, 9), (8, 9), (6, -1), (7, 3), (7, 5)],
    ("d", 0): [(6, 6), (8, 8), (6, 8), (7, 6), (7, 8), (7, 4), (8, 4)],
    ("e", 1): [(9, 9)],
    ("e", 0): [(-7, -7)],
}
PERMUTES = ("a", "f", "g", "b", "e")
SIZES = {name: len(SENT[name, 1]) for name in DISTANCES}
SIZES["f"] = SIZES["g"] = SIZES["c"]
STAGED = {
    parity: [
        (name, n, (k, j))
        for name in DISTANCES
        for n, (k, j) in enumerate(SENT[name, parity])
        if k % 2 != j % 2 or (k, j) == (-7, -7)
    ]
    for parity in (0, 1)
}
STAGED_SIZE = max(len(found) for found in STAGED.values())


def columns_of(parity):
    return [j for j in range(LOW, HIGH + 1) if j % 2 == parity]


def own_parity():
    return (lax.axis_index("row") + lax.axis_index("col")) % 2


def for_own_parity(body):
    parity = own_parity()
    for mine in (0, 1):
        pl.when(parity == mine)(functools.partial(body, mine))


def received_c_first():
    place = lax.axis_index("row") % 4
    return (place == 1) | (place == 2)


def slot_position(rows_ref, cols_ref, slot, nblocks):
    panel = lax.axis_index("row")
    row = rows_ref[0, slot] - panel * BR
    band = cols_ref[0, slot] - rows_ref[0, slot] + HB
    band = jnp.where(band < 0, band + nblocks, band)
    band = jnp.where(band >= nblocks, band - nblocks, band)
    odd = panel % 2 == 1
    return row, jnp.where(odd, BR - 1 - row, row), jnp.where(odd, WIDTH - 1 - band, band)


def index_copies(hbm_refs, smem_refs, sems):
    return [pltpu.make_async_copy(a, b, sems.at[i]) for i, (a, b) in enumerate(zip(hbm_refs, smem_refs))]


def position_at_sender(name, k, j):
    distance = DISTANCES[name]
    row, col = k - BR * distance, j - BR * distance
    return (BR - 1 - row, BR - 1 - col) if distance % 2 == 1 else (row, col)


def pack_kernel(nblocks, slots, rows_ref, cols_ref, values_ref, *rest):
    a_ref, f_ref, g_ref, b_ref, left_ref, held, table, *index, sems, value_sem = rest
    load = pltpu.make_async_copy(values_ref.at[0], held.at[pl.ds(0, slots)], value_sem)
    load.start()
    copies = index_copies((rows_ref, cols_ref), index, sems)
    for copy in copies:
        copy.start()
    held[slots] = jnp.zeros((BLK, BLK), held.dtype)
    for i in range(BR * WIDTH + 1):
        table[i] = slots
    for copy in copies:
        copy.wait()
    for m in reversed(range(slots)):
        real_row, row, band = slot_position(*index, m, nblocks)
        table[jnp.where(real_row >= 0, row * WIDTH + band, BR * WIDTH)] = m
    load.wait()
    sends_c_in_f = ~received_c_first()

    def table_place(name, k, j):
        row, col = position_at_sender(name, k, j)
        return row * WIDTH + col - row + HB

    @for_own_parity
    def _(mine):
        for name, ref in (("a", a_ref), ("b", b_ref)):
            for n, (k, j) in enumerate(SENT[name, 1 - mine]):
                ref[n] = held[table[table_place(name, k, j)]]
        for n in range(SIZES["f"]):
            c, d = (table_place(name, *SENT[name, mine][n]) for name in "cd")
            f_ref[n] = held[table[jnp.where(sends_c_in_f, c, d)]]
            g_ref[n] = held[table[jnp.where(sends_c_in_f, d, c)]]
        columns = columns_of(mine)
        for i in range(BR):
            for n in range(NCOL):
                rows, cols = pl.ds(i * BLK, BLK), pl.ds(n * BLK, BLK)
                if n < len(columns) and abs(columns[n] - i) <= HB:
                    left_ref[rows, cols] = held[table[i * WIDTH + columns[n] - i + HB]]
                else:
                    left_ref[rows, cols] = jnp.zeros((BLK, BLK), left_ref.dtype)


def pack_e_kernel(left_ref, left_other_ref, e_ref):
    @for_own_parity
    def _(mine):
        i = 2 if mine == 0 else 0
        n = columns_of(0).index(i)
        e_ref[0] = (left_ref if mine == 0 else left_other_ref)[pl.ds(i * BLK, BLK), pl.ds(n * BLK, BLK)]


def find_block(parity, k, j):
    if abs(k - j) > HB:
        return None
    if 0 <= k < BR:
        return ("left", parity == j % 2), (k, columns_of(j % 2).index(j)), False
    if 0 <= j < BR:
        return ("left", parity == k % 2), (j, columns_of(k % 2).index(k)), True
    for a, b, flip in ((k, j, False), (j, k, True)):
        for name in DISTANCES:
            if (a, b) in SENT[name, parity]:
                return name, SENT[name, parity].index((a, b)), flip
        staged = [position for _, _, position in STAGED[1 - parity]]
        if (a, b) in staged:
            return "staged", staged.index((a, b)), flip
    raise AssertionError((k, j))


def read_block(refs, source, place):
    if isinstance(place, tuple):
        return refs[source][pl.ds(place[0] * BLK, BLK), pl.ds(place[1] * BLK, BLK)]
    if source in ("c", "d"):
        f, g = refs["f"][place], refs["g"][place]
        return jnp.where(received_c_first(), *((f, g) if source == "c" else (g, f)))
    return refs[source][place]


def columns_product(refs, right, parity, js, wanted):
    total = None
    for own in (True, False):
        kind = parity if own else 1 - parity
        found = {}
        for k in columns_of(kind):
            for j in js:
                place = find_block(parity, k, j)
                if place is not None and wanted(place[0]):
                    found[k, j] = place
        if not found:
            continue
        first, last = min(k for k, _ in found), max(k for k, _ in found)
        ks = [k for k in columns_of(kind) if first <= k <= last]
        side = right.at[0 if own else 1]
        for x, k in enumerate(ks):
            for y, j in enumerate(js):
                if (k, j) in found:
                    source, place, flip = found[k, j]
                    block = read_block(refs, source, place)
                    block = block.T if flip else block
                else:
                    block = jnp.zeros((BLK, BLK), right.dtype)
                side[pl.ds(x * BLK, BLK), pl.ds(y * BLK, BLK)] = block
        start = columns_of(kind).index(first)
        part = jnp.dot(
            refs["left", own][:, pl.ds(start * BLK, len(ks) * BLK)],
            side[pl.ds(0, len(ks) * BLK), pl.ds(0, len(js) * BLK)],
            preferred_element_type=jnp.float32,
        )
        total = part if total is None else total + part
    return total


def block_of(total, i, y):
    return total[i * BLK : (i + 1) * BLK, y * BLK : (y + 1) * BLK]


def outer_pairs(parity):
    outer = [j for j in columns_of(parity) if not 0 <= j < BR]
    return [outer[n : n + 2] for n in range(0, len(outer), 2)]


def inner_kernel(nblocks, slots, rows_ref, cols_ref, counts_ref, left_ref, left_other_ref, *rest):
    made_ref, table_ref, right, table, *index, sems, table_sem = rest
    copies = index_copies((rows_ref, cols_ref), index, sems)
    for copy in copies:
        copy.start()
    refs = {("left", True): left_ref, ("left", False): left_other_ref}

    @for_own_parity
    def _(mine):
        js = [j for j in columns_of(mine) if 0 <= j < BR]
        total = columns_product(refs, right, mine, js, lambda source: True)
        for i in range(BR):
            for y in range(2):
                made_ref[i * 2 + y] = block_of(total, i, y) if y < len(js) else jnp.zeros((BLK, BLK), made_ref.dtype)

    for i in range(BR * NCOL + 1):
        table[0, i] = -1
    for copy in copies:
        copy.wait()
    count = counts_ref[0, 0]
    for m in range(slots):
        _, row, band = slot_position(*index, m, nblocks)
        place = jnp.where(m < count, row * NCOL + (row + band) // 2, BR * NCOL)
        table[0, place] = m
        table[0, PLACES + m] = place
    copy = pltpu.make_async_copy(table, table_ref, table_sem)
    copy.start()
    copy.wait()


def stage_kernel(*refs):
    got = dict(zip(PERMUTES, refs))
    out_ref = refs[-1]

    @for_own_parity
    def _(mine):
        for n, (name, place, _) in enumerate(STAGED[mine]):
            out_ref[n] = read_block(got, name, place)
        for n in range(len(STAGED[mine]), STAGED_SIZE):
            out_ref[n] = jnp.zeros((BLK, BLK), out_ref.dtype)


def outer_kernel(left_ref, left_other_ref, *rest):
    refs = {("left", True): left_ref, ("left", False): left_other_ref, **dict(zip(PERMUTES, rest))}
    out_ref, right = rest[len(PERMUTES) :]

    @for_own_parity
    def _(mine):
        for pair, js in enumerate(outer_pairs(mine)):
            total = columns_product(refs, right.at[pair], mine, js, lambda source: source != "staged")
            for i in range(BR):
                for y, j in enumerate(js):
                    if abs(i - j) <= HB:
                        out_ref[i * NCOL + columns_of(mine).index(j)] = block_of(total, i, y)


def multiply_kernel(slots, left_ref, left_other_ref, staged_ref, outer_ref, inner_ref, table_ref, out_ref, *rest):
    right, made, zero, table, table_sem, out_sems = rest
    refs = {("left", True): left_ref, ("left", False): left_other_ref, "staged": staged_ref}
    load = pltpu.make_async_copy(table_ref, table, table_sem)
    load.start()
    zero[...] = jnp.zeros((BLK, BLK), zero.dtype)
    load.wait()

    def store(block, place):
        slot = table[0, place]

        @pl.when(slot >= 0)
        def _():
            pltpu.make_async_copy(block, out_ref.at[0, slot], out_sems.at[slot]).start()

    @for_own_parity
    def _(mine):
        columns = columns_of(mine)
        for pair, js in enumerate(outer_pairs(mine)):
            total = columns_product(refs, right.at[pair], mine, js, lambda source: source == "staged")
            for i in range(BR):
                for y, j in enumerate(js):
                    if abs(i - j) <= HB:
                        place = i * NCOL + columns.index(j)
                        made[place] = outer_ref[place] + block_of(total, i, y)
                        store(made.at[place], place)
        for i in range(BR):
            for y, j in enumerate(j for j in columns if 0 <= j < BR):
                store(inner_ref.at[i * 2 + y], i * NCOL + columns.index(j))

    for m in range(slots):

        @pl.when(table[0, PLACES + m] == BR * NCOL)
        def _(m=m):
            pltpu.make_async_copy(zero, out_ref.at[0, m], out_sems.at[m]).start()

    for m in range(slots):
        pltpu.make_async_copy(zero, out_ref.at[0, m], out_sems.at[m]).wait()


def local(values, block_rows, block_cols, counts):
    slots = values.shape[1]
    row_count, col_count = lax.axis_size("row"), lax.axis_size("col")
    nblocks = BR * row_count
    smem = pl.BlockSpec(memory_space=pltpu.SMEM)
    vmem = pl.BlockSpec(memory_space=pltpu.VMEM)
    hbm = pl.BlockSpec(memory_space=pltpu.HBM)
    params = pltpu.CompilerParams(vmem_limit_bytes=VMEM_LIMIT)
    values, *places = (pltpu.with_memory_space_constraint(x, pltpu.HBM) for x in (values, block_rows, block_cols))
    index_scratch = [
        pltpu.SMEM((1, slots), jnp.int32),
        pltpu.SMEM((1, slots), jnp.int32),
        pltpu.SemaphoreType.DMA((2,)),
    ]
    table_shape = (1, BLK)

    def blocks(count, dtype=values.dtype):
        return jax.ShapeDtypeStruct((count, BLK, BLK), dtype)

    def cost(products, nbytes):
        return pl.CostEstimate(flops=2 * products * BLK**3, bytes_accessed=nbytes, transcendentals=0)

    def right_scratch(pairs):
        return pltpu.VMEM((pairs, 2, NCOL * BLK, 2 * BLK), values.dtype)

    *packed, left = pl.pallas_call(
        functools.partial(pack_kernel, nblocks, slots),
        out_shape=[blocks(SIZES[name]) for name in "afgb"]
        + [jax.ShapeDtypeStruct((BR * BLK, NCOL * BLK), values.dtype)],
        in_specs=[hbm] * 3,
        out_specs=[vmem] * 5,
        scratch_shapes=[
            pltpu.VMEM((slots + 1, BLK, BLK), values.dtype),
            pltpu.SMEM((BR * WIDTH + 1,), jnp.int32),
            *index_scratch,
            pltpu.SemaphoreType.DMA,
        ],
        compiler_params=params,
        name="pack",
    )(*places, values)

    def towards(name, message):
        pairs = []
        for r in range(row_count):
            for c in range(col_count):
                if name == "f":
                    distance = 2 if r % 4 < 2 else -2
                elif name == "g":
                    distance = -2 if r % 4 < 2 else 2
                else:
                    distance = DISTANCES[name] or (3 if (r + c) % 2 == 1 else -3)
                    distance = -distance if r % 2 == 1 else distance
                pairs.append(((r + distance) % row_count * col_count + c, r * col_count + c))
        return lax.ppermute(message, ("row", "col"), pairs)

    def swapped(block):
        return lax.ppermute(block, "col", [(0, 1), (1, 0)])

    left_other = swapped(left)
    message_e = pl.pallas_call(
        pack_e_kernel,
        out_shape=blocks(SIZES["e"]),
        in_specs=[vmem] * 2,
        out_specs=vmem,
        compiler_params=params,
        name="pack_e",
    )(left, left_other)
    got = [towards(name, message) for name, message in zip(PERMUTES, (*packed, message_e))]
    inner, table = pl.pallas_call(
        functools.partial(inner_kernel, nblocks, slots),
        out_shape=[blocks(INNER, jnp.float32), jax.ShapeDtypeStruct(table_shape, jnp.int32)],
        in_specs=[hbm] * 2 + [smem] + [vmem] * 2,
        out_specs=[vmem] * 2,
        scratch_shapes=[
            pltpu.VMEM((2, NCOL * BLK, 2 * BLK), values.dtype),
            pltpu.SMEM(table_shape, jnp.int32),
            *index_scratch,
            pltpu.SemaphoreType.DMA,
        ],
        compiler_params=params,
        cost_estimate=cost(3 * 2 * 17, 4 * values.size),
        name="inner",
    )(*places, counts, left, left_other)
    *got, inner = lax.optimization_barrier((*got, inner))
    staged = swapped(
        pl.pallas_call(
            stage_kernel,
            out_shape=blocks(STAGED_SIZE),
            in_specs=[vmem] * 5,
            out_specs=vmem,
            compiler_params=params,
            name="stage",
        )(*got)
    )
    outer = pl.pallas_call(
        outer_kernel,
        out_shape=blocks(BR * NCOL, jnp.float32),
        in_specs=[vmem] * 7,
        out_specs=vmem,
        scratch_shapes=[right_scratch(4)],
        compiler_params=params,
        cost_estimate=cost(3 * 2 * 56, 10 * values.size),
        name="outer",
    )(left, left_other, *got)
    return pl.pallas_call(
        functools.partial(multiply_kernel, slots),
        out_shape=jax.ShapeDtypeStruct(values.shape, jnp.float32),
        in_specs=[vmem] * 6,
        out_specs=hbm,
        scratch_shapes=[
            right_scratch(4),
            pltpu.VMEM((BR * NCOL, BLK, BLK), jnp.float32),
            pltpu.VMEM((BLK, BLK), jnp.float32),
            pltpu.SMEM(table_shape, jnp.int32),
            pltpu.SemaphoreType.DMA,
            pltpu.SemaphoreType.DMA((slots,)),
        ],
        compiler_params=params,
        name="multiply",
    )(left, left_other, staged, outer, inner, table)


def solution(mesh):
    return jax.shard_map(
        local,
        mesh=mesh,
        in_specs=(
            P(("parts", "row"), "col", None, None),
            P(("parts", "row"), "col"),
            P(("parts", "row"), "col"),
            P(("parts", "row"), "col"),
        ),
        out_specs=P(("parts", "row"), "col", None, None),
        check_vma=False,
    )
```

```python
import functools

import jax
import jax.numpy as jnp
from jax import lax
from jax.experimental import pallas as pl
from jax.experimental.pallas import tpu as pltpu
from jax.sharding import PartitionSpec as P

BLK = 128
BR = 3
HB = 7
WIDTH = 2 * HB + 1
LOW, HIGH = -HB, BR - 1 + HB
NCOL = 9
INNER = 6
PLACES = 32
VMEM_LIMIT = 12 * 2**20

DISTANCES = {"a": 1, "c": -2, "d": 2, "w": 1, "e": None}
SENT = {
    ("a", 1): [(3, 3), (5, 5), (3, 5), (3, 7), (4, 7), (5, 7), (3, 9), (4, 9), (5, 9), (3, -3), (3, -1), (4, -3), (5, -1)],
    ("a", 0): [(4, 4), (3, 4), (5, 4), (3, 6), (4, 6), (5, 6), (3, 8), (4, 8), (5, 8), (3, -2), (4, -2), (5, -2), (3, -4)],
    ("c", 1): [(-5, -5), (-4, -7), (-5, -7), (-6, -7), (-5, -1), (-5, -3), (-6, -1), (-6, -3)],
    ("c", 0): [(-4, -4), (-6, -6), (-4, -6), (-5, -4), (-5, -6), (-5, -2), (-6, -2)],
    ("d", 1): [(7, 7), (6, 7), (6, 9), (7, 9), (8, 9), (6, -1), (6, 1)],
    ("d", 0): [(6, 6), (8, 8), (6, 8), (7, 8), (6, 12), (7, 12), (8, 12)],
    ("e", 1): [(9, 9)],
    ("e", 0): [(-7, -7)],
}
for parity in (0, 1):
    SENT["w", parity] = [(5 - k, 5 - j) for k, j in SENT["d", 1 - parity]]
SIZES = {name: max(len(SENT[name, parity]) for parity in (0, 1)) for name in DISTANCES}


def outside(k, j):
    return all(LOW <= w <= HIGH and not 0 <= w < BR for w in (k, j))


def needed_by_other_core(parity):
    there = [{k, j} for name in DISTANCES for k, j in SENT[name, 1 - parity]]
    return [
        (name, n, (k, j))
        for name in DISTANCES
        for n, (k, j) in enumerate(SENT[name, parity])
        if outside(k, j) and (k % 2 != j % 2 and {k, j} not in there or (k, j) == (-7, -7))
    ]


STAGED = {parity: needed_by_other_core(parity) for parity in (0, 1)}
STAGED_SIZE = max(len(found) for found in STAGED.values())


def columns_of(parity):
    return [j for j in range(LOW, HIGH + 1) if j % 2 == parity]


def own_parity():
    return (lax.axis_index("row") + lax.axis_index("col")) % 2


def for_own_parity(body):
    parity = own_parity()
    for mine in (0, 1):
        pl.when(parity == mine)(functools.partial(body, mine))


def slot_position(rows_ref, cols_ref, slot, nblocks):
    panel = lax.axis_index("row")
    row = rows_ref[0, slot] - panel * BR
    band = cols_ref[0, slot] - rows_ref[0, slot] + HB
    band = jnp.where(band < 0, band + nblocks, band)
    band = jnp.where(band >= nblocks, band - nblocks, band)
    odd = panel % 2 == 1
    return row, jnp.where(odd, BR - 1 - row, row), jnp.where(odd, WIDTH - 1 - band, band)


def index_copies(hbm_refs, smem_refs, sems):
    return [pltpu.make_async_copy(a, b, sems.at[i]) for i, (a, b) in enumerate(zip(hbm_refs, smem_refs))]


def position_at_sender(name, k, j):
    distance = DISTANCES[name]
    row, col = k - BR * distance, j - BR * distance
    return (BR - 1 - row, BR - 1 - col) if distance % 2 == 1 else (row, col)


def pack_kernel(nblocks, slots, rows_ref, cols_ref, values_ref, *rest):
    a_ref, c_ref, d_ref, left_ref, held, table, *index, sems, value_sem = rest
    load = pltpu.make_async_copy(values_ref.at[0], held.at[pl.ds(0, slots)], value_sem)
    load.start()
    copies = index_copies((rows_ref, cols_ref), index, sems)
    for copy in copies:
        copy.start()
    held[slots] = jnp.zeros((BLK, BLK), held.dtype)
    for i in range(BR * WIDTH + 1):
        table[i] = slots
    for copy in copies:
        copy.wait()
    for m in reversed(range(slots)):
        real_row, row, band = slot_position(*index, m, nblocks)
        table[jnp.where(real_row >= 0, row * WIDTH + band, BR * WIDTH)] = m
    load.wait()

    def table_place(name, k, j):
        row, col = position_at_sender(name, k, j)
        return row * WIDTH + col - row + HB

    @for_own_parity
    def _(mine):
        for name, ref in (("a", a_ref), ("c", c_ref), ("d", d_ref)):
            wanted = SENT[name, (mine + DISTANCES[name]) % 2]
            for n in range(SIZES[name]):
                if n < len(wanted):
                    ref[n] = held[table[table_place(name, *wanted[n])]]
                else:
                    ref[n] = jnp.zeros((BLK, BLK), ref.dtype)
        columns = columns_of(mine)
        for i in range(BR):
            for n in range(NCOL):
                rows, cols = pl.ds(i * BLK, BLK), pl.ds(n * BLK, BLK)
                if n < len(columns) and abs(columns[n] - i) <= HB:
                    left_ref[rows, cols] = held[table[i * WIDTH + columns[n] - i + HB]]
                else:
                    left_ref[rows, cols] = jnp.zeros((BLK, BLK), left_ref.dtype)


def pack_e_kernel(left_ref, left_other_ref, e_ref):
    @for_own_parity
    def _(mine):
        i = 2 if mine == 0 else 0
        n = columns_of(0).index(i)
        e_ref[0] = (left_ref if mine == 0 else left_other_ref)[pl.ds(i * BLK, BLK), pl.ds(n * BLK, BLK)]


def find_block(parity, k, j):
    if abs(k - j) > HB:
        return None
    if 0 <= k < BR:
        return ("left", parity == j % 2), (k, columns_of(j % 2).index(j)), False
    if 0 <= j < BR:
        return ("left", parity == k % 2), (j, columns_of(k % 2).index(k)), True
    for a, b, flip in ((k, j, False), (j, k, True)):
        for name in DISTANCES:
            if (a, b) in SENT[name, parity]:
                return name, SENT[name, parity].index((a, b)), flip
        staged = [position for _, _, position in STAGED[1 - parity]]
        if (a, b) in staged:
            return "staged", staged.index((a, b)), flip
    raise AssertionError((k, j))


def read_block(refs, source, place):
    if isinstance(place, tuple):
        return refs[source][pl.ds(place[0] * BLK, BLK), pl.ds(place[1] * BLK, BLK)]
    return refs[source][place]


def columns_product(refs, right, parity, js, wanted):
    total = None
    for own in (True, False):
        kind = parity if own else 1 - parity
        found = {}
        for k in columns_of(kind):
            for j in js:
                place = find_block(parity, k, j)
                if place is not None and wanted(place[0]):
                    found[k, j] = place
        if not found:
            continue
        first, last = min(k for k, _ in found), max(k for k, _ in found)
        ks = [k for k in columns_of(kind) if first <= k <= last]
        side = right.at[0 if own else 1]
        for x, k in enumerate(ks):
            for y, j in enumerate(js):
                if (k, j) in found:
                    source, place, flip = found[k, j]
                    block = read_block(refs, source, place)
                    block = block.T if flip else block
                else:
                    block = jnp.zeros((BLK, BLK), right.dtype)
                side[pl.ds(x * BLK, BLK), pl.ds(y * BLK, BLK)] = block
        start = columns_of(kind).index(first)
        part = jnp.dot(
            refs["left", own][:, pl.ds(start * BLK, len(ks) * BLK)],
            side[pl.ds(0, len(ks) * BLK), pl.ds(0, len(js) * BLK)],
            preferred_element_type=jnp.float32,
        )
        total = part if total is None else total + part
    return total


def block_of(total, i, y):
    return total[i * BLK : (i + 1) * BLK, y * BLK : (y + 1) * BLK]


def outer_pairs(parity):
    outer = [j for j in columns_of(parity) if not 0 <= j < BR]
    return [outer[n : n + 2] for n in range(0, len(outer), 2)]


def inner_kernel(nblocks, slots, rows_ref, cols_ref, counts_ref, left_ref, left_other_ref, *rest):
    made_ref, table_ref, right, table, *index, sems, table_sem = rest
    copies = index_copies((rows_ref, cols_ref), index, sems)
    for copy in copies:
        copy.start()
    refs = {("left", True): left_ref, ("left", False): left_other_ref}

    @for_own_parity
    def _(mine):
        js = [j for j in columns_of(mine) if 0 <= j < BR]
        total = columns_product(refs, right, mine, js, lambda source: True)
        for i in range(BR):
            for y in range(2):
                made_ref[i * 2 + y] = block_of(total, i, y) if y < len(js) else jnp.zeros((BLK, BLK), made_ref.dtype)

    for i in range(BR * NCOL + 1):
        table[0, i] = -1
    for copy in copies:
        copy.wait()
    count = counts_ref[0, 0]
    for m in range(slots):
        _, row, band = slot_position(*index, m, nblocks)
        place = jnp.where(m < count, row * NCOL + (row + band) // 2, BR * NCOL)
        table[0, place] = m
        table[0, PLACES + m] = place
    copy = pltpu.make_async_copy(table, table_ref, table_sem)
    copy.start()
    copy.wait()


def stage_kernel(*refs):
    got = dict(zip(DISTANCES, refs))
    out_ref = refs[-1]

    @for_own_parity
    def _(mine):
        for n, (name, place, _) in enumerate(STAGED[mine]):
            out_ref[n] = read_block(got, name, place)
        for n in range(len(STAGED[mine]), STAGED_SIZE):
            out_ref[n] = jnp.zeros((BLK, BLK), out_ref.dtype)


def outer_kernel(left_ref, left_other_ref, *rest):
    refs = {("left", True): left_ref, ("left", False): left_other_ref, **dict(zip(DISTANCES, rest))}
    out_ref, right = rest[len(DISTANCES) :]

    @for_own_parity
    def _(mine):
        for pair, js in enumerate(outer_pairs(mine)):
            total = columns_product(refs, right.at[pair], mine, js, lambda source: source != "staged")
            for i in range(BR):
                for y, j in enumerate(js):
                    if abs(i - j) <= HB:
                        out_ref[i * NCOL + columns_of(mine).index(j)] = block_of(total, i, y)


def multiply_kernel(slots, left_ref, left_other_ref, staged_ref, outer_ref, inner_ref, table_ref, out_ref, *rest):
    right, made, zero, table, table_sem, out_sems = rest
    refs = {("left", True): left_ref, ("left", False): left_other_ref, "staged": staged_ref}
    load = pltpu.make_async_copy(table_ref, table, table_sem)
    load.start()
    zero[...] = jnp.zeros((BLK, BLK), zero.dtype)
    load.wait()

    def store(block, place):
        slot = table[0, place]

        @pl.when(slot >= 0)
        def _():
            pltpu.make_async_copy(block, out_ref.at[0, slot], out_sems.at[slot]).start()

    @for_own_parity
    def _(mine):
        columns = columns_of(mine)
        for pair, js in enumerate(outer_pairs(mine)):
            total = columns_product(refs, right.at[pair], mine, js, lambda source: source == "staged")
            for i in range(BR):
                for y, j in enumerate(js):
                    if abs(i - j) <= HB:
                        place = i * NCOL + columns.index(j)
                        made[place] = outer_ref[place] + block_of(total, i, y)
                        store(made.at[place], place)
        for i in range(BR):
            for y, j in enumerate(j for j in columns if 0 <= j < BR):
                store(inner_ref.at[i * 2 + y], i * NCOL + columns.index(j))

    for m in range(slots):

        @pl.when(table[0, PLACES + m] == BR * NCOL)
        def _(m=m):
            pltpu.make_async_copy(zero, out_ref.at[0, m], out_sems.at[m]).start()

    for m in range(slots):
        pltpu.make_async_copy(zero, out_ref.at[0, m], out_sems.at[m]).wait()


def local(values, block_rows, block_cols, counts):
    slots = values.shape[1]
    row_count, col_count = lax.axis_size("row"), lax.axis_size("col")
    nblocks = BR * row_count
    smem = pl.BlockSpec(memory_space=pltpu.SMEM)
    vmem = pl.BlockSpec(memory_space=pltpu.VMEM)
    hbm = pl.BlockSpec(memory_space=pltpu.HBM)
    params = pltpu.CompilerParams(vmem_limit_bytes=VMEM_LIMIT)
    values, *places = (pltpu.with_memory_space_constraint(x, pltpu.HBM) for x in (values, block_rows, block_cols))
    index_scratch = [
        pltpu.SMEM((1, slots), jnp.int32),
        pltpu.SMEM((1, slots), jnp.int32),
        pltpu.SemaphoreType.DMA((2,)),
    ]
    table_shape = (1, BLK)

    def blocks(count, dtype=values.dtype):
        return jax.ShapeDtypeStruct((count, BLK, BLK), dtype)

    def cost(products, nbytes):
        return pl.CostEstimate(flops=2 * products * BLK**3, bytes_accessed=nbytes, transcendentals=0)

    def right_scratch(pairs):
        return pltpu.VMEM((pairs, 2, NCOL * BLK, 2 * BLK), values.dtype)

    *packed, left = pl.pallas_call(
        functools.partial(pack_kernel, nblocks, slots),
        out_shape=[blocks(SIZES[name]) for name in "acd"]
        + [jax.ShapeDtypeStruct((BR * BLK, NCOL * BLK), values.dtype)],
        in_specs=[hbm] * 3,
        out_specs=[vmem] * 4,
        scratch_shapes=[
            pltpu.VMEM((slots + 1, BLK, BLK), values.dtype),
            pltpu.SMEM((BR * WIDTH + 1,), jnp.int32),
            *index_scratch,
            pltpu.SemaphoreType.DMA,
        ],
        compiler_params=params,
        name="pack",
    )(*places, values)

    def towards(name, message):
        pairs = []
        for r in range(row_count):
            for c in range(col_count):
                distance = DISTANCES[name] or (3 if (r + c) % 2 == 1 else -3)
                distance = -distance if r % 2 == 1 else distance
                pairs.append(((r + distance) % row_count * col_count + c, r * col_count + c))
        return lax.ppermute(message, ("row", "col"), pairs)

    def swapped(block):
        return lax.ppermute(block, "col", [(0, 1), (1, 0)])

    left_other = swapped(left)
    message_e = pl.pallas_call(
        pack_e_kernel,
        out_shape=blocks(SIZES["e"]),
        in_specs=[vmem] * 2,
        out_specs=vmem,
        compiler_params=params,
        name="pack_e",
    )(left, left_other)
    a, c, d = (towards(name, message) for name, message in zip("acd", packed))
    got = [a, c, d, towards("w", d), towards("e", message_e)]
    inner, table = pl.pallas_call(
        functools.partial(inner_kernel, nblocks, slots),
        out_shape=[blocks(INNER, jnp.float32), jax.ShapeDtypeStruct(table_shape, jnp.int32)],
        in_specs=[hbm] * 2 + [smem] + [vmem] * 2,
        out_specs=[vmem] * 2,
        scratch_shapes=[
            pltpu.VMEM((2, NCOL * BLK, 2 * BLK), values.dtype),
            pltpu.SMEM(table_shape, jnp.int32),
            *index_scratch,
            pltpu.SemaphoreType.DMA,
        ],
        compiler_params=params,
        cost_estimate=cost(3 * 2 * 17, 4 * values.size),
        name="inner",
    )(*places, counts, left, left_other)
    *got, inner = lax.optimization_barrier((*got, inner))
    staged = swapped(
        pl.pallas_call(
            stage_kernel,
            out_shape=blocks(STAGED_SIZE),
            in_specs=[vmem] * 5,
            out_specs=vmem,
            compiler_params=params,
            name="stage",
        )(*got)
    )
    outer = pl.pallas_call(
        outer_kernel,
        out_shape=blocks(BR * NCOL, jnp.float32),
        in_specs=[vmem] * 7,
        out_specs=vmem,
        scratch_shapes=[right_scratch(4)],
        compiler_params=params,
        cost_estimate=cost(3 * 2 * 56, 10 * values.size),
        name="outer",
    )(left, left_other, *got)
    return pl.pallas_call(
        functools.partial(multiply_kernel, slots),
        out_shape=jax.ShapeDtypeStruct(values.shape, jnp.float32),
        in_specs=[vmem] * 6,
        out_specs=hbm,
        scratch_shapes=[
            right_scratch(4),
            pltpu.VMEM((BR * NCOL, BLK, BLK), jnp.float32),
            pltpu.VMEM((BLK, BLK), jnp.float32),
            pltpu.SMEM(table_shape, jnp.int32),
            pltpu.SemaphoreType.DMA,
            pltpu.SemaphoreType.DMA((slots,)),
        ],
        compiler_params=params,
        name="multiply",
    )(left, left_other, staged, outer, inner, table)


def solution(mesh):
    return jax.shard_map(
        local,
        mesh=mesh,
        in_specs=(
            P(("parts", "row"), "col", None, None),
            P(("parts", "row"), "col"),
            P(("parts", "row"), "col"),
            P(("parts", "row"), "col"),
        ),
        out_specs=P(("parts", "row"), "col", None, None),
        check_vma=False,
    )
```

```python
import functools

import jax
import jax.numpy as jnp
from jax import lax
from jax.experimental import pallas as pl
from jax.experimental.pallas import tpu as pltpu
from jax.sharding import PartitionSpec as P

BLK = 128
BR = 3
HB = 7
WIDTH = 2 * HB + 1
LOW, HIGH = -HB, BR - 1 + HB
NCOL = 9
INNER = 6
PLACES = 32
VMEM_LIMIT = 12 * 2**20

DISTANCES = {"a": 1, "b": -1, "c": -2, "d": 2, "e": None}
SENT = {
    ("a", 1): [(3, 3), (5, 5), (3, 5), (3, 7), (4, 7), (5, 7), (3, 9), (4, 9), (5, 9), (3, -3), (3, -1), (4, -3), (5, -1)],
    ("a", 0): [(4, 4), (3, 4), (5, 4), (3, 6), (4, 6), (5, 6), (3, 8), (4, 8), (5, 8), (3, -2), (4, -2), (5, -2), (3, -4)],
    ("b", 1): [(-1, -1), (-3, -3), (-1, -3), (-1, -7), (-2, -7), (-3, -7)],
    ("b", 0): [(-2, -2), (-1, -2), (-3, -2), (-1, 4), (-1, -4), (-1, -6)],
    ("c", 1): [(-5, -5), (-4, -7), (-5, -7), (-6, -7), (-4, -3), (-5, -1), (-5, -3), (-6, -3)],
    ("c", 0): [(-4, -4), (-6, -6), (-4, -6), (-4, -2), (-5, -2), (-6, -2), (-5, -4), (-5, -6)],
    ("d", 1): [(6, 9), (7, 7), (7, 9), (8, 9), (6, -1)],
    ("d", 0): [(6, 6), (6, 8), (8, 8), (7, 6), (7, 8)],
    ("e", 1): [(9, 9)],
    ("e", 0): [(-7, -7)],
}
SIZES = {name: len(SENT[name, 1]) for name in DISTANCES}
STAGED = {
    parity: [
        (name, n, (k, j))
        for name in DISTANCES
        for n, (k, j) in enumerate(SENT[name, parity])
        if k % 2 != j % 2 or (k, j) == (-7, -7)
    ]
    for parity in (0, 1)
}
STAGED_SIZE = max(len(found) for found in STAGED.values())


def columns_of(parity):
    return [j for j in range(LOW, HIGH + 1) if j % 2 == parity]


def own_parity():
    return (lax.axis_index("row") + lax.axis_index("col")) % 2


def for_own_parity(body):
    parity = own_parity()
    for mine in (0, 1):
        pl.when(parity == mine)(functools.partial(body, mine))


def slot_position(rows_ref, cols_ref, slot, nblocks):
    panel = lax.axis_index("row")
    row = rows_ref[0, slot] - panel * BR
    band = cols_ref[0, slot] - rows_ref[0, slot] + HB
    band = jnp.where(band < 0, band + nblocks, band)
    band = jnp.where(band >= nblocks, band - nblocks, band)
    odd = panel % 2 == 1
    return row, jnp.where(odd, BR - 1 - row, row), jnp.where(odd, WIDTH - 1 - band, band)


def index_copies(hbm_refs, smem_refs, sems):
    return [pltpu.make_async_copy(a, b, sems.at[i]) for i, (a, b) in enumerate(zip(hbm_refs, smem_refs))]


def pack_kernel(nblocks, slots, rows_ref, cols_ref, values_ref, *rest):
    out_refs = dict(zip("abcd", rest[:4]))
    left_ref, held, table, *index, sems, value_sem = rest[4:]
    load = pltpu.make_async_copy(values_ref.at[0], held.at[pl.ds(0, slots)], value_sem)
    load.start()
    copies = index_copies((rows_ref, cols_ref), index, sems)
    for copy in copies:
        copy.start()
    held[slots] = jnp.zeros((BLK, BLK), held.dtype)
    for i in range(BR * WIDTH + 1):
        table[i] = slots
    for copy in copies:
        copy.wait()
    for m in reversed(range(slots)):
        real_row, row, band = slot_position(*index, m, nblocks)
        table[jnp.where(real_row >= 0, row * WIDTH + band, BR * WIDTH)] = m
    load.wait()

    @for_own_parity
    def _(mine):
        for name, ref in out_refs.items():
            distance = DISTANCES[name]
            for n, (k, j) in enumerate(SENT[name, (mine + distance) % 2]):
                at = (k - BR * distance) * WIDTH + j - k + HB
                if distance % 2 == 1:
                    at = BR * WIDTH - 1 - at
                ref[n] = held[table[at]]
        columns = columns_of(mine)
        for i in range(BR):
            for n in range(NCOL):
                rows, cols = pl.ds(i * BLK, BLK), pl.ds(n * BLK, BLK)
                if n < len(columns) and abs(columns[n] - i) <= HB:
                    left_ref[rows, cols] = held[table[i * WIDTH + columns[n] - i + HB]]
                else:
                    left_ref[rows, cols] = jnp.zeros((BLK, BLK), left_ref.dtype)


def find_block(parity, k, j):
    if abs(k - j) > HB:
        return None
    if 0 <= k < BR:
        return ("left", parity == j % 2), (k, columns_of(j % 2).index(j)), False
    if 0 <= j < BR:
        return ("left", parity == k % 2), (j, columns_of(k % 2).index(k)), True
    for a, b, flip in ((k, j, False), (j, k, True)):
        for name in DISTANCES:
            if (a, b) in SENT[name, parity]:
                return name, SENT[name, parity].index((a, b)), flip
        staged = [position for _, _, position in STAGED[1 - parity]]
        if (a, b) in staged:
            return "staged", staged.index((a, b)), flip
    raise AssertionError((k, j))


def columns_product(refs, right, parity, js, wanted):
    total = None
    for own in (True, False):
        kind = parity if own else 1 - parity
        found = {}
        for k in columns_of(kind):
            for j in js:
                place = find_block(parity, k, j)
                if place is not None and wanted(place[0]):
                    found[k, j] = place
        if not found:
            continue
        first, last = min(k for k, _ in found), max(k for k, _ in found)
        ks = [k for k in columns_of(kind) if first <= k <= last]
        side = right.at[0 if own else 1]
        for x, k in enumerate(ks):
            for y, j in enumerate(js):
                if (k, j) in found:
                    source, place, flip = found[k, j]
                    if isinstance(place, tuple):
                        block = refs[source][pl.ds(place[0] * BLK, BLK), pl.ds(place[1] * BLK, BLK)]
                    else:
                        block = refs[source][place]
                    block = block.T if flip else block
                else:
                    block = jnp.zeros((BLK, BLK), right.dtype)
                side[pl.ds(x * BLK, BLK), pl.ds(y * BLK, BLK)] = block
        start = columns_of(kind).index(first)
        part = jnp.dot(
            refs["left", own][:, pl.ds(start * BLK, len(ks) * BLK)],
            side[pl.ds(0, len(ks) * BLK), pl.ds(0, len(js) * BLK)],
            preferred_element_type=jnp.float32,
        )
        total = part if total is None else total + part
    return total


def block_of(total, i, y):
    return total[i * BLK : (i + 1) * BLK, y * BLK : (y + 1) * BLK]


def outer_pairs(parity):
    outer = [j for j in columns_of(parity) if not 0 <= j < BR]
    return [outer[n : n + 2] for n in range(0, len(outer), 2)]


def inner_kernel(nblocks, slots, rows_ref, cols_ref, counts_ref, left_ref, left_other_ref, *rest):
    table_ref, out_ref, right, made, table, *index, sems, table_sem, out_sems = rest
    copies = index_copies((rows_ref, cols_ref), index, sems)
    for copy in copies:
        copy.start()
    refs = {("left", True): left_ref, ("left", False): left_other_ref}

    @for_own_parity
    def _(mine):
        js = [j for j in columns_of(mine) if 0 <= j < BR]
        total = columns_product(refs, right, mine, js, lambda source: True)
        for i in range(BR):
            for y in range(2):
                made[i * 2 + y] = block_of(total, i, y) if y < len(js) else jnp.zeros((BLK, BLK), made.dtype)

    made[INNER] = jnp.zeros((BLK, BLK), made.dtype)
    for i in range(BR * NCOL + 1):
        table[0, i] = -1
    for copy in copies:
        copy.wait()
    count = counts_ref[0, 0]
    parity = own_parity()
    first, last = jnp.where(parity == 1, 4, 3), 4
    stores = []
    for m in range(slots):
        _, row, band = slot_position(*index, m, nblocks)
        column = (row + band) // 2
        used = m < count
        place = jnp.where(used, row * NCOL + column, BR * NCOL)
        table[0, place] = m
        here = ~used | ((column >= first) & (column <= last))
        table[0, PLACES + m] = jnp.where(here, 0, 1)
        source = jnp.where(used, row * 2 + column - first, INNER)
        stores.append((here, pltpu.make_async_copy(made.at[jnp.where(here, source, 0)], out_ref.at[0, m], out_sems.at[m])))
    copy = pltpu.make_async_copy(table, table_ref, table_sem)
    copy.start()
    for here, store in stores:
        pl.when(here)(store.start)
    copy.wait()
    for here, store in stores:
        pl.when(here)(store.wait)


def pack_e_kernel(left_ref, left_other_ref, e_ref):
    @for_own_parity
    def _(mine):
        i = 2 if mine == 0 else 0
        n = columns_of(0).index(i)
        e_ref[0] = (left_ref if mine == 0 else left_other_ref)[pl.ds(i * BLK, BLK), pl.ds(n * BLK, BLK)]


def stage_kernel(*refs):
    got = dict(zip(DISTANCES, refs))
    out_ref = refs[-1]

    @for_own_parity
    def _(mine):
        for n, (name, place, _) in enumerate(STAGED[mine]):
            out_ref[n] = got[name][place]
        for n in range(len(STAGED[mine]), STAGED_SIZE):
            out_ref[n] = jnp.zeros((BLK, BLK), out_ref.dtype)


def outer_kernel(left_ref, left_other_ref, *rest):
    refs = {("left", True): left_ref, ("left", False): left_other_ref, **dict(zip(DISTANCES, rest))}
    out_ref, right = rest[len(DISTANCES) :]

    @for_own_parity
    def _(mine):
        for pair, js in enumerate(outer_pairs(mine)):
            total = columns_product(refs, right.at[pair], mine, js, lambda source: source != "staged")
            for i in range(BR):
                for y, j in enumerate(js):
                    if abs(i - j) <= HB:
                        out_ref[i * NCOL + columns_of(mine).index(j)] = block_of(total, i, y)


def multiply_kernel(slots, left_ref, left_other_ref, staged_ref, outer_ref, table_ref, _, out_ref, *rest):
    right, made, table, table_sem, out_sems = rest
    refs = {("left", True): left_ref, ("left", False): left_other_ref, "staged": staged_ref}
    load = pltpu.make_async_copy(table_ref, table, table_sem)
    load.start()

    @for_own_parity
    def _(mine):
        for pair, js in enumerate(outer_pairs(mine)):
            total = columns_product(refs, right.at[pair], mine, js, lambda source: source == "staged")
            if pair == 0:
                load.wait()
            for i in range(BR):
                for y, j in enumerate(js):
                    if abs(i - j) <= HB:
                        place = i * NCOL + columns_of(mine).index(j)
                        made[place] = outer_ref[place] + block_of(total, i, y)
                        slot = table[0, place]

                        @pl.when(slot >= 0)
                        def _(place=place, slot=slot):
                            pltpu.make_async_copy(made.at[place], out_ref.at[0, slot], out_sems.at[slot]).start()

    for m in range(slots):

        @pl.when(table[0, PLACES + m] == 1)
        def _(m=m):
            pltpu.make_async_copy(made.at[0], out_ref.at[0, m], out_sems.at[m]).wait()


def local(values, block_rows, block_cols, counts):
    slots = values.shape[1]
    row_count, col_count = lax.axis_size("row"), lax.axis_size("col")
    nblocks = BR * row_count
    smem = pl.BlockSpec(memory_space=pltpu.SMEM)
    vmem = pl.BlockSpec(memory_space=pltpu.VMEM)
    hbm = pl.BlockSpec(memory_space=pltpu.HBM)
    params = pltpu.CompilerParams(vmem_limit_bytes=VMEM_LIMIT)
    values, *places = (pltpu.with_memory_space_constraint(x, pltpu.HBM) for x in (values, block_rows, block_cols))
    index_scratch = [
        pltpu.SMEM((1, slots), jnp.int32),
        pltpu.SMEM((1, slots), jnp.int32),
        pltpu.SemaphoreType.DMA((2,)),
    ]
    table_shape = (1, BLK)

    def blocks(count, dtype=values.dtype):
        return jax.ShapeDtypeStruct((count, BLK, BLK), dtype)

    def cost(products, nbytes):
        return pl.CostEstimate(flops=2 * products * BLK**3, bytes_accessed=nbytes, transcendentals=0)

    def right_scratch(pairs):
        return pltpu.VMEM((pairs, 2, NCOL * BLK, 2 * BLK), values.dtype)

    *packed, left = pl.pallas_call(
        functools.partial(pack_kernel, nblocks, slots),
        out_shape=[blocks(SIZES[name]) for name in "abcd"]
        + [jax.ShapeDtypeStruct((BR * BLK, NCOL * BLK), values.dtype)],
        in_specs=[hbm] * 3,
        out_specs=[vmem] * 5,
        scratch_shapes=[
            pltpu.VMEM((slots + 1, BLK, BLK), values.dtype),
            pltpu.SMEM((BR * WIDTH + 1,), jnp.int32),
            *index_scratch,
            pltpu.SemaphoreType.DMA,
        ],
        compiler_params=params,
        name="pack",
    )(*places, values)

    def towards(name, message):
        pairs = []
        for r in range(row_count):
            for c in range(col_count):
                distance = DISTANCES[name] or (3 if (r + c) % 2 == 1 else -3)
                source = (r - distance if r % 2 == 1 else r + distance) % row_count
                pairs.append((source * col_count + c, r * col_count + c))
        return lax.ppermute(message, ("row", "col"), pairs)

    def swapped(block):
        return lax.ppermute(block, "col", [(0, 1), (1, 0)])

    left_other = swapped(left)
    got = [towards(name, message) for name, message in zip("abcd", packed)]
    message = pl.pallas_call(
        pack_e_kernel,
        out_shape=blocks(SIZES["e"]),
        in_specs=[vmem] * 2,
        out_specs=vmem,
        compiler_params=params,
        name="pack_e",
    )(left, left_other)
    got.append(towards("e", message))
    table, out = pl.pallas_call(
        functools.partial(inner_kernel, nblocks, slots),
        out_shape=[jax.ShapeDtypeStruct(table_shape, jnp.int32), jax.ShapeDtypeStruct(values.shape, jnp.float32)],
        in_specs=[hbm] * 2 + [smem] + [vmem] * 2,
        out_specs=[vmem, hbm],
        scratch_shapes=[
            pltpu.VMEM((2, NCOL * BLK, 2 * BLK), values.dtype),
            pltpu.VMEM((INNER + 1, BLK, BLK), jnp.float32),
            pltpu.SMEM(table_shape, jnp.int32),
            *index_scratch,
            pltpu.SemaphoreType.DMA,
            pltpu.SemaphoreType.DMA((slots,)),
        ],
        compiler_params=params,
        cost_estimate=cost(3 * 2 * 17, 4 * values.size),
        name="inner",
    )(*places, counts, left, left_other)
    *got, table = lax.optimization_barrier((*got, table))
    staged = swapped(
        pl.pallas_call(
            stage_kernel,
            out_shape=blocks(STAGED_SIZE),
            in_specs=[vmem] * 5,
            out_specs=vmem,
            compiler_params=params,
            name="stage",
        )(*got)
    )
    outer = pl.pallas_call(
        outer_kernel,
        out_shape=blocks(BR * NCOL, jnp.float32),
        in_specs=[vmem] * 7,
        out_specs=vmem,
        scratch_shapes=[right_scratch(4)],
        compiler_params=params,
        cost_estimate=cost(3 * 2 * 56, 10 * values.size),
        name="outer",
    )(left, left_other, *got)
    return pl.pallas_call(
        functools.partial(multiply_kernel, slots),
        out_shape=jax.ShapeDtypeStruct(values.shape, jnp.float32),
        in_specs=[vmem] * 5 + [hbm],
        out_specs=hbm,
        scratch_shapes=[
            right_scratch(4),
            pltpu.VMEM((BR * NCOL, BLK, BLK), jnp.float32),
            pltpu.SMEM(table_shape, jnp.int32),
            pltpu.SemaphoreType.DMA,
            pltpu.SemaphoreType.DMA((slots,)),
        ],
        input_output_aliases={5: 0},
        compiler_params=params,
        name="multiply",
    )(left, left_other, staged, outer, table, out)


def solution(mesh):
    return jax.shard_map(
        local,
        mesh=mesh,
        in_specs=(
            P(("parts", "row"), "col", None, None),
            P(("parts", "row"), "col"),
            P(("parts", "row"), "col"),
            P(("parts", "row"), "col"),
        ),
        out_specs=P(("parts", "row"), "col", None, None),
        check_vma=False,
    )
```

```python
import functools

import jax
import jax.numpy as jnp
from jax import lax
from jax.experimental import pallas as pl
from jax.experimental.pallas import tpu as pltpu
from jax.sharding import PartitionSpec as P

BLK = 128
BR = 3
HB = 7
WIDTH = 2 * HB + 1
LOW, HIGH = -HB, BR - 1 + HB
NCOL = 9
INNER = 6
CHUNK = 6
VMEM_LIMIT = 12 * 2**20

DISTANCES = {"a": 1, "b": -1, "c": -2, "d": 2, "e": None}
SENT = {
    ("a", 1): [(3, 3), (5, 5), (3, 5), (3, 7), (4, 7), (5, 7), (3, 9), (4, 9), (5, 9), (3, -3), (3, -1), (4, -3), (5, -1)],
    ("a", 0): [(4, 4), (3, 4), (5, 4), (3, 6), (4, 6), (5, 6), (3, 8), (4, 8), (5, 8), (3, -2), (4, -2), (5, -2), (3, -4)],
    ("b", 1): [(-1, -1), (-3, -3), (-1, -3), (-1, -7), (-2, -7), (-3, -7)],
    ("b", 0): [(-2, -2), (-1, -2), (-3, -2), (-1, 4), (-1, -4), (-1, -6)],
    ("c", 1): [(-5, -5), (-4, -7), (-5, -7), (-6, -7), (-4, -3), (-5, -1), (-5, -3), (-6, -3)],
    ("c", 0): [(-4, -4), (-6, -6), (-4, -6), (-4, -2), (-5, -2), (-6, -2), (-5, -4), (-5, -6)],
    ("d", 1): [(6, 9), (7, 7), (7, 9), (8, 9), (6, -1)],
    ("d", 0): [(6, 6), (6, 8), (8, 8), (7, 6), (7, 8)],
    ("e", 1): [(9, 9)],
    ("e", 0): [(-7, -7)],
}
SIZES = {name: len(SENT[name, 1]) for name in DISTANCES}
STAGED = {
    parity: [
        (name, n, (k, j))
        for name in DISTANCES
        for n, (k, j) in enumerate(SENT[name, parity])
        if k % 2 != j % 2 or (k, j) == (-7, -7)
    ]
    for parity in (0, 1)
}
STAGED_SIZE = max(len(found) for found in STAGED.values())


def columns_of(parity):
    return [j for j in range(LOW, HIGH + 1) if j % 2 == parity]


def own_parity():
    return (lax.axis_index("row") + lax.axis_index("col")) % 2


def for_own_parity(body):
    parity = own_parity()
    for mine in (0, 1):
        pl.when(parity == mine)(functools.partial(body, mine))


def slot_position(rows_ref, cols_ref, slot, nblocks):
    panel = lax.axis_index("row")
    row = rows_ref[0, slot] - panel * BR
    band = cols_ref[0, slot] - rows_ref[0, slot] + HB
    band = jnp.where(band < 0, band + nblocks, band)
    band = jnp.where(band >= nblocks, band - nblocks, band)
    odd = panel % 2 == 1
    return row, jnp.where(odd, BR - 1 - row, row), jnp.where(odd, WIDTH - 1 - band, band)


def index_copies(hbm_refs, smem_refs, sems):
    return [pltpu.make_async_copy(a, b, sems.at[i]) for i, (a, b) in enumerate(zip(hbm_refs, smem_refs))]


def pack_kernel(nblocks, slots, rows_ref, cols_ref, values_ref, *rest):
    out_refs = dict(zip("abcd", rest[:4]))
    left_ref, held, table, *index, sems, value_sems = rest[4:]
    loads = []
    for n, first in enumerate(range(0, slots, CHUNK)):
        part = pl.ds(first, min(CHUNK, slots - first))
        loads.append(pltpu.make_async_copy(values_ref.at[0, part], held.at[part], value_sems.at[n]))
        loads[-1].start()
    copies = index_copies((rows_ref, cols_ref), index, sems)
    for copy in copies:
        copy.start()
    held[slots] = jnp.zeros((BLK, BLK), held.dtype)
    for i in range(BR * WIDTH + 1):
        table[i] = slots
    for copy in copies:
        copy.wait()
    for m in reversed(range(slots)):
        real_row, row, band = slot_position(*index, m, nblocks)
        table[jnp.where(real_row >= 0, row * WIDTH + band, BR * WIDTH)] = m
    for load in loads:
        load.wait()

    @for_own_parity
    def _(mine):
        for name, ref in out_refs.items():
            distance = DISTANCES[name]
            for n, (k, j) in enumerate(SENT[name, (mine + distance) % 2]):
                at = (k - BR * distance) * WIDTH + j - k + HB
                if distance % 2 == 1:
                    at = BR * WIDTH - 1 - at
                ref[n] = held[table[at]]
        columns = columns_of(mine)
        for i in range(BR):
            for n in range(NCOL):
                rows, cols = pl.ds(i * BLK, BLK), pl.ds(n * BLK, BLK)
                if n < len(columns) and abs(columns[n] - i) <= HB:
                    left_ref[rows, cols] = held[table[i * WIDTH + columns[n] - i + HB]]
                else:
                    left_ref[rows, cols] = jnp.zeros((BLK, BLK), left_ref.dtype)


def find_block(parity, k, j):
    if abs(k - j) > HB:
        return None
    if 0 <= k < BR:
        return ("left", parity == j % 2), (k, columns_of(j % 2).index(j)), False
    if 0 <= j < BR:
        return ("left", parity == k % 2), (j, columns_of(k % 2).index(k)), True
    for a, b, flip in ((k, j, False), (j, k, True)):
        for name in DISTANCES:
            if (a, b) in SENT[name, parity]:
                return name, SENT[name, parity].index((a, b)), flip
        staged = [position for _, _, position in STAGED[1 - parity]]
        if (a, b) in staged:
            return "staged", staged.index((a, b)), flip
    raise AssertionError((k, j))


def columns_product(refs, right, parity, js, wanted):
    total = None
    for own in (True, False):
        kind = parity if own else 1 - parity
        found = {}
        for k in columns_of(kind):
            for j in js:
                place = find_block(parity, k, j)
                if place is not None and wanted(place[0]):
                    found[k, j] = place
        if not found:
            continue
        first, last = min(k for k, _ in found), max(k for k, _ in found)
        ks = [k for k in columns_of(kind) if first <= k <= last]
        side = right.at[0 if own else 1]
        for x, k in enumerate(ks):
            for y, j in enumerate(js):
                if (k, j) in found:
                    source, place, flip = found[k, j]
                    if isinstance(place, tuple):
                        block = refs[source][pl.ds(place[0] * BLK, BLK), pl.ds(place[1] * BLK, BLK)]
                    else:
                        block = refs[source][place]
                    block = block.T if flip else block
                else:
                    block = jnp.zeros((BLK, BLK), right.dtype)
                side[pl.ds(x * BLK, BLK), pl.ds(y * BLK, BLK)] = block
        start = columns_of(kind).index(first)
        part = jnp.dot(
            refs["left", own][:, pl.ds(start * BLK, len(ks) * BLK)],
            side[pl.ds(0, len(ks) * BLK), pl.ds(0, len(js) * BLK)],
            preferred_element_type=jnp.float32,
        )
        total = part if total is None else total + part
    return total


def block_of(total, i, y):
    return total[i * BLK : (i + 1) * BLK, y * BLK : (y + 1) * BLK]


def outer_pairs(parity):
    outer = [j for j in columns_of(parity) if not 0 <= j < BR]
    return [outer[n : n + 2] for n in range(0, len(outer), 2)]


def inner_kernel(nblocks, slots, rows_ref, cols_ref, counts_ref, left_ref, left_other_ref, *rest):
    made_ref, places_ref, right, places, *index, sems, places_sem = rest
    copies = index_copies((rows_ref, cols_ref), index, sems)
    for copy in copies:
        copy.start()
    refs = {("left", True): left_ref, ("left", False): left_other_ref}

    @for_own_parity
    def _(mine):
        js = [j for j in columns_of(mine) if 0 <= j < BR]
        total = columns_product(refs, right, mine, js, lambda source: True)
        for i in range(BR):
            for y in range(2):
                made_ref[i * 2 + y] = block_of(total, i, y) if y < len(js) else jnp.zeros((BLK, BLK), made_ref.dtype)

    for copy in copies:
        copy.wait()
    count = counts_ref[0, 0]
    for m in range(slots):
        _, row, band = slot_position(*index, m, nblocks)
        places[0, m] = jnp.where(m < count, row * NCOL + (row + band) // 2, BR * NCOL)
    copy = pltpu.make_async_copy(places, places_ref, places_sem)
    copy.start()
    copy.wait()


def pack_e_kernel(left_ref, left_other_ref, e_ref):
    @for_own_parity
    def _(mine):
        i = 2 if mine == 0 else 0
        n = columns_of(0).index(i)
        e_ref[0] = (left_ref if mine == 0 else left_other_ref)[pl.ds(i * BLK, BLK), pl.ds(n * BLK, BLK)]


def stage_kernel(*refs):
    got = dict(zip(DISTANCES, refs))
    out_ref = refs[-1]

    @for_own_parity
    def _(mine):
        for n, (name, place, _) in enumerate(STAGED[mine]):
            out_ref[n] = got[name][place]
        for n in range(len(STAGED[mine]), STAGED_SIZE):
            out_ref[n] = jnp.zeros((BLK, BLK), out_ref.dtype)


def outer_kernel(left_ref, left_other_ref, *rest):
    refs = {("left", True): left_ref, ("left", False): left_other_ref, **dict(zip(DISTANCES, rest))}
    out_ref, right = rest[len(DISTANCES) :]

    @for_own_parity
    def _(mine):
        for pair, js in enumerate(outer_pairs(mine)):
            total = columns_product(refs, right.at[pair], mine, js, lambda source: source != "staged")
            for i in range(BR):
                for y, j in enumerate(js):
                    if abs(i - j) <= HB:
                        out_ref[i * NCOL + columns_of(mine).index(j)] = block_of(total, i, y)


def multiply_kernel(slots, left_ref, left_other_ref, staged_ref, outer_ref, inner_ref, places_ref, out_ref, *rest):
    right, made, places, places_sem, out_sem = rest
    refs = {("left", True): left_ref, ("left", False): left_other_ref, "staged": staged_ref}
    load = pltpu.make_async_copy(places_ref, places, places_sem)
    load.start()

    @for_own_parity
    def _(mine):
        columns = columns_of(mine)
        for pair, js in enumerate(outer_pairs(mine)):
            total = columns_product(refs, right.at[pair], mine, js, lambda source: source == "staged")
            for i in range(BR):
                for y, j in enumerate(js):
                    if abs(i - j) <= HB:
                        place = i * NCOL + columns.index(j)
                        made[place] = outer_ref[place] + block_of(total, i, y)
        for i in range(BR):
            for y, j in enumerate(j for j in columns if 0 <= j < BR):
                made[i * NCOL + columns.index(j)] = inner_ref[i * 2 + y]
        made[BR * NCOL] = jnp.zeros((BLK, BLK), made.dtype)

    load.wait()
    for m in range(slots):
        pltpu.make_async_copy(made.at[places[0, m]], out_ref.at[0, m], out_sem).start()
    pltpu.make_async_copy(made.at[pl.ds(0, slots)], out_ref.at[0], out_sem).wait()


def local(values, block_rows, block_cols, counts):
    slots = values.shape[1]
    row_count, col_count = lax.axis_size("row"), lax.axis_size("col")
    nblocks = BR * row_count
    smem = pl.BlockSpec(memory_space=pltpu.SMEM)
    vmem = pl.BlockSpec(memory_space=pltpu.VMEM)
    hbm = pl.BlockSpec(memory_space=pltpu.HBM)
    params = pltpu.CompilerParams(vmem_limit_bytes=VMEM_LIMIT)
    values, *places = (pltpu.with_memory_space_constraint(x, pltpu.HBM) for x in (values, block_rows, block_cols))
    index_scratch = [
        pltpu.SMEM((1, slots), jnp.int32),
        pltpu.SMEM((1, slots), jnp.int32),
        pltpu.SemaphoreType.DMA((2,)),
    ]
    places_shape = (1, BLK)

    def blocks(count, dtype=values.dtype):
        return jax.ShapeDtypeStruct((count, BLK, BLK), dtype)

    def cost(products, nbytes):
        return pl.CostEstimate(flops=2 * products * BLK**3, bytes_accessed=nbytes, transcendentals=0)

    def right_scratch(pairs):
        return pltpu.VMEM((pairs, 2, NCOL * BLK, 2 * BLK), values.dtype)

    *packed, left = pl.pallas_call(
        functools.partial(pack_kernel, nblocks, slots),
        out_shape=[blocks(SIZES[name]) for name in "abcd"]
        + [jax.ShapeDtypeStruct((BR * BLK, NCOL * BLK), values.dtype)],
        in_specs=[hbm] * 3,
        out_specs=[vmem] * 5,
        scratch_shapes=[
            pltpu.VMEM((slots + 1, BLK, BLK), values.dtype),
            pltpu.SMEM((BR * WIDTH + 1,), jnp.int32),
            *index_scratch,
            pltpu.SemaphoreType.DMA((-(-slots // CHUNK),)),
        ],
        compiler_params=params,
        name="pack",
    )(*places, values)

    def towards(name, message):
        pairs = []
        for r in range(row_count):
            for c in range(col_count):
                distance = DISTANCES[name] or (3 if (r + c) % 2 == 1 else -3)
                source = (r - distance if r % 2 == 1 else r + distance) % row_count
                pairs.append((source * col_count + c, r * col_count + c))
        return lax.ppermute(message, ("row", "col"), pairs)

    def swapped(block):
        return lax.ppermute(block, "col", [(0, 1), (1, 0)])

    left_other = swapped(left)
    got = [towards(name, message) for name, message in zip("abcd", packed)]
    message = pl.pallas_call(
        pack_e_kernel,
        out_shape=blocks(SIZES["e"]),
        in_specs=[vmem] * 2,
        out_specs=vmem,
        compiler_params=params,
        name="pack_e",
    )(left, left_other)
    got.append(towards("e", message))
    inner, slot_places = pl.pallas_call(
        functools.partial(inner_kernel, nblocks, slots),
        out_shape=[blocks(INNER, jnp.float32), jax.ShapeDtypeStruct(places_shape, jnp.int32)],
        in_specs=[hbm] * 2 + [smem] + [vmem] * 2,
        out_specs=[vmem] * 2,
        scratch_shapes=[
            pltpu.VMEM((2, NCOL * BLK, 2 * BLK), values.dtype),
            pltpu.SMEM(places_shape, jnp.int32),
            *index_scratch,
            pltpu.SemaphoreType.DMA,
        ],
        compiler_params=params,
        cost_estimate=cost(3 * 2 * 17, 4 * values.size),
        name="inner",
    )(*places, counts, left, left_other)
    *got, inner = lax.optimization_barrier((*got, inner))
    staged = swapped(
        pl.pallas_call(
            stage_kernel,
            out_shape=blocks(STAGED_SIZE),
            in_specs=[vmem] * 5,
            out_specs=vmem,
            compiler_params=params,
            name="stage",
        )(*got)
    )
    outer = pl.pallas_call(
        outer_kernel,
        out_shape=blocks(BR * NCOL, jnp.float32),
        in_specs=[vmem] * 7,
        out_specs=vmem,
        scratch_shapes=[right_scratch(4)],
        compiler_params=params,
        cost_estimate=cost(3 * 2 * 56, 10 * values.size),
        name="outer",
    )(left, left_other, *got)
    return pl.pallas_call(
        functools.partial(multiply_kernel, slots),
        out_shape=jax.ShapeDtypeStruct(values.shape, jnp.float32),
        in_specs=[vmem] * 6,
        out_specs=hbm,
        scratch_shapes=[
            right_scratch(4),
            pltpu.VMEM((BR * NCOL + 1, BLK, BLK), jnp.float32),
            pltpu.SMEM(places_shape, jnp.int32),
            pltpu.SemaphoreType.DMA,
            pltpu.SemaphoreType.DMA,
        ],
        compiler_params=params,
        name="multiply",
    )(left, left_other, staged, outer, inner, slot_places)


def solution(mesh):
    return jax.shard_map(
        local,
        mesh=mesh,
        in_specs=(
            P(("parts", "row"), "col", None, None),
            P(("parts", "row"), "col"),
            P(("parts", "row"), "col"),
            P(("parts", "row"), "col"),
        ),
        out_specs=P(("parts", "row"), "col", None, None),
        check_vma=False,
    )
```

```python
import functools

import jax
import jax.numpy as jnp
from jax import lax
from jax.experimental import pallas as pl
from jax.experimental.pallas import tpu as pltpu
from jax.sharding import PartitionSpec as P

BLK = 128
BR = 3
HB = 7
WIDTH = 2 * HB + 1
LOW, HIGH = -HB, BR - 1 + HB
NCOL = 9
INNER = 6
VMEM_LIMIT = 12 * 2**20

DISTANCES = {"a": 1, "b": -1, "c": -2, "d": 2, "e": None}
SENT = {
    ("a", 1): [(3, 3), (5, 5), (3, 5), (3, 7), (4, 7), (5, 7), (3, 9), (4, 9), (5, 9), (3, -3), (3, -1), (4, -3), (5, -1)],
    ("a", 0): [(4, 4), (3, 4), (5, 4), (3, 6), (4, 6), (5, 6), (3, 8), (4, 8), (5, 8), (3, -2), (4, -2), (5, -2), (3, -4)],
    ("b", 1): [(-1, -1), (-3, -3), (-1, -3), (-1, -7), (-2, -7), (-3, -7)],
    ("b", 0): [(-2, -2), (-1, -2), (-3, -2), (-1, 4), (-1, -4), (-1, -6)],
    ("c", 1): [(-5, -5), (-4, -7), (-5, -7), (-6, -7), (-4, -3), (-5, -1), (-5, -3), (-6, -3)],
    ("c", 0): [(-4, -4), (-6, -6), (-4, -6), (-4, -2), (-5, -2), (-6, -2), (-5, -4), (-5, -6)],
    ("d", 1): [(6, 9), (7, 7), (7, 9), (8, 9), (6, -1)],
    ("d", 0): [(6, 6), (6, 8), (8, 8), (7, 6), (7, 8)],
    ("e", 1): [(9, 9)],
    ("e", 0): [(-7, -7)],
}
SIZES = {name: len(SENT[name, 1]) for name in DISTANCES}
STAGED = {
    parity: [
        (name, n, (k, j))
        for name in DISTANCES
        for n, (k, j) in enumerate(SENT[name, parity])
        if k % 2 != j % 2 or (k, j) == (-7, -7)
    ]
    for parity in (0, 1)
}
STAGED_SIZE = max(len(found) for found in STAGED.values())


def columns_of(parity):
    return [j for j in range(LOW, HIGH + 1) if j % 2 == parity]


def own_parity():
    return (lax.axis_index("row") + lax.axis_index("col")) % 2


def for_own_parity(body):
    parity = own_parity()
    for mine in (0, 1):
        pl.when(parity == mine)(functools.partial(body, mine))


def slot_position(rows_ref, cols_ref, slot, nblocks):
    panel = lax.axis_index("row")
    row = rows_ref[0, slot] - panel * BR
    band = cols_ref[0, slot] - rows_ref[0, slot] + HB
    band = jnp.where(band < 0, band + nblocks, band)
    band = jnp.where(band >= nblocks, band - nblocks, band)
    odd = panel % 2 == 1
    return row, jnp.where(odd, BR - 1 - row, row), jnp.where(odd, WIDTH - 1 - band, band)


def index_copies(hbm_refs, smem_refs, sems):
    return [pltpu.make_async_copy(a, b, sems.at[i]) for i, (a, b) in enumerate(zip(hbm_refs, smem_refs))]


def pack_kernel(nblocks, slots, rows_ref, cols_ref, values_ref, *rest):
    out_refs = dict(zip("abcd", rest[:4]))
    left_ref, held, table, *index, sems, value_sem = rest[4:]
    copies = index_copies((rows_ref, cols_ref), index, sems)
    load = pltpu.make_async_copy(values_ref.at[0], held.at[pl.ds(0, slots)], value_sem)
    for copy in (*copies, load):
        copy.start()
    held[slots] = jnp.zeros((BLK, BLK), held.dtype)
    for i in range(BR * WIDTH + 1):
        table[i] = slots
    for copy in copies:
        copy.wait()
    for m in reversed(range(slots)):
        real_row, row, band = slot_position(*index, m, nblocks)
        table[jnp.where(real_row >= 0, row * WIDTH + band, BR * WIDTH)] = m
    load.wait()

    @for_own_parity
    def _(mine):
        for name, ref in out_refs.items():
            distance = DISTANCES[name]
            for n, (k, j) in enumerate(SENT[name, (mine + distance) % 2]):
                at = (k - BR * distance) * WIDTH + j - k + HB
                if distance % 2 == 1:
                    at = BR * WIDTH - 1 - at
                ref[n] = held[table[at]]
        columns = columns_of(mine)
        for i in range(BR):
            for n in range(NCOL):
                rows, cols = pl.ds(i * BLK, BLK), pl.ds(n * BLK, BLK)
                if n < len(columns) and abs(columns[n] - i) <= HB:
                    left_ref[rows, cols] = held[table[i * WIDTH + columns[n] - i + HB]]
                else:
                    left_ref[rows, cols] = jnp.zeros((BLK, BLK), left_ref.dtype)


def find_block(parity, k, j):
    if abs(k - j) > HB:
        return None
    if 0 <= k < BR:
        return ("left", parity == j % 2), (k, columns_of(j % 2).index(j)), False
    if 0 <= j < BR:
        return ("left", parity == k % 2), (j, columns_of(k % 2).index(k)), True
    for a, b, flip in ((k, j, False), (j, k, True)):
        for name in DISTANCES:
            if (a, b) in SENT[name, parity]:
                return name, SENT[name, parity].index((a, b)), flip
        staged = [position for _, _, position in STAGED[1 - parity]]
        if (a, b) in staged:
            return "staged", staged.index((a, b)), flip
    raise AssertionError((k, j))


def columns_product(refs, right, parity, js, wanted):
    total = None
    for own in (True, False):
        kind = parity if own else 1 - parity
        found = {}
        for k in columns_of(kind):
            for j in js:
                place = find_block(parity, k, j)
                if place is not None and wanted(place[0]):
                    found[k, j] = place
        if not found:
            continue
        first, last = min(k for k, _ in found), max(k for k, _ in found)
        ks = [k for k in columns_of(kind) if first <= k <= last]
        side = right.at[0 if own else 1]
        for x, k in enumerate(ks):
            for y, j in enumerate(js):
                if (k, j) in found:
                    source, place, flip = found[k, j]
                    if isinstance(place, tuple):
                        block = refs[source][pl.ds(place[0] * BLK, BLK), pl.ds(place[1] * BLK, BLK)]
                    else:
                        block = refs[source][place]
                    block = block.T if flip else block
                else:
                    block = jnp.zeros((BLK, BLK), right.dtype)
                side[pl.ds(x * BLK, BLK), pl.ds(y * BLK, BLK)] = block
        start = columns_of(kind).index(first)
        part = jnp.dot(
            refs["left", own][:, pl.ds(start * BLK, len(ks) * BLK)],
            side[pl.ds(0, len(ks) * BLK), pl.ds(0, len(js) * BLK)],
            preferred_element_type=jnp.float32,
        )
        total = part if total is None else total + part
    return total


def block_of(total, i, y):
    return total[i * BLK : (i + 1) * BLK, y * BLK : (y + 1) * BLK]


def outer_pairs(parity):
    outer = [j for j in columns_of(parity) if not 0 <= j < BR]
    return [outer[n : n + 2] for n in range(0, len(outer), 2)]


def inner_kernel(nblocks, slots, rows_ref, cols_ref, counts_ref, left_ref, left_other_ref, *rest):
    made_ref, places_ref, right, places, *index, sems, places_sem = rest
    copies = index_copies((rows_ref, cols_ref), index, sems)
    for copy in copies:
        copy.start()
    refs = {("left", True): left_ref, ("left", False): left_other_ref}

    @for_own_parity
    def _(mine):
        js = [j for j in columns_of(mine) if 0 <= j < BR]
        total = columns_product(refs, right, mine, js, lambda source: True)
        for i in range(BR):
            for y in range(2):
                made_ref[i * 2 + y] = block_of(total, i, y) if y < len(js) else jnp.zeros((BLK, BLK), made_ref.dtype)

    for copy in copies:
        copy.wait()
    count = counts_ref[0, 0]
    for m in range(slots):
        _, row, band = slot_position(*index, m, nblocks)
        places[0, m] = jnp.where(m < count, row * NCOL + (row + band) // 2, BR * NCOL)
    copy = pltpu.make_async_copy(places, places_ref, places_sem)
    copy.start()
    copy.wait()


def pack_e_kernel(left_ref, left_other_ref, e_ref):
    @for_own_parity
    def _(mine):
        i = 2 if mine == 0 else 0
        n = columns_of(0).index(i)
        e_ref[0] = (left_ref if mine == 0 else left_other_ref)[pl.ds(i * BLK, BLK), pl.ds(n * BLK, BLK)]


def keep_kernel(*refs):
    pass


def stage_kernel(*refs):
    got = dict(zip(DISTANCES, refs))
    out_ref = refs[-1]

    @for_own_parity
    def _(mine):
        for n, (name, place, _) in enumerate(STAGED[mine]):
            out_ref[n] = got[name][place]
        for n in range(len(STAGED[mine]), STAGED_SIZE):
            out_ref[n] = jnp.zeros((BLK, BLK), out_ref.dtype)


def outer_kernel(left_ref, left_other_ref, *rest):
    refs = {("left", True): left_ref, ("left", False): left_other_ref, **dict(zip(DISTANCES, rest))}
    out_ref, right = rest[len(DISTANCES) :]

    @for_own_parity
    def _(mine):
        for pair, js in enumerate(outer_pairs(mine)):
            total = columns_product(refs, right.at[pair], mine, js, lambda source: source != "staged")
            for i in range(BR):
                for y, j in enumerate(js):
                    if abs(i - j) <= HB:
                        out_ref[i * NCOL + columns_of(mine).index(j)] = block_of(total, i, y)


def multiply_kernel(slots, left_ref, left_other_ref, staged_ref, outer_ref, inner_ref, places_ref, out_ref, *rest):
    right, made, places, places_sem, out_sem = rest
    refs = {("left", True): left_ref, ("left", False): left_other_ref, "staged": staged_ref}
    load = pltpu.make_async_copy(places_ref, places, places_sem)
    load.start()

    @for_own_parity
    def _(mine):
        columns = columns_of(mine)
        for pair, js in enumerate(outer_pairs(mine)):
            total = columns_product(refs, right.at[pair], mine, js, lambda source: source == "staged")
            for i in range(BR):
                for y, j in enumerate(js):
                    if abs(i - j) <= HB:
                        place = i * NCOL + columns.index(j)
                        made[place] = outer_ref[place] + block_of(total, i, y)
        for i in range(BR):
            for y, j in enumerate(j for j in columns if 0 <= j < BR):
                made[i * NCOL + columns.index(j)] = inner_ref[i * 2 + y]
        made[BR * NCOL] = jnp.zeros((BLK, BLK), made.dtype)

    load.wait()
    for m in range(slots):
        pltpu.make_async_copy(made.at[places[0, m]], out_ref.at[0, m], out_sem).start()
    pltpu.make_async_copy(made.at[pl.ds(0, slots)], out_ref.at[0], out_sem).wait()


def local(values, block_rows, block_cols, counts):
    slots = values.shape[1]
    row_count, col_count = lax.axis_size("row"), lax.axis_size("col")
    nblocks = BR * row_count
    smem = pl.BlockSpec(memory_space=pltpu.SMEM)
    vmem = pl.BlockSpec(memory_space=pltpu.VMEM)
    hbm = pl.BlockSpec(memory_space=pltpu.HBM)
    params = pltpu.CompilerParams(vmem_limit_bytes=VMEM_LIMIT)
    values, *places = (pltpu.with_memory_space_constraint(x, pltpu.HBM) for x in (values, block_rows, block_cols))
    index_scratch = [
        pltpu.SMEM((1, slots), jnp.int32),
        pltpu.SMEM((1, slots), jnp.int32),
        pltpu.SemaphoreType.DMA((2,)),
    ]
    places_shape = (1, BLK)

    def blocks(count, dtype=values.dtype):
        return jax.ShapeDtypeStruct((count, BLK, BLK), dtype)

    def cost(products, nbytes):
        return pl.CostEstimate(flops=2 * products * BLK**3, bytes_accessed=nbytes, transcendentals=0)

    def right_scratch(pairs):
        return pltpu.VMEM((pairs, 2, NCOL * BLK, 2 * BLK), values.dtype)

    *packed, left = pl.pallas_call(
        functools.partial(pack_kernel, nblocks, slots),
        out_shape=[blocks(SIZES[name]) for name in "abcd"]
        + [jax.ShapeDtypeStruct((BR * BLK, NCOL * BLK), values.dtype)],
        in_specs=[hbm] * 3,
        out_specs=[vmem] * 5,
        scratch_shapes=[
            pltpu.VMEM((slots + 1, BLK, BLK), values.dtype),
            pltpu.SMEM((BR * WIDTH + 1,), jnp.int32),
            *index_scratch,
            pltpu.SemaphoreType.DMA,
        ],
        compiler_params=params,
        name="pack",
    )(*places, values)

    def towards(name, message):
        pairs = []
        for r in range(row_count):
            for c in range(col_count):
                distance = DISTANCES[name] or (3 if (r + c) % 2 == 1 else -3)
                source = (r - distance if r % 2 == 1 else r + distance) % row_count
                pairs.append((source * col_count + c, r * col_count + c))
        return lax.ppermute(message, ("row", "col"), pairs)

    def keep(arrays, flops):
        return pl.pallas_call(
            keep_kernel,
            out_shape=[jax.ShapeDtypeStruct(x.shape, x.dtype) for x in arrays],
            in_specs=[vmem] * len(arrays),
            out_specs=[vmem] * len(arrays),
            input_output_aliases={n: n for n in range(len(arrays))},
            compiler_params=params,
            cost_estimate=pl.CostEstimate(flops=flops, bytes_accessed=0, transcendentals=0),
            name="keep",
        )(*arrays)

    def swapped(block):
        return lax.ppermute(block, "col", [(0, 1), (1, 0)])

    left_other = swapped(left)
    got = [towards(name, message) for name, message in zip("abcd", packed)]
    message = pl.pallas_call(
        pack_e_kernel,
        out_shape=blocks(SIZES["e"]),
        in_specs=[vmem] * 2,
        out_specs=vmem,
        compiler_params=params,
        name="pack_e",
    )(left, left_other)
    got.append(towards("e", message))
    inner, slot_places = pl.pallas_call(
        functools.partial(inner_kernel, nblocks, slots),
        out_shape=[blocks(INNER, jnp.float32), jax.ShapeDtypeStruct(places_shape, jnp.int32)],
        in_specs=[hbm] * 2 + [smem] + [vmem] * 2,
        out_specs=[vmem] * 2,
        scratch_shapes=[
            pltpu.VMEM((2, NCOL * BLK, 2 * BLK), values.dtype),
            pltpu.SMEM(places_shape, jnp.int32),
            *index_scratch,
            pltpu.SemaphoreType.DMA,
        ],
        compiler_params=params,
        cost_estimate=cost(3 * 2 * 17, 4 * values.size),
        name="inner",
    )(*places, counts, left, left_other)
    got[2], inner, = keep((got[2], inner,), 4000000000)
    *got, inner = lax.optimization_barrier((*got, inner))
    staged = swapped(
        pl.pallas_call(
            stage_kernel,
            out_shape=blocks(STAGED_SIZE),
            in_specs=[vmem] * 5,
            out_specs=vmem,
            compiler_params=params,
            name="stage",
        )(*got)
    )
    outer = pl.pallas_call(
        outer_kernel,
        out_shape=blocks(BR * NCOL, jnp.float32),
        in_specs=[vmem] * 7,
        out_specs=vmem,
        scratch_shapes=[right_scratch(4)],
        compiler_params=params,
        cost_estimate=cost(3 * 2 * 56, 10 * values.size),
        name="outer",
    )(left, left_other, *got)
    return pl.pallas_call(
        functools.partial(multiply_kernel, slots),
        out_shape=jax.ShapeDtypeStruct(values.shape, jnp.float32),
        in_specs=[vmem] * 6,
        out_specs=hbm,
        scratch_shapes=[
            right_scratch(4),
            pltpu.VMEM((BR * NCOL + 1, BLK, BLK), jnp.float32),
            pltpu.SMEM(places_shape, jnp.int32),
            pltpu.SemaphoreType.DMA,
            pltpu.SemaphoreType.DMA,
        ],
        compiler_params=params,
        name="multiply",
    )(left, left_other, staged, outer, inner, slot_places)


def solution(mesh):
    return jax.shard_map(
        local,
        mesh=mesh,
        in_specs=(
            P(("parts", "row"), "col", None, None),
            P(("parts", "row"), "col"),
            P(("parts", "row"), "col"),
            P(("parts", "row"), "col"),
        ),
        out_specs=P(("parts", "row"), "col", None, None),
        check_vma=False,
    )
```

```python
import functools

import jax
import jax.numpy as jnp
from jax import lax
from jax.experimental import pallas as pl
from jax.experimental.pallas import tpu as pltpu
from jax.sharding import PartitionSpec as P

BLK = 128
BR = 3
HB = 7
WIDTH = 2 * HB + 1
LOW, HIGH = -HB, BR - 1 + HB
NCOL = 9
INNER = 6
EARLY_COST = 1000
LATE_COST = 50
VMEM_LIMIT = 12 * 2**20

DISTANCES = {"a": 1, "b": -1, "c": -2, "d": 2, "e": None}
SENT = {
    ("a", 1): [(3, 3), (5, 5), (3, 5), (3, 7), (4, 7), (5, 7), (3, 9), (4, 9), (5, 9), (3, -3), (3, -1), (4, -3), (5, -1)],
    ("a", 0): [(4, 4), (3, 4), (5, 4), (3, 6), (4, 6), (5, 6), (3, 8), (4, 8), (5, 8), (3, -2), (4, -2), (5, -2), (3, -4)],
    ("b", 1): [(-1, -1), (-3, -3), (-1, -3), (-1, -7), (-2, -7), (-3, -7)],
    ("b", 0): [(-2, -2), (-1, -2), (-3, -2), (-1, 4), (-1, -4), (-1, -6)],
    ("c", 1): [(-5, -5), (-4, -7), (-5, -7), (-6, -7), (-4, -3), (-5, -1), (-5, -3), (-6, -3)],
    ("c", 0): [(-4, -4), (-6, -6), (-4, -6), (-4, -2), (-5, -2), (-6, -2), (-5, -4), (-5, -6)],
    ("d", 1): [(6, 9), (7, 7), (7, 9), (8, 9), (6, -1)],
    ("d", 0): [(6, 6), (6, 8), (8, 8), (7, 6), (7, 8)],
    ("e", 1): [(9, 9)],
    ("e", 0): [(-7, -7)],
}
SIZES = {name: len(SENT[name, 1]) for name in DISTANCES}
PARTS = {"early": "ac", "late": "bde"}
STAGED = {
    (part, parity): [
        (name, n, (k, j))
        for name in names
        for n, (k, j) in enumerate(SENT[name, parity])
        if k % 2 != j % 2 or (k, j) == (-7, -7)
    ]
    for part, names in PARTS.items()
    for parity in (0, 1)
}
STAGED_SIZE = {part: max(len(STAGED[part, parity]) for parity in (0, 1)) for part in PARTS}


def columns_of(parity):
    return [j for j in range(LOW, HIGH + 1) if j % 2 == parity]


def own_parity():
    return (lax.axis_index("row") + lax.axis_index("col")) % 2


def for_own_parity(body):
    parity = own_parity()
    for mine in (0, 1):
        pl.when(parity == mine)(functools.partial(body, mine))


def slot_position(rows_ref, cols_ref, slot, nblocks):
    panel = lax.axis_index("row")
    row = rows_ref[0, slot] - panel * BR
    band = cols_ref[0, slot] - rows_ref[0, slot] + HB
    band = jnp.where(band < 0, band + nblocks, band)
    band = jnp.where(band >= nblocks, band - nblocks, band)
    odd = panel % 2 == 1
    return row, jnp.where(odd, BR - 1 - row, row), jnp.where(odd, WIDTH - 1 - band, band)


def index_copies(hbm_refs, smem_refs, sems):
    return [pltpu.make_async_copy(a, b, sems.at[i]) for i, (a, b) in enumerate(zip(hbm_refs, smem_refs))]


def pack_kernel(nblocks, slots, rows_ref, cols_ref, values_ref, *rest):
    out_refs = dict(zip("abcd", rest[:4]))
    left_ref, held, table, *index, sems, value_sem = rest[4:]
    copies = index_copies((rows_ref, cols_ref), index, sems)
    load = pltpu.make_async_copy(values_ref.at[0], held.at[pl.ds(0, slots)], value_sem)
    for copy in (*copies, load):
        copy.start()
    held[slots] = jnp.zeros((BLK, BLK), held.dtype)
    for i in range(BR * WIDTH + 1):
        table[i] = slots
    for copy in copies:
        copy.wait()
    for m in reversed(range(slots)):
        real_row, row, band = slot_position(*index, m, nblocks)
        table[jnp.where(real_row >= 0, row * WIDTH + band, BR * WIDTH)] = m
    load.wait()

    @for_own_parity
    def _(mine):
        for name, ref in out_refs.items():
            distance = DISTANCES[name]
            for n, (k, j) in enumerate(SENT[name, (mine + distance) % 2]):
                at = (k - BR * distance) * WIDTH + j - k + HB
                if distance % 2 == 1:
                    at = BR * WIDTH - 1 - at
                ref[n] = held[table[at]]
        columns = columns_of(mine)
        for i in range(BR):
            for n in range(NCOL):
                rows, cols = pl.ds(i * BLK, BLK), pl.ds(n * BLK, BLK)
                if n < len(columns) and abs(columns[n] - i) <= HB:
                    left_ref[rows, cols] = held[table[i * WIDTH + columns[n] - i + HB]]
                else:
                    left_ref[rows, cols] = jnp.zeros((BLK, BLK), left_ref.dtype)


def find_block(parity, k, j):
    if abs(k - j) > HB:
        return None
    if 0 <= k < BR:
        return ("left", parity == j % 2), (k, columns_of(j % 2).index(j)), False
    if 0 <= j < BR:
        return ("left", parity == k % 2), (j, columns_of(k % 2).index(k)), True
    for a, b, flip in ((k, j, False), (j, k, True)):
        for name in DISTANCES:
            if (a, b) in SENT[name, parity]:
                return name, SENT[name, parity].index((a, b)), flip
        for part in PARTS:
            staged = [position for _, _, position in STAGED[part, 1 - parity]]
            if (a, b) in staged:
                return part, staged.index((a, b)), flip
    raise AssertionError((k, j))


def columns_product(refs, right, parity, js, wanted):
    total = None
    for own in (True, False):
        kind = parity if own else 1 - parity
        found = {}
        for k in columns_of(kind):
            for j in js:
                place = find_block(parity, k, j)
                if place is not None and place[0] in wanted:
                    found[k, j] = place
        if not found:
            continue
        first, last = min(k for k, _ in found), max(k for k, _ in found)
        ks = [k for k in columns_of(kind) if first <= k <= last]
        side = right.at[0 if own else 1]
        for x, k in enumerate(ks):
            for y, j in enumerate(js):
                if (k, j) in found:
                    source, place, flip = found[k, j]
                    if isinstance(place, tuple):
                        block = refs[source][pl.ds(place[0] * BLK, BLK), pl.ds(place[1] * BLK, BLK)]
                    else:
                        block = refs[source][place]
                    block = block.T if flip else block
                else:
                    block = jnp.zeros((BLK, BLK), right.dtype)
                side[pl.ds(x * BLK, BLK), pl.ds(y * BLK, BLK)] = block
        start = columns_of(kind).index(first)
        part = jnp.dot(
            refs["left", own][:, pl.ds(start * BLK, len(ks) * BLK)],
            side[pl.ds(0, len(ks) * BLK), pl.ds(0, len(js) * BLK)],
            preferred_element_type=jnp.float32,
        )
        total = part if total is None else total + part
    return total


LEFT = (("left", True), ("left", False))


def block_of(total, i, y):
    return total[i * BLK : (i + 1) * BLK, y * BLK : (y + 1) * BLK]


def outer_pairs(parity):
    outer = [j for j in columns_of(parity) if not 0 <= j < BR]
    return [outer[n : n + 2] for n in range(0, len(outer), 2)]


def inner_kernel(nblocks, slots, rows_ref, cols_ref, counts_ref, left_ref, left_other_ref, *rest):
    made_ref, places_ref, right, places, *index, sems, places_sem = rest
    copies = index_copies((rows_ref, cols_ref), index, sems)
    for copy in copies:
        copy.start()
    refs = {("left", True): left_ref, ("left", False): left_other_ref}

    @for_own_parity
    def _(mine):
        js = [j for j in columns_of(mine) if 0 <= j < BR]
        total = columns_product(refs, right, mine, js, LEFT)
        for i in range(BR):
            for y in range(2):
                made_ref[i * 2 + y] = block_of(total, i, y) if y < len(js) else jnp.zeros((BLK, BLK), made_ref.dtype)

    for copy in copies:
        copy.wait()
    count = counts_ref[0, 0]
    for m in range(slots):
        _, row, band = slot_position(*index, m, nblocks)
        places[0, m] = jnp.where(m < count, row * NCOL + (row + band) // 2, BR * NCOL)
    copy = pltpu.make_async_copy(places, places_ref, places_sem)
    copy.start()
    copy.wait()


def pack_e_kernel(left_ref, left_other_ref, e_ref):
    @for_own_parity
    def _(mine):
        i = 2 if mine == 0 else 0
        n = columns_of(0).index(i)
        e_ref[0] = (left_ref if mine == 0 else left_other_ref)[pl.ds(i * BLK, BLK), pl.ds(n * BLK, BLK)]


def stage_kernel(part, *refs):
    got = dict(zip(PARTS[part], refs))
    out_ref = refs[-1]

    @for_own_parity
    def _(mine):
        staged = STAGED[part, mine]
        for n, (name, place, _) in enumerate(staged):
            out_ref[n] = got[name][place]
        for n in range(len(staged), STAGED_SIZE[part]):
            out_ref[n] = jnp.zeros((BLK, BLK), out_ref.dtype)


def add_columns(refs, wanted, old_ref, new_ref, right, mine):
    for pair, js in enumerate(outer_pairs(mine)):
        total = columns_product(refs, right.at[pair], mine, js, wanted)
        for i in range(BR):
            for y, j in enumerate(js):
                if abs(i - j) <= HB:
                    place = i * NCOL + columns_of(mine).index(j)
                    if old_ref is None:
                        new_ref[place] = block_of(total, i, y)
                    else:
                        new_ref[place] = old_ref[place] if total is None else old_ref[place] + block_of(total, i, y)


def early_kernel(left_ref, left_other_ref, a_ref, c_ref, out_ref, right):
    refs = {("left", True): left_ref, ("left", False): left_other_ref, "a": a_ref, "c": c_ref}
    for_own_parity(functools.partial(add_columns, refs, (*LEFT, "a", "c"), None, out_ref, right))


def staged_early_kernel(left_ref, left_other_ref, staged_ref, old_ref, out_ref, right):
    refs = {("left", True): left_ref, ("left", False): left_other_ref, "early": staged_ref}
    for_own_parity(functools.partial(add_columns, refs, ("early",), old_ref, out_ref, right))


def late_kernel(left_ref, left_other_ref, b_ref, d_ref, e_ref, old_ref, out_ref, right):
    refs = {("left", True): left_ref, ("left", False): left_other_ref, "b": b_ref, "d": d_ref, "e": e_ref}
    for_own_parity(functools.partial(add_columns, refs, ("b", "d", "e"), old_ref, out_ref, right))


def multiply_kernel(slots, left_ref, left_other_ref, staged_ref, old_ref, inner_ref, places_ref, out_ref, *rest):
    right, made, places, places_sem, out_sem = rest
    refs = {("left", True): left_ref, ("left", False): left_other_ref, "late": staged_ref}
    load = pltpu.make_async_copy(places_ref, places, places_sem)
    load.start()

    @for_own_parity
    def _(mine):
        add_columns(refs, ("late",), old_ref, made, right, mine)
        columns = columns_of(mine)
        for i in range(BR):
            for y, j in enumerate(j for j in columns if 0 <= j < BR):
                made[i * NCOL + columns.index(j)] = inner_ref[i * 2 + y]
        made[BR * NCOL] = jnp.zeros((BLK, BLK), made.dtype)

    load.wait()
    for m in range(slots):
        pltpu.make_async_copy(made.at[places[0, m]], out_ref.at[0, m], out_sem).start()
    pltpu.make_async_copy(made.at[pl.ds(0, slots)], out_ref.at[0], out_sem).wait()


def local(values, block_rows, block_cols, counts):
    slots = values.shape[1]
    row_count, col_count = lax.axis_size("row"), lax.axis_size("col")
    nblocks = BR * row_count
    smem = pl.BlockSpec(memory_space=pltpu.SMEM)
    vmem = pl.BlockSpec(memory_space=pltpu.VMEM)
    hbm = pl.BlockSpec(memory_space=pltpu.HBM)
    params = pltpu.CompilerParams(vmem_limit_bytes=VMEM_LIMIT)
    values, *places = (pltpu.with_memory_space_constraint(x, pltpu.HBM) for x in (values, block_rows, block_cols))
    index_scratch = [
        pltpu.SMEM((1, slots), jnp.int32),
        pltpu.SMEM((1, slots), jnp.int32),
        pltpu.SemaphoreType.DMA((2,)),
    ]
    places_shape = (1, BLK)

    def blocks(count, dtype=values.dtype):
        return jax.ShapeDtypeStruct((count, BLK, BLK), dtype)

    def cost(products, nbytes):
        return pl.CostEstimate(flops=2 * products * BLK**3, bytes_accessed=nbytes, transcendentals=0)

    def right_scratch(pairs):
        return pltpu.VMEM((pairs, 2, NCOL * BLK, 2 * BLK), values.dtype)

    *packed, left = pl.pallas_call(
        functools.partial(pack_kernel, nblocks, slots),
        out_shape=[blocks(SIZES[name]) for name in "abcd"]
        + [jax.ShapeDtypeStruct((BR * BLK, NCOL * BLK), values.dtype)],
        in_specs=[hbm] * 3,
        out_specs=[vmem] * 5,
        scratch_shapes=[
            pltpu.VMEM((slots + 1, BLK, BLK), values.dtype),
            pltpu.SMEM((BR * WIDTH + 1,), jnp.int32),
            *index_scratch,
            pltpu.SemaphoreType.DMA,
        ],
        compiler_params=params,
        name="pack",
    )(*places, values)

    def towards(name, message):
        pairs = []
        for r in range(row_count):
            for c in range(col_count):
                distance = DISTANCES[name] or (3 if (r + c) % 2 == 1 else -3)
                source = (r - distance if r % 2 == 1 else r + distance) % row_count
                pairs.append((source * col_count + c, r * col_count + c))
        return lax.ppermute(message, ("row", "col"), pairs)

    def swapped(block):
        return lax.ppermute(block, "col", [(0, 1), (1, 0)])

    left_other = swapped(left)
    got = [towards(name, message) for name, message in zip("abcd", packed)]
    message = pl.pallas_call(
        pack_e_kernel,
        out_shape=blocks(SIZES["e"]),
        in_specs=[vmem] * 2,
        out_specs=vmem,
        compiler_params=params,
        name="pack_e",
    )(left, left_other)
    got.append(towards("e", message))
    inner, slot_places = pl.pallas_call(
        functools.partial(inner_kernel, nblocks, slots),
        out_shape=[blocks(INNER, jnp.float32), jax.ShapeDtypeStruct(places_shape, jnp.int32)],
        in_specs=[hbm] * 2 + [smem] + [vmem] * 2,
        out_specs=[vmem] * 2,
        scratch_shapes=[
            pltpu.VMEM((2, NCOL * BLK, 2 * BLK), values.dtype),
            pltpu.SMEM(places_shape, jnp.int32),
            *index_scratch,
            pltpu.SemaphoreType.DMA,
        ],
        compiler_params=params,
        cost_estimate=cost(3 * 2 * 17, 4 * values.size),
        name="inner",
    )(*places, counts, left, left_other)
    a, b, c, d, e = got

    def staged(part, arrays):
        return swapped(
            pl.pallas_call(
                functools.partial(stage_kernel, part),
                out_shape=blocks(STAGED_SIZE[part]),
                in_specs=[vmem] * len(arrays),
                out_specs=vmem,
                compiler_params=params,
                name="stage_" + part,
            )(*arrays)
        )

    def added(kernel, name, products, arrays):
        return pl.pallas_call(
            kernel,
            out_shape=blocks(BR * NCOL, jnp.float32),
            in_specs=[vmem] * len(arrays),
            out_specs=vmem,
            scratch_shapes=[right_scratch(4)],
            compiler_params=params,
            cost_estimate=cost(products, 0),
            name=name,
        )(*arrays)

    a, c, inner = lax.optimization_barrier((a, c, inner))
    staged_early = staged("early", (a, c))
    early = added(early_kernel, "early", EARLY_COST, (left, left_other, a, c))
    early = added(staged_early_kernel, "staged_early", 1, (left, left_other, staged_early, early))
    b, d, e, early = lax.optimization_barrier((b, d, e, early))
    staged_late = staged("late", (b, d, e))
    late = added(late_kernel, "late", LATE_COST, (left, left_other, b, d, e, early))
    return pl.pallas_call(
        functools.partial(multiply_kernel, slots),
        out_shape=jax.ShapeDtypeStruct(values.shape, jnp.float32),
        in_specs=[vmem] * 6,
        out_specs=hbm,
        scratch_shapes=[
            right_scratch(4),
            pltpu.VMEM((BR * NCOL + 1, BLK, BLK), jnp.float32),
            pltpu.SMEM(places_shape, jnp.int32),
            pltpu.SemaphoreType.DMA,
            pltpu.SemaphoreType.DMA,
        ],
        compiler_params=params,
        name="multiply",
    )(left, left_other, staged_late, late, inner, slot_places)


def solution(mesh):
    return jax.shard_map(
        local,
        mesh=mesh,
        in_specs=(
            P(("parts", "row"), "col", None, None),
            P(("parts", "row"), "col"),
            P(("parts", "row"), "col"),
            P(("parts", "row"), "col"),
        ),
        out_specs=P(("parts", "row"), "col", None, None),
        check_vma=False,
    )
```

```python
import functools

import jax
import jax.numpy as jnp
from jax import lax
from jax.experimental import pallas as pl
from jax.experimental.pallas import tpu as pltpu
from jax.sharding import PartitionSpec as P

BLK = 128
BR = 3
HB = 7
WIDTH = 2 * HB + 1
LOW, HIGH = -HB, BR - 1 + HB
NCOL = 9
SOURCES = 32
VMEM_LIMIT = 12 * 2**20

DISTANCES = {"a": 1, "b": -1, "c": -2, "d": 2, "e": None}
SENT = {
    ("a", 1): [(3, 3), (5, 5), (3, 5), (3, 7), (4, 7), (5, 7), (3, 9), (4, 9), (5, 9), (3, -3), (3, -1), (4, -3), (5, -1)],
    ("a", 0): [(4, 4), (3, 4), (5, 4), (3, 6), (4, 6), (5, 6), (3, 8), (4, 8), (5, 8), (3, -2), (4, -2), (5, -2), (3, -4)],
    ("b", 1): [(-1, -1), (-3, -3), (-1, -3), (-1, -7), (-2, -7), (-3, -7)],
    ("b", 0): [(-2, -2), (-1, -2), (-3, -2), (-1, 4), (-1, -4), (-1, -6)],
    ("c", 1): [(-5, -5), (-4, -7), (-5, -7), (-6, -7), (-4, -3), (-5, -1), (-5, -3), (-6, -3)],
    ("c", 0): [(-4, -4), (-6, -6), (-4, -6), (-4, -2), (-5, -2), (-6, -2), (-5, -4), (-5, -6)],
    ("d", 1): [(6, 9), (7, 7), (7, 9), (8, 9), (6, -1)],
    ("d", 0): [(6, 6), (6, 8), (8, 8), (7, 6), (7, 8)],
    ("e", 1): [(9, 9)],
    ("e", 0): [(-7, -7)],
}
SIZES = {name: len(SENT[name, 1]) for name in DISTANCES}
STAGED = {
    parity: [
        (name, n, (k, j))
        for name in DISTANCES
        for n, (k, j) in enumerate(SENT[name, parity])
        if k % 2 != j % 2 or (k, j) == (-7, -7)
    ]
    for parity in (0, 1)
}
STAGED_SIZE = max(len(found) for found in STAGED.values())


def columns_of(parity):
    return [j for j in range(LOW, HIGH + 1) if j % 2 == parity]


def own_parity():
    return (lax.axis_index("row") + lax.axis_index("col")) % 2


def for_own_parity(body):
    parity = own_parity()
    for mine in (0, 1):
        pl.when(parity == mine)(functools.partial(body, mine))


def slot_position(rows_ref, cols_ref, slot, nblocks):
    panel = lax.axis_index("row")
    row = rows_ref[0, slot] - panel * BR
    band = cols_ref[0, slot] - rows_ref[0, slot] + HB
    band = jnp.where(band < 0, band + nblocks, band)
    band = jnp.where(band >= nblocks, band - nblocks, band)
    odd = panel % 2 == 1
    return row, jnp.where(odd, BR - 1 - row, row), jnp.where(odd, WIDTH - 1 - band, band)


def index_copies(hbm_refs, smem_refs, sems):
    return [pltpu.make_async_copy(a, b, sems.at[i]) for i, (a, b) in enumerate(zip(hbm_refs, smem_refs))]


def pack_kernel(nblocks, slots, rows_ref, cols_ref, values_ref, *rest):
    out_refs = dict(zip("abcd", rest[:4]))
    left_ref, held, table, *index, sems, value_sem = rest[4:]
    copies = index_copies((rows_ref, cols_ref), index, sems)
    load = pltpu.make_async_copy(values_ref.at[0], held.at[pl.ds(0, slots)], value_sem)
    for copy in (*copies, load):
        copy.start()
    held[slots] = jnp.zeros((BLK, BLK), held.dtype)
    for i in range(BR * WIDTH + 1):
        table[i] = slots
    for copy in copies:
        copy.wait()
    for m in reversed(range(slots)):
        real_row, row, band = slot_position(*index, m, nblocks)
        table[jnp.where(real_row >= 0, row * WIDTH + band, BR * WIDTH)] = m
    load.wait()

    @for_own_parity
    def _(mine):
        for name, ref in out_refs.items():
            distance = DISTANCES[name]
            for n, (k, j) in enumerate(SENT[name, (mine + distance) % 2]):
                at = (k - BR * distance) * WIDTH + j - k + HB
                if distance % 2 == 1:
                    at = BR * WIDTH - 1 - at
                ref[n] = held[table[at]]
        columns = columns_of(mine)
        for i in range(BR):
            for n in range(NCOL):
                rows, cols = pl.ds(i * BLK, BLK), pl.ds(n * BLK, BLK)
                if n < len(columns) and abs(columns[n] - i) <= HB:
                    left_ref[rows, cols] = held[table[i * WIDTH + columns[n] - i + HB]]
                else:
                    left_ref[rows, cols] = jnp.zeros((BLK, BLK), left_ref.dtype)


def find_block(parity, k, j):
    if abs(k - j) > HB:
        return None
    if 0 <= k < BR:
        return ("left", parity == j % 2), (k, columns_of(j % 2).index(j)), False
    if 0 <= j < BR:
        return ("left", parity == k % 2), (j, columns_of(k % 2).index(k)), True
    for a, b, flip in ((k, j, False), (j, k, True)):
        for name in DISTANCES:
            if (a, b) in SENT[name, parity]:
                return name, SENT[name, parity].index((a, b)), flip
        staged = [position for _, _, position in STAGED[1 - parity]]
        if (a, b) in staged:
            return "staged", staged.index((a, b)), flip
    raise AssertionError((k, j))


def columns_product(refs, right, parity, js, wanted):
    total = None
    for own in (True, False):
        kind = parity if own else 1 - parity
        found = {}
        for k in columns_of(kind):
            for j in js:
                place = find_block(parity, k, j)
                if place is not None and wanted(place[0]):
                    found[k, j] = place
        if not found:
            continue
        first, last = min(k for k, _ in found), max(k for k, _ in found)
        ks = [k for k in columns_of(kind) if first <= k <= last]
        side = right.at[0 if own else 1]
        for x, k in enumerate(ks):
            for y, j in enumerate(js):
                if (k, j) in found:
                    source, place, flip = found[k, j]
                    if isinstance(place, tuple):
                        block = refs[source][pl.ds(place[0] * BLK, BLK), pl.ds(place[1] * BLK, BLK)]
                    else:
                        block = refs[source][place]
                    block = block.T if flip else block
                else:
                    block = jnp.zeros((BLK, BLK), right.dtype)
                side[pl.ds(x * BLK, BLK), pl.ds(y * BLK, BLK)] = block
        start = columns_of(kind).index(first)
        part = jnp.dot(
            refs["left", own][:, pl.ds(start * BLK, len(ks) * BLK)],
            side[pl.ds(0, len(ks) * BLK), pl.ds(0, len(js) * BLK)],
            preferred_element_type=jnp.float32,
        )
        total = part if total is None else total + part
    return total


def block_of(total, i, y):
    return total[i * BLK : (i + 1) * BLK, y * BLK : (y + 1) * BLK]


def stored_places(parity):
    columns = columns_of(parity)
    return [i * NCOL + n for i in range(BR) for n, j in enumerate(columns) if abs(i - j) <= HB]


def outer_pairs(parity):
    outer = [j for j in columns_of(parity) if not 0 <= j < BR]
    return [outer[n : n + 2] for n in range(0, len(outer), 2)]


def inner_kernel(nblocks, slots, rows_ref, cols_ref, counts_ref, left_ref, left_other_ref, *rest):
    made_ref, table_ref, right, table, *index, sems, table_sem = rest
    copies = index_copies((rows_ref, cols_ref), index, sems)
    for copy in copies:
        copy.start()
    refs = {("left", True): left_ref, ("left", False): left_other_ref}

    @for_own_parity
    def _(mine):
        js = [j for j in columns_of(mine) if 0 <= j < BR]
        total = columns_product(refs, right, mine, js, lambda source: True)
        for i in range(BR):
            for y in range(2):
                if y < len(js):
                    made_ref[i * NCOL + columns_of(mine).index(js[y])] = block_of(total, i, y)
        made_ref[BR * NCOL] = jnp.zeros((BLK, BLK), made_ref.dtype)

    for copy in copies:
        copy.wait()
    for place in range(BR * NCOL + 1):
        table[0, place] = -1
    count = counts_ref[0, 0]
    for m in range(slots):
        _, row, band = slot_position(*index, m, nblocks)
        table[0, jnp.where(m < count, row * NCOL + (row + band) // 2, BR * NCOL)] = m

    @for_own_parity
    def _(mine):
        unused = count
        for place in stored_places(mine):
            slot = table[0, place]
            absent = slot < 0
            table[0, place] = jnp.where(absent, unused, slot)
            table[0, SOURCES + place] = jnp.where(absent, BR * NCOL, place)
            unused = jnp.where(absent, unused + 1, unused)
        table[0, BR * NCOL] = unused

    copy = pltpu.make_async_copy(table, table_ref, table_sem)
    copy.start()
    copy.wait()


def pack_e_kernel(left_ref, left_other_ref, e_ref):
    @for_own_parity
    def _(mine):
        i = 2 if mine == 0 else 0
        n = columns_of(0).index(i)
        e_ref[0] = (left_ref if mine == 0 else left_other_ref)[pl.ds(i * BLK, BLK), pl.ds(n * BLK, BLK)]


def stage_kernel(*refs):
    got = dict(zip(DISTANCES, refs))
    out_ref = refs[-1]

    @for_own_parity
    def _(mine):
        for n, (name, place, _) in enumerate(STAGED[mine]):
            out_ref[n] = got[name][place]
        for n in range(len(STAGED[mine]), STAGED_SIZE):
            out_ref[n] = jnp.zeros((BLK, BLK), out_ref.dtype)


def outer_kernel(left_ref, left_other_ref, *rest):
    refs = {("left", True): left_ref, ("left", False): left_other_ref, **dict(zip(DISTANCES, rest))}
    out_ref, right = rest[len(DISTANCES) :]

    @for_own_parity
    def _(mine):
        for pair, js in enumerate(outer_pairs(mine)):
            total = columns_product(refs, right.at[pair], mine, js, lambda source: source != "staged")
            for i in range(BR):
                for y, j in enumerate(js):
                    if abs(i - j) <= HB:
                        out_ref[i * NCOL + columns_of(mine).index(j)] = block_of(total, i, y)


def multiply_kernel(slots, left_ref, left_other_ref, staged_ref, outer_ref, inner_ref, table_ref, out_ref, *rest):
    right, made, table, table_sem, out_sem = rest
    refs = {("left", True): left_ref, ("left", False): left_other_ref, "staged": staged_ref}
    load = pltpu.make_async_copy(table_ref, table, table_sem)
    load.start()
    made[BR * NCOL] = jnp.zeros((BLK, BLK), made.dtype)

    def store(source_ref, place):
        source = source_ref.at[table[0, SOURCES + place]]
        pltpu.make_async_copy(source, out_ref.at[0, table[0, place]], out_sem).start()

    @for_own_parity
    def _(mine):
        columns = columns_of(mine)
        pairs = outer_pairs(mine)
        inner = [n for n, j in enumerate(columns) if 0 <= j < BR]
        load.wait()
        for i in range(BR):
            for n in inner:
                store(inner_ref, i * NCOL + n)
        for pair, js in enumerate(pairs):
            total = columns_product(refs, right.at[pair], mine, js, lambda source: source == "staged")
            places = [(i, y, i * NCOL + columns.index(j)) for i in range(BR) for y, j in enumerate(js) if abs(i - j) <= HB]
            for i, y, place in places:
                made[place] = outer_ref[place] + block_of(total, i, y)
            for _, _, place in places:
                store(made, place)
        if len(stored_places(mine)) < slots:
            pltpu.make_async_copy(made.at[BR * NCOL], out_ref.at[0, table[0, BR * NCOL]], out_sem).start()

    pltpu.make_async_copy(made.at[pl.ds(0, slots)], out_ref.at[0], out_sem).wait()


def local(values, block_rows, block_cols, counts):
    slots = values.shape[1]
    row_count, col_count = lax.axis_size("row"), lax.axis_size("col")
    nblocks = BR * row_count
    smem = pl.BlockSpec(memory_space=pltpu.SMEM)
    vmem = pl.BlockSpec(memory_space=pltpu.VMEM)
    hbm = pl.BlockSpec(memory_space=pltpu.HBM)
    params = pltpu.CompilerParams(vmem_limit_bytes=VMEM_LIMIT)
    values, *places = (pltpu.with_memory_space_constraint(x, pltpu.HBM) for x in (values, block_rows, block_cols))
    index_scratch = [
        pltpu.SMEM((1, slots), jnp.int32),
        pltpu.SMEM((1, slots), jnp.int32),
        pltpu.SemaphoreType.DMA((2,)),
    ]
    table_shape = (1, BLK)

    def blocks(count, dtype=values.dtype):
        return jax.ShapeDtypeStruct((count, BLK, BLK), dtype)

    def cost(products, nbytes):
        return pl.CostEstimate(flops=2 * products * BLK**3, bytes_accessed=nbytes, transcendentals=0)

    def right_scratch(pairs):
        return pltpu.VMEM((pairs, 2, NCOL * BLK, 2 * BLK), values.dtype)

    *packed, left = pl.pallas_call(
        functools.partial(pack_kernel, nblocks, slots),
        out_shape=[blocks(SIZES[name]) for name in "abcd"]
        + [jax.ShapeDtypeStruct((BR * BLK, NCOL * BLK), values.dtype)],
        in_specs=[hbm] * 3,
        out_specs=[vmem] * 5,
        scratch_shapes=[
            pltpu.VMEM((slots + 1, BLK, BLK), values.dtype),
            pltpu.SMEM((BR * WIDTH + 1,), jnp.int32),
            *index_scratch,
            pltpu.SemaphoreType.DMA,
        ],
        compiler_params=params,
        name="pack",
    )(*places, values)

    def towards(name, message):
        pairs = []
        for r in range(row_count):
            for c in range(col_count):
                distance = DISTANCES[name] or (3 if (r + c) % 2 == 1 else -3)
                source = (r - distance if r % 2 == 1 else r + distance) % row_count
                pairs.append((source * col_count + c, r * col_count + c))
        return lax.ppermute(message, ("row", "col"), pairs)

    def swapped(block):
        return lax.ppermute(block, "col", [(0, 1), (1, 0)])

    left_other = swapped(left)
    got = [towards(name, message) for name, message in zip("abcd", packed)]
    message = pl.pallas_call(
        pack_e_kernel,
        out_shape=blocks(SIZES["e"]),
        in_specs=[vmem] * 2,
        out_specs=vmem,
        compiler_params=params,
        name="pack_e",
    )(left, left_other)
    got.append(towards("e", message))
    inner, table = pl.pallas_call(
        functools.partial(inner_kernel, nblocks, slots),
        out_shape=[blocks(BR * NCOL + 1, jnp.float32), jax.ShapeDtypeStruct(table_shape, jnp.int32)],
        in_specs=[hbm] * 2 + [smem] + [vmem] * 2,
        out_specs=[vmem] * 2,
        scratch_shapes=[
            pltpu.VMEM((2, NCOL * BLK, 2 * BLK), values.dtype),
            pltpu.SMEM(table_shape, jnp.int32),
            *index_scratch,
            pltpu.SemaphoreType.DMA,
        ],
        compiler_params=params,
        cost_estimate=cost(3 * 2 * 17, 4 * values.size),
        name="inner",
    )(*places, counts, left, left_other)
    *got, inner = lax.optimization_barrier((*got, inner))
    staged = swapped(
        pl.pallas_call(
            stage_kernel,
            out_shape=blocks(STAGED_SIZE),
            in_specs=[vmem] * 5,
            out_specs=vmem,
            compiler_params=params,
            name="stage",
        )(*got)
    )
    outer = pl.pallas_call(
        outer_kernel,
        out_shape=blocks(BR * NCOL, jnp.float32),
        in_specs=[vmem] * 7,
        out_specs=vmem,
        scratch_shapes=[right_scratch(4)],
        compiler_params=params,
        cost_estimate=cost(3 * 2 * 56, 10 * values.size),
        name="outer",
    )(left, left_other, *got)
    return pl.pallas_call(
        functools.partial(multiply_kernel, slots),
        out_shape=jax.ShapeDtypeStruct(values.shape, jnp.float32),
        in_specs=[vmem] * 6,
        out_specs=hbm,
        scratch_shapes=[
            right_scratch(4),
            pltpu.VMEM((BR * NCOL + 1, BLK, BLK), jnp.float32),
            pltpu.SMEM(table_shape, jnp.int32),
            pltpu.SemaphoreType.DMA,
            pltpu.SemaphoreType.DMA,
        ],
        compiler_params=params,
        name="multiply",
    )(left, left_other, staged, outer, inner, table)


def solution(mesh):
    return jax.shard_map(
        local,
        mesh=mesh,
        in_specs=(
            P(("parts", "row"), "col", None, None),
            P(("parts", "row"), "col"),
            P(("parts", "row"), "col"),
            P(("parts", "row"), "col"),
        ),
        out_specs=P(("parts", "row"), "col", None, None),
        check_vma=False,
    )
```

```python
import functools

import jax
import jax.numpy as jnp
from jax import lax
from jax.experimental import pallas as pl
from jax.experimental.pallas import tpu as pltpu
from jax.sharding import PartitionSpec as P

BLK = 128
BR = 3
HB = 7
WIDTH = 2 * HB + 1
LOW, HIGH = -HB, BR - 1 + HB
NCOL = 9
SOURCES = 32
VMEM_LIMIT = 12 * 2**20

DISTANCES = {"a": 1, "b": -1, "c": -2, "d": 2, "e": None}
SENT = {
    ("a", 1): [(3, 3), (5, 5), (3, 5), (3, 7), (4, 7), (5, 7), (3, 9), (4, 9), (5, 9), (3, -3), (3, -1), (4, -3), (5, -1)],
    ("a", 0): [(4, 4), (3, 4), (5, 4), (3, 6), (4, 6), (5, 6), (3, 8), (4, 8), (5, 8), (3, -2), (4, -2), (5, -2), (3, -4)],
    ("b", 1): [(-1, -1), (-3, -3), (-1, -3), (-1, -7), (-2, -7), (-3, -7)],
    ("b", 0): [(-2, -2), (-1, -2), (-3, -2), (-1, 4), (-1, -4), (-1, -6)],
    ("c", 1): [(-5, -5), (-4, -7), (-5, -7), (-6, -7), (-4, -3), (-5, -1), (-5, -3), (-6, -3)],
    ("c", 0): [(-4, -4), (-6, -6), (-4, -6), (-4, -2), (-5, -2), (-6, -2), (-5, -4), (-5, -6)],
    ("d", 1): [(6, 9), (7, 7), (7, 9), (8, 9), (6, -1)],
    ("d", 0): [(6, 6), (6, 8), (8, 8), (7, 6), (7, 8)],
    ("e", 1): [(9, 9)],
    ("e", 0): [(-7, -7)],
}
SIZES = {name: len(SENT[name, 1]) for name in DISTANCES}
STAGED = {
    parity: [
        (name, n, (k, j))
        for name in "acbde"
        for n, (k, j) in enumerate(SENT[name, parity])
        if k % 2 != j % 2 or (k, j) == (-7, -7)
    ]
    for parity in (0, 1)
}
EARLY = {parity: [found for found in STAGED[parity] if found[0] in "ac"] for parity in (0, 1)}
EARLY_SIZE = max(len(found) for found in EARLY.values())
STAGED_SIZE = max(len(found) for found in STAGED.values())


def columns_of(parity):
    return [j for j in range(LOW, HIGH + 1) if j % 2 == parity]


def own_parity():
    return (lax.axis_index("row") + lax.axis_index("col")) % 2


def for_own_parity(body):
    parity = own_parity()
    for mine in (0, 1):
        pl.when(parity == mine)(functools.partial(body, mine))


def slot_position(rows_ref, cols_ref, slot, nblocks):
    panel = lax.axis_index("row")
    row = rows_ref[0, slot] - panel * BR
    band = cols_ref[0, slot] - rows_ref[0, slot] + HB
    band = jnp.where(band < 0, band + nblocks, band)
    band = jnp.where(band >= nblocks, band - nblocks, band)
    odd = panel % 2 == 1
    return row, jnp.where(odd, BR - 1 - row, row), jnp.where(odd, WIDTH - 1 - band, band)


def index_copies(hbm_refs, smem_refs, sems):
    return [pltpu.make_async_copy(a, b, sems.at[i]) for i, (a, b) in enumerate(zip(hbm_refs, smem_refs))]


def pack_kernel(nblocks, slots, rows_ref, cols_ref, values_ref, *rest):
    out_refs = dict(zip("abcd", rest[:4]))
    left_ref, held, table, *index, sems, value_sem = rest[4:]
    copies = index_copies((rows_ref, cols_ref), index, sems)
    load = pltpu.make_async_copy(values_ref.at[0], held.at[pl.ds(0, slots)], value_sem)
    for copy in (*copies, load):
        copy.start()
    held[slots] = jnp.zeros((BLK, BLK), held.dtype)
    for i in range(BR * WIDTH + 1):
        table[i] = slots
    for copy in copies:
        copy.wait()
    for m in reversed(range(slots)):
        real_row, row, band = slot_position(*index, m, nblocks)
        table[jnp.where(real_row >= 0, row * WIDTH + band, BR * WIDTH)] = m
    load.wait()

    @for_own_parity
    def _(mine):
        for name, ref in out_refs.items():
            distance = DISTANCES[name]
            for n, (k, j) in enumerate(SENT[name, (mine + distance) % 2]):
                at = (k - BR * distance) * WIDTH + j - k + HB
                if distance % 2 == 1:
                    at = BR * WIDTH - 1 - at
                ref[n] = held[table[at]]
        columns = columns_of(mine)
        for i in range(BR):
            for n in range(NCOL):
                rows, cols = pl.ds(i * BLK, BLK), pl.ds(n * BLK, BLK)
                if n < len(columns) and abs(columns[n] - i) <= HB:
                    left_ref[rows, cols] = held[table[i * WIDTH + columns[n] - i + HB]]
                else:
                    left_ref[rows, cols] = jnp.zeros((BLK, BLK), left_ref.dtype)


def find_block(parity, k, j):
    if abs(k - j) > HB:
        return None
    if 0 <= k < BR:
        return ("left", parity == j % 2), (k, columns_of(j % 2).index(j)), False
    if 0 <= j < BR:
        return ("left", parity == k % 2), (j, columns_of(k % 2).index(k)), True
    for a, b, flip in ((k, j, False), (j, k, True)):
        for name in DISTANCES:
            if (a, b) in SENT[name, parity]:
                return name, SENT[name, parity].index((a, b)), flip
        staged = [position for _, _, position in STAGED[1 - parity]]
        if (a, b) in staged:
            return "staged", staged.index((a, b)), not flip
    raise AssertionError((k, j))


def columns_product(refs, right, parity, js, wanted):
    total = None
    for own in (True, False):
        kind = parity if own else 1 - parity
        found = {}
        for k in columns_of(kind):
            for j in js:
                place = find_block(parity, k, j)
                if place is not None and wanted(place[0]):
                    found[k, j] = place
        if not found:
            continue
        first, last = min(k for k, _ in found), max(k for k, _ in found)
        ks = [k for k in columns_of(kind) if first <= k <= last]
        side = right.at[0 if own else 1]
        for x, k in enumerate(ks):
            for y, j in enumerate(js):
                if (k, j) in found:
                    source, place, flip = found[k, j]
                    if isinstance(place, tuple):
                        block = refs[source][pl.ds(place[0] * BLK, BLK), pl.ds(place[1] * BLK, BLK)]
                    else:
                        block = refs[source][place]
                    block = block.T if flip else block
                else:
                    block = jnp.zeros((BLK, BLK), right.dtype)
                side[pl.ds(x * BLK, BLK), pl.ds(y * BLK, BLK)] = block
        start = columns_of(kind).index(first)
        part = jnp.dot(
            refs["left", own][:, pl.ds(start * BLK, len(ks) * BLK)],
            side[pl.ds(0, len(ks) * BLK), pl.ds(0, len(js) * BLK)],
            preferred_element_type=jnp.float32,
        )
        total = part if total is None else total + part
    return total


def block_of(total, i, y):
    return total[i * BLK : (i + 1) * BLK, y * BLK : (y + 1) * BLK]


def stored_places(parity):
    columns = columns_of(parity)
    return [i * NCOL + n for i in range(BR) for n, j in enumerate(columns) if abs(i - j) <= HB]


def inner_places(parity):
    return [i * NCOL + n for i in range(BR) for n, j in enumerate(columns_of(parity)) if 0 <= j < BR]


def store(made, table, out_ref, place, sem):
    source = made.at[table[0, SOURCES + place]]
    pltpu.make_async_copy(source, out_ref.at[0, table[0, place]], sem).start()


def wait_for(count, made, out_ref, sem):
    pltpu.make_async_copy(made.at[pl.ds(0, count)], out_ref.at[0, pl.ds(0, count)], sem).wait()


def outer_pairs(parity):
    outer = [j for j in columns_of(parity) if not 0 <= j < BR]
    return [outer[n : n + 2] for n in range(0, len(outer), 2)]


def inner_kernel(nblocks, slots, rows_ref, cols_ref, counts_ref, left_ref, left_other_ref, *rest):
    table_ref, out_ref, right, made, table, *index, sems, table_sem, out_sem = rest
    copies = index_copies((rows_ref, cols_ref), index, sems)
    for copy in copies:
        copy.start()
    refs = {("left", True): left_ref, ("left", False): left_other_ref}

    @for_own_parity
    def _(mine):
        js = [j for j in columns_of(mine) if 0 <= j < BR]
        total = columns_product(refs, right, mine, js, lambda source: True)
        for i in range(BR):
            for y in range(2):
                if y < len(js):
                    made[i * NCOL + columns_of(mine).index(js[y])] = block_of(total, i, y)
        made[BR * NCOL] = jnp.zeros((BLK, BLK), made.dtype)

    for copy in copies:
        copy.wait()
    for place in range(BR * NCOL + 1):
        table[0, place] = -1
    count = counts_ref[0, 0]
    for m in range(slots):
        _, row, band = slot_position(*index, m, nblocks)
        table[0, jnp.where(m < count, row * NCOL + (row + band) // 2, BR * NCOL)] = m

    @for_own_parity
    def _(mine):
        unused = count
        for place in stored_places(mine):
            slot = table[0, place]
            absent = slot < 0
            table[0, place] = jnp.where(absent, unused, slot)
            table[0, SOURCES + place] = jnp.where(absent, BR * NCOL, place)
            unused = jnp.where(absent, unused + 1, unused)
        table[0, BR * NCOL] = unused
        here = [place for place in stored_places(mine) if place in inner_places(mine)]
        for place in here:
            store(made, table, out_ref, place, out_sem)
        stored = len(here)
        if len(stored_places(mine)) < slots:
            pltpu.make_async_copy(made.at[BR * NCOL], out_ref.at[0, unused], out_sem).start()
            stored += 1
        wait_for(stored, made, out_ref, out_sem)

    copy = pltpu.make_async_copy(table, table_ref, table_sem)
    copy.start()
    copy.wait()


def pack_e_kernel(left_ref, left_other_ref, e_ref):
    @for_own_parity
    def _(mine):
        i = 2 if mine == 0 else 0
        n = columns_of(0).index(i)
        e_ref[0] = (left_ref if mine == 0 else left_other_ref)[pl.ds(i * BLK, BLK), pl.ds(n * BLK, BLK)]


def stage_early_kernel(a_ref, c_ref, out_ref):
    got = {"a": a_ref, "c": c_ref}

    @for_own_parity
    def _(mine):
        for n in range(EARLY_SIZE):
            if n < len(EARLY[mine]):
                name, place, _ = EARLY[mine][n]
                out_ref[n] = got[name][place].T
            else:
                out_ref[n] = jnp.zeros((BLK, BLK), out_ref.dtype)


def stage_kernel(early_ref, b_ref, d_ref, e_ref, out_ref):
    got = {"b": b_ref, "d": d_ref, "e": e_ref}

    @for_own_parity
    def _(mine):
        for n in range(STAGED_SIZE):
            if n < len(EARLY[mine]):
                out_ref[n] = early_ref[n]
            elif n < len(STAGED[mine]):
                name, place, _ = STAGED[mine][n]
                out_ref[n] = got[name][place].T
            else:
                out_ref[n] = jnp.zeros((BLK, BLK), out_ref.dtype)


def outer_kernel(left_ref, left_other_ref, *rest):
    refs = {("left", True): left_ref, ("left", False): left_other_ref, **dict(zip(DISTANCES, rest))}
    out_ref, right = rest[len(DISTANCES) :]

    @for_own_parity
    def _(mine):
        for pair, js in enumerate(outer_pairs(mine)):
            total = columns_product(refs, right.at[pair], mine, js, lambda source: source != "staged")
            for i in range(BR):
                for y, j in enumerate(js):
                    if abs(i - j) <= HB:
                        out_ref[i * NCOL + columns_of(mine).index(j)] = block_of(total, i, y)


def multiply_kernel(left_ref, left_other_ref, staged_ref, outer_ref, table_ref, _, out_ref, *rest):
    right, made, table, table_sem, out_sem = rest
    refs = {("left", True): left_ref, ("left", False): left_other_ref, "staged": staged_ref}
    load = pltpu.make_async_copy(table_ref, table, table_sem)
    load.start()
    made[BR * NCOL] = jnp.zeros((BLK, BLK), made.dtype)

    @for_own_parity
    def _(mine):
        for pair, js in enumerate(outer_pairs(mine)):
            total = columns_product(refs, right.at[pair], mine, js, lambda source: source == "staged")
            for i in range(BR):
                for y, j in enumerate(js):
                    if abs(i - j) <= HB:
                        place = i * NCOL + columns_of(mine).index(j)
                        made[place] = outer_ref[place] + block_of(total, i, y)
        load.wait()
        here = [place for place in stored_places(mine) if place not in inner_places(mine)]
        for place in here:
            store(made, table, out_ref, place, out_sem)
        wait_for(len(here), made, out_ref, out_sem)


def local(values, block_rows, block_cols, counts):
    slots = values.shape[1]
    row_count, col_count = lax.axis_size("row"), lax.axis_size("col")
    nblocks = BR * row_count
    smem = pl.BlockSpec(memory_space=pltpu.SMEM)
    vmem = pl.BlockSpec(memory_space=pltpu.VMEM)
    hbm = pl.BlockSpec(memory_space=pltpu.HBM)
    params = pltpu.CompilerParams(vmem_limit_bytes=VMEM_LIMIT)
    values, *places = (pltpu.with_memory_space_constraint(x, pltpu.HBM) for x in (values, block_rows, block_cols))
    index_scratch = [
        pltpu.SMEM((1, slots), jnp.int32),
        pltpu.SMEM((1, slots), jnp.int32),
        pltpu.SemaphoreType.DMA((2,)),
    ]
    table_shape = (1, BLK)

    def blocks(count, dtype=values.dtype):
        return jax.ShapeDtypeStruct((count, BLK, BLK), dtype)

    def cost(products, nbytes):
        return pl.CostEstimate(flops=2 * products * BLK**3, bytes_accessed=nbytes, transcendentals=0)

    def right_scratch(pairs):
        return pltpu.VMEM((pairs, 2, NCOL * BLK, 2 * BLK), values.dtype)

    *packed, left = pl.pallas_call(
        functools.partial(pack_kernel, nblocks, slots),
        out_shape=[blocks(SIZES[name]) for name in "abcd"]
        + [jax.ShapeDtypeStruct((BR * BLK, NCOL * BLK), values.dtype)],
        in_specs=[hbm] * 3,
        out_specs=[vmem] * 5,
        scratch_shapes=[
            pltpu.VMEM((slots + 1, BLK, BLK), values.dtype),
            pltpu.SMEM((BR * WIDTH + 1,), jnp.int32),
            *index_scratch,
            pltpu.SemaphoreType.DMA,
        ],
        compiler_params=params,
        name="pack",
    )(*places, values)

    def towards(name, message):
        pairs = []
        for r in range(row_count):
            for c in range(col_count):
                distance = DISTANCES[name] or (3 if (r + c) % 2 == 1 else -3)
                source = (r - distance if r % 2 == 1 else r + distance) % row_count
                pairs.append((source * col_count + c, r * col_count + c))
        return lax.ppermute(message, ("row", "col"), pairs)

    def swapped(block):
        return lax.ppermute(block, "col", [(0, 1), (1, 0)])

    left_other = swapped(left)
    got = [towards(name, message) for name, message in zip("abcd", packed)]
    message = pl.pallas_call(
        pack_e_kernel,
        out_shape=blocks(SIZES["e"]),
        in_specs=[vmem] * 2,
        out_specs=vmem,
        compiler_params=params,
        name="pack_e",
    )(left, left_other)
    got.append(towards("e", message))
    table, out = pl.pallas_call(
        functools.partial(inner_kernel, nblocks, slots),
        out_shape=[jax.ShapeDtypeStruct(table_shape, jnp.int32), jax.ShapeDtypeStruct(values.shape, jnp.float32)],
        in_specs=[hbm] * 2 + [smem] + [vmem] * 2,
        out_specs=[vmem, hbm],
        scratch_shapes=[
            pltpu.VMEM((2, NCOL * BLK, 2 * BLK), values.dtype),
            pltpu.VMEM((BR * NCOL + 1, BLK, BLK), jnp.float32),
            pltpu.SMEM(table_shape, jnp.int32),
            *index_scratch,
            pltpu.SemaphoreType.DMA,
            pltpu.SemaphoreType.DMA,
        ],
        compiler_params=params,
        cost_estimate=cost(3 * 2 * 17, 4 * values.size),
        name="inner",
    )(*places, counts, left, left_other)
    a, b, c, d, e = got
    a, c, table = lax.optimization_barrier((a, c, table))
    early = pl.pallas_call(
        stage_early_kernel,
        out_shape=blocks(EARLY_SIZE),
        in_specs=[vmem] * 2,
        out_specs=vmem,
        compiler_params=params,
        name="stage_early",
    )(a, c)
    b, d, e, early = lax.optimization_barrier((b, d, e, early))
    got = [a, b, c, d, e]
    staged = swapped(
        pl.pallas_call(
            stage_kernel,
            out_shape=blocks(STAGED_SIZE),
            in_specs=[vmem] * 4,
            out_specs=vmem,
            compiler_params=params,
            name="stage",
        )(early, b, d, e)
    )
    outer = pl.pallas_call(
        outer_kernel,
        out_shape=blocks(BR * NCOL, jnp.float32),
        in_specs=[vmem] * 7,
        out_specs=vmem,
        scratch_shapes=[right_scratch(4)],
        compiler_params=params,
        cost_estimate=cost(3 * 2 * 56, 10 * values.size),
        name="outer",
    )(left, left_other, *got)
    return pl.pallas_call(
        multiply_kernel,
        out_shape=jax.ShapeDtypeStruct(values.shape, jnp.float32),
        in_specs=[vmem] * 5 + [hbm],
        out_specs=hbm,
        scratch_shapes=[
            right_scratch(4),
            pltpu.VMEM((BR * NCOL + 1, BLK, BLK), jnp.float32),
            pltpu.SMEM(table_shape, jnp.int32),
            pltpu.SemaphoreType.DMA,
            pltpu.SemaphoreType.DMA,
        ],
        input_output_aliases={5: 0},
        compiler_params=params,
        name="multiply",
    )(left, left_other, staged, outer, table, out)


def solution(mesh):
    return jax.shard_map(
        local,
        mesh=mesh,
        in_specs=(
            P(("parts", "row"), "col", None, None),
            P(("parts", "row"), "col"),
            P(("parts", "row"), "col"),
            P(("parts", "row"), "col"),
        ),
        out_specs=P(("parts", "row"), "col", None, None),
        check_vma=False,
    )
```

```python
import functools

import jax
import jax.numpy as jnp
from jax import lax
from jax.experimental import pallas as pl
from jax.experimental.pallas import tpu as pltpu
from jax.sharding import PartitionSpec as P

BLK = 128
BR = 3
HB = 7
WIDTH = 2 * HB + 1
LOW, HIGH = -HB, BR - 1 + HB
NCOL = 9
SOURCES = 32
EARLY_COST = 500
VMEM_LIMIT = 12 * 2**20

DISTANCES = {"a": 1, "b": -1, "c": -2, "d": 2, "e": None}
SENT = {
    ("a", 1): [(3, 3), (5, 5), (3, 5), (3, 7), (3, 9), (4, 9), (5, 9), (3, -3), (3, -1), (4, -3), (4, -1), (5, -1)],
    ("a", 0): [(4, 4), (3, 4), (5, 4), (3, 6), (4, 6), (5, 6), (3, 8), (4, 8), (5, 8), (3, -2), (5, -2), (3, -4)],
    ("b", 1): [(-1, -1), (-3, -3), (-1, -3), (-1, -7), (-2, -7), (-3, -7), (-1, -5), (-2, -5)],
    ("b", 0): [(-2, -2), (-1, -2), (-3, -2), (-2, 4), (-1, -4), (-3, -4), (-1, -6), (-3, -6)],
    ("c", 1): [(-5, -5), (-4, -7), (-5, -7), (-6, -7), (-5, -3), (-4, -5)],
    ("c", 0): [(-4, -4), (-6, -6), (-4, -6), (-4, -2), (-6, -2), (-5, -6)],
    ("d", 1): [(7, 7), (6, 9), (7, 9), (8, 9), (6, -1), (7, 5)],
    ("d", 0): [(6, 6), (8, 8), (6, 8), (7, 6), (7, 8), (7, 4)],
    ("e", 1): [(9, 9)],
    ("e", 0): [(-7, -7)],
}
PERMUTES = ("a", "f", "g", "b", "e")
SIZES = {name: len(SENT[name, 1]) for name in DISTANCES}
SIZES["f"] = SIZES["g"] = SIZES["c"]
STAGED = {
    parity: [
        (name, n, (k, j))
        for name in "acbde"
        for n, (k, j) in enumerate(SENT[name, parity])
        if k % 2 != j % 2 or (k, j) == (-7, -7)
    ]
    for parity in (0, 1)
}
EARLY = {parity: [found for found in STAGED[parity] if found[0] == "a"] for parity in (0, 1)}
EARLY_SIZE = max(len(found) for found in EARLY.values())
STAGED_SIZE = max(len(found) for found in STAGED.values())


def columns_of(parity):
    return [j for j in range(LOW, HIGH + 1) if j % 2 == parity]


def own_parity():
    return (lax.axis_index("row") + lax.axis_index("col")) % 2


def c_is_in_f():
    return lax.axis_index("col") == 0


def for_own_parity(body):
    parity = own_parity()
    for mine in (0, 1):
        pl.when(parity == mine)(functools.partial(body, mine))


def slot_position(rows_ref, cols_ref, slot, nblocks):
    panel = lax.axis_index("row")
    row = rows_ref[0, slot] - panel * BR
    band = cols_ref[0, slot] - rows_ref[0, slot] + HB
    band = jnp.where(band < 0, band + nblocks, band)
    band = jnp.where(band >= nblocks, band - nblocks, band)
    odd = panel % 2 == 1
    return row, jnp.where(odd, BR - 1 - row, row), jnp.where(odd, WIDTH - 1 - band, band)


def index_copies(hbm_refs, smem_refs, sems):
    return [pltpu.make_async_copy(a, b, sems.at[i]) for i, (a, b) in enumerate(zip(hbm_refs, smem_refs))]


def place_at_sender(name, k, j):
    distance = DISTANCES[name]
    place = (k - BR * distance) * WIDTH + j - k + HB
    return BR * WIDTH - 1 - place if distance % 2 == 1 else place


def pack_kernel(nblocks, slots, rows_ref, cols_ref, values_ref, *rest):
    out_refs = dict(zip(PERMUTES, rest[:4]))
    left_ref, held, table, *index, sems, value_sem = rest[4:]
    copies = index_copies((rows_ref, cols_ref), index, sems)
    load = pltpu.make_async_copy(values_ref.at[0], held.at[pl.ds(0, slots)], value_sem)
    for copy in (*copies, load):
        copy.start()
    held[slots] = jnp.zeros((BLK, BLK), held.dtype)
    for i in range(BR * WIDTH + 1):
        table[i] = slots
    for copy in copies:
        copy.wait()
    for m in reversed(range(slots)):
        real_row, row, band = slot_position(*index, m, nblocks)
        table[jnp.where(real_row >= 0, row * WIDTH + band, BR * WIDTH)] = m
    load.wait()

    @for_own_parity
    def _(mine):
        for name in "ab":
            for n, (k, j) in enumerate(SENT[name, 1 - mine]):
                out_refs[name][n] = held[table[place_at_sender(name, k, j)]]
        for n in range(SIZES["f"]):
            c, d = (place_at_sender(name, *SENT[name, mine][n]) for name in "cd")
            out_refs["f"][n] = held[table[jnp.where(c_is_in_f(), c, d)]]
            out_refs["g"][n] = held[table[jnp.where(c_is_in_f(), d, c)]]
        columns = columns_of(mine)
        for i in range(BR):
            for n in range(NCOL):
                rows, cols = pl.ds(i * BLK, BLK), pl.ds(n * BLK, BLK)
                if n < len(columns) and abs(columns[n] - i) <= HB:
                    left_ref[rows, cols] = held[table[i * WIDTH + columns[n] - i + HB]]
                else:
                    left_ref[rows, cols] = jnp.zeros((BLK, BLK), left_ref.dtype)


def find_block(parity, k, j):
    if abs(k - j) > HB:
        return None
    if 0 <= k < BR:
        return ("left", parity == j % 2), (k, columns_of(j % 2).index(j)), False
    if 0 <= j < BR:
        return ("left", parity == k % 2), (j, columns_of(k % 2).index(k)), True
    for a, b, flip in ((k, j, False), (j, k, True)):
        for name in DISTANCES:
            if (a, b) in SENT[name, parity]:
                return name, SENT[name, parity].index((a, b)), flip
        staged = [position for _, _, position in STAGED[1 - parity]]
        if (a, b) in staged:
            return "staged", staged.index((a, b)), not flip
    raise AssertionError((k, j))


def read_block(refs, source, place):
    if isinstance(place, tuple):
        return refs[source][pl.ds(place[0] * BLK, BLK), pl.ds(place[1] * BLK, BLK)]
    if source in ("c", "d"):
        f, g = refs["f"][place], refs["g"][place]
        return jnp.where(c_is_in_f(), *((f, g) if source == "c" else (g, f)))
    return refs[source][place]


def columns_product(refs, right, parity, js, wanted):
    total = None
    for own in (True, False):
        kind = parity if own else 1 - parity
        found = {}
        for k in columns_of(kind):
            for j in js:
                place = find_block(parity, k, j)
                if place is not None and wanted(place[0]):
                    found[k, j] = place
        if not found:
            continue
        first, last = min(k for k, _ in found), max(k for k, _ in found)
        ks = [k for k in columns_of(kind) if first <= k <= last]
        side = right.at[0 if own else 1]
        for x, k in enumerate(ks):
            for y, j in enumerate(js):
                if (k, j) in found:
                    source, place, flip = found[k, j]
                    block = read_block(refs, source, place)
                    block = block.T if flip else block
                else:
                    block = jnp.zeros((BLK, BLK), right.dtype)
                side[pl.ds(x * BLK, BLK), pl.ds(y * BLK, BLK)] = block
        start = columns_of(kind).index(first)
        part = jnp.dot(
            refs["left", own][:, pl.ds(start * BLK, len(ks) * BLK)],
            side[pl.ds(0, len(ks) * BLK), pl.ds(0, len(js) * BLK)],
            preferred_element_type=jnp.float32,
        )
        total = part if total is None else total + part
    return total


def block_of(total, i, y):
    return total[i * BLK : (i + 1) * BLK, y * BLK : (y + 1) * BLK]


def stored_places(parity):
    columns = columns_of(parity)
    return [i * NCOL + n for i in range(BR) for n, j in enumerate(columns) if abs(i - j) <= HB]


def inner_places(parity):
    return [i * NCOL + n for i in range(BR) for n, j in enumerate(columns_of(parity)) if 0 <= j < BR]


def store(made, table, out_ref, place, sem):
    source = made.at[table[0, SOURCES + place]]
    pltpu.make_async_copy(source, out_ref.at[0, table[0, place]], sem).start()


def wait_for(count, made, out_ref, sem):
    pltpu.make_async_copy(made.at[pl.ds(0, count)], out_ref.at[0, pl.ds(0, count)], sem).wait()


def outer_pairs(parity):
    outer = [j for j in columns_of(parity) if not 0 <= j < BR]
    return [outer[n : n + 2] for n in range(0, len(outer), 2)]


def inner_kernel(nblocks, slots, rows_ref, cols_ref, counts_ref, left_ref, left_other_ref, *rest):
    table_ref, out_ref, right, made, table, *index, sems, table_sem, out_sem = rest
    copies = index_copies((rows_ref, cols_ref), index, sems)
    for copy in copies:
        copy.start()
    refs = {("left", True): left_ref, ("left", False): left_other_ref}

    @for_own_parity
    def _(mine):
        js = [j for j in columns_of(mine) if 0 <= j < BR]
        total = columns_product(refs, right, mine, js, lambda source: True)
        for i in range(BR):
            for y in range(2):
                if y < len(js):
                    made[i * NCOL + columns_of(mine).index(js[y])] = block_of(total, i, y)
        made[BR * NCOL] = jnp.zeros((BLK, BLK), made.dtype)

    for copy in copies:
        copy.wait()
    for place in range(BR * NCOL + 1):
        table[0, place] = -1
    count = counts_ref[0, 0]
    for m in range(slots):
        _, row, band = slot_position(*index, m, nblocks)
        table[0, jnp.where(m < count, row * NCOL + (row + band) // 2, BR * NCOL)] = m

    @for_own_parity
    def _(mine):
        unused = count
        for place in stored_places(mine):
            slot = table[0, place]
            absent = slot < 0
            table[0, place] = jnp.where(absent, unused, slot)
            table[0, SOURCES + place] = jnp.where(absent, BR * NCOL, place)
            unused = jnp.where(absent, unused + 1, unused)
        table[0, BR * NCOL] = unused
        here = [place for place in stored_places(mine) if place in inner_places(mine)]
        for place in here:
            store(made, table, out_ref, place, out_sem)
        stored = len(here)
        if len(stored_places(mine)) < slots:
            pltpu.make_async_copy(made.at[BR * NCOL], out_ref.at[0, unused], out_sem).start()
            stored += 1
        wait_for(stored, made, out_ref, out_sem)

    copy = pltpu.make_async_copy(table, table_ref, table_sem)
    copy.start()
    copy.wait()


def pack_e_kernel(left_ref, left_other_ref, e_ref):
    @for_own_parity
    def _(mine):
        i = 2 if mine == 0 else 0
        n = columns_of(0).index(i)
        e_ref[0] = (left_ref if mine == 0 else left_other_ref)[pl.ds(i * BLK, BLK), pl.ds(n * BLK, BLK)]


def stage_early_kernel(a_ref, out_ref):
    @for_own_parity
    def _(mine):
        for n in range(EARLY_SIZE):
            if n < len(EARLY[mine]):
                out_ref[n] = a_ref[EARLY[mine][n][1]].T
            else:
                out_ref[n] = jnp.zeros((BLK, BLK), out_ref.dtype)


def stage_kernel(early_ref, *refs):
    got = dict(zip(PERMUTES[1:], refs))
    out_ref = refs[-1]

    @for_own_parity
    def _(mine):
        for n in range(STAGED_SIZE):
            if n < len(EARLY[mine]):
                out_ref[n] = early_ref[n]
            elif n < len(STAGED[mine]):
                name, place, _ = STAGED[mine][n]
                out_ref[n] = read_block(got, name, place).T
            else:
                out_ref[n] = jnp.zeros((BLK, BLK), out_ref.dtype)


def outer_kernel(left_ref, left_other_ref, *rest):
    refs = {("left", True): left_ref, ("left", False): left_other_ref, **dict(zip(PERMUTES, rest))}
    out_ref, right = rest[len(PERMUTES) :]

    @for_own_parity
    def _(mine):
        for pair, js in enumerate(outer_pairs(mine)):
            total = columns_product(refs, right.at[pair], mine, js, lambda source: source != "staged")
            for i in range(BR):
                for y, j in enumerate(js):
                    if abs(i - j) <= HB:
                        out_ref[i * NCOL + columns_of(mine).index(j)] = block_of(total, i, y)


def multiply_kernel(left_ref, left_other_ref, staged_ref, outer_ref, table_ref, _, out_ref, *rest):
    right, made, table, table_sem, out_sem = rest
    refs = {("left", True): left_ref, ("left", False): left_other_ref, "staged": staged_ref}
    load = pltpu.make_async_copy(table_ref, table, table_sem)
    load.start()
    made[BR * NCOL] = jnp.zeros((BLK, BLK), made.dtype)

    @for_own_parity
    def _(mine):
        for pair, js in enumerate(outer_pairs(mine)):
            total = columns_product(refs, right.at[pair], mine, js, lambda source: source == "staged")
            for i in range(BR):
                for y, j in enumerate(js):
                    if abs(i - j) <= HB:
                        place = i * NCOL + columns_of(mine).index(j)
                        made[place] = outer_ref[place] + block_of(total, i, y)
        load.wait()
        here = [place for place in stored_places(mine) if place not in inner_places(mine)]
        for place in here:
            store(made, table, out_ref, place, out_sem)
        wait_for(len(here), made, out_ref, out_sem)


def local(values, block_rows, block_cols, counts):
    slots = values.shape[1]
    row_count, col_count = lax.axis_size("row"), lax.axis_size("col")
    nblocks = BR * row_count
    smem = pl.BlockSpec(memory_space=pltpu.SMEM)
    vmem = pl.BlockSpec(memory_space=pltpu.VMEM)
    hbm = pl.BlockSpec(memory_space=pltpu.HBM)
    params = pltpu.CompilerParams(vmem_limit_bytes=VMEM_LIMIT)
    values, *places = (pltpu.with_memory_space_constraint(x, pltpu.HBM) for x in (values, block_rows, block_cols))
    index_scratch = [
        pltpu.SMEM((1, slots), jnp.int32),
        pltpu.SMEM((1, slots), jnp.int32),
        pltpu.SemaphoreType.DMA((2,)),
    ]
    table_shape = (1, BLK)

    def blocks(count, dtype=values.dtype):
        return jax.ShapeDtypeStruct((count, BLK, BLK), dtype)

    def cost(products, nbytes):
        return pl.CostEstimate(flops=2 * products * BLK**3, bytes_accessed=nbytes, transcendentals=0)

    def right_scratch(pairs):
        return pltpu.VMEM((pairs, 2, NCOL * BLK, 2 * BLK), values.dtype)

    *packed, left = pl.pallas_call(
        functools.partial(pack_kernel, nblocks, slots),
        out_shape=[blocks(SIZES[name]) for name in PERMUTES[:4]]
        + [jax.ShapeDtypeStruct((BR * BLK, NCOL * BLK), values.dtype)],
        in_specs=[hbm] * 3,
        out_specs=[vmem] * 5,
        scratch_shapes=[
            pltpu.VMEM((slots + 1, BLK, BLK), values.dtype),
            pltpu.SMEM((BR * WIDTH + 1,), jnp.int32),
            *index_scratch,
            pltpu.SemaphoreType.DMA,
        ],
        compiler_params=params,
        name="pack",
    )(*places, values)

    def towards(name, message):
        pairs = []
        for r in range(row_count):
            for c in range(col_count):
                if name in ("f", "g"):
                    distance = DISTANCES["c" if (name == "f") == (c == 0) else "d"]
                else:
                    distance = DISTANCES[name] or (3 if (r + c) % 2 == 1 else -3)
                source = (r - distance if r % 2 == 1 else r + distance) % row_count
                pairs.append((source * col_count + c, r * col_count + c))
        return lax.ppermute(message, ("row", "col"), pairs)

    def swapped(block):
        return lax.ppermute(block, "col", [(0, 1), (1, 0)])

    left_other = swapped(left)
    got = [towards(name, message) for name, message in zip(PERMUTES, packed)]
    message = pl.pallas_call(
        pack_e_kernel,
        out_shape=blocks(SIZES["e"]),
        in_specs=[vmem] * 2,
        out_specs=vmem,
        compiler_params=params,
        name="pack_e",
    )(left, left_other)
    got.append(towards("e", message))
    table, out = pl.pallas_call(
        functools.partial(inner_kernel, nblocks, slots),
        out_shape=[jax.ShapeDtypeStruct(table_shape, jnp.int32), jax.ShapeDtypeStruct(values.shape, jnp.float32)],
        in_specs=[hbm] * 2 + [smem] + [vmem] * 2,
        out_specs=[vmem, hbm],
        scratch_shapes=[
            pltpu.VMEM((2, NCOL * BLK, 2 * BLK), values.dtype),
            pltpu.VMEM((BR * NCOL + 1, BLK, BLK), jnp.float32),
            pltpu.SMEM(table_shape, jnp.int32),
            *index_scratch,
            pltpu.SemaphoreType.DMA,
            pltpu.SemaphoreType.DMA,
        ],
        compiler_params=params,
        cost_estimate=cost(3 * 2 * 17, 4 * values.size),
        name="inner",
    )(*places, counts, left, left_other)
    a, f, g, b, e = got
    a, f, table = lax.optimization_barrier((a, f, table))
    early = pl.pallas_call(
        stage_early_kernel,
        out_shape=blocks(EARLY_SIZE),
        in_specs=[vmem],
        out_specs=vmem,
        compiler_params=params,
        cost_estimate=cost(EARLY_COST, 0),
        name="stage_early",
    )(a)
    f, g, b, e, early = lax.optimization_barrier((f, g, b, e, early))
    got = [a, f, g, b, e]
    staged = swapped(
        pl.pallas_call(
            stage_kernel,
            out_shape=blocks(STAGED_SIZE),
            in_specs=[vmem] * 5,
            out_specs=vmem,
            compiler_params=params,
            name="stage",
        )(early, f, g, b, e)
    )
    outer = pl.pallas_call(
        outer_kernel,
        out_shape=blocks(BR * NCOL, jnp.float32),
        in_specs=[vmem] * 7,
        out_specs=vmem,
        scratch_shapes=[right_scratch(4)],
        compiler_params=params,
        cost_estimate=cost(3 * 2 * 56, 10 * values.size),
        name="outer",
    )(left, left_other, *got)
    return pl.pallas_call(
        multiply_kernel,
        out_shape=jax.ShapeDtypeStruct(values.shape, jnp.float32),
        in_specs=[vmem] * 5 + [hbm],
        out_specs=hbm,
        scratch_shapes=[
            right_scratch(4),
            pltpu.VMEM((BR * NCOL + 1, BLK, BLK), jnp.float32),
            pltpu.SMEM(table_shape, jnp.int32),
            pltpu.SemaphoreType.DMA,
            pltpu.SemaphoreType.DMA,
        ],
        input_output_aliases={5: 0},
        compiler_params=params,
        name="multiply",
    )(left, left_other, staged, outer, table, out)


def solution(mesh):
    return jax.shard_map(
        local,
        mesh=mesh,
        in_specs=(
            P(("parts", "row"), "col", None, None),
            P(("parts", "row"), "col"),
            P(("parts", "row"), "col"),
            P(("parts", "row"), "col"),
        ),
        out_specs=P(("parts", "row"), "col", None, None),
        check_vma=False,
    )
```

```python
import functools

import jax
import jax.numpy as jnp
from jax import lax
from jax.experimental import pallas as pl
from jax.experimental.pallas import tpu as pltpu
from jax.sharding import PartitionSpec as P

BLK = 128
BR = 3
HB = 7
WIDTH = 2 * HB + 1
LOW, HIGH = -HB, BR - 1 + HB
NCOL = 9
SOURCES = 32
EARLY_COST = 1
LATE_COST = 4000
VMEM_LIMIT = 12 * 2**20

DISTANCES = {"a": 1, "b": -1, "c": -2, "d": 2, "e": None}
SENT = {
    ("a", 1): [(3, 3), (5, 5), (3, 5), (3, 7), (4, 7), (5, 7), (3, 9), (4, 9), (5, 9), (3, -3), (3, -1), (4, -3), (5, -1)],
    ("a", 0): [(4, 4), (3, 4), (5, 4), (3, 6), (4, 6), (5, 6), (3, 8), (4, 8), (5, 8), (3, -2), (4, -2), (5, -2), (3, -4)],
    ("b", 1): [(-1, -1), (-3, -3), (-1, -3), (-1, -7), (-2, -7), (-3, -7)],
    ("b", 0): [(-2, -2), (-1, -2), (-3, -2), (-1, 4), (-1, -4), (-1, -6)],
    ("c", 1): [(-5, -5), (-4, -7), (-5, -7), (-6, -7), (-4, -3), (-5, -1), (-5, -3), (-6, -3)],
    ("c", 0): [(-4, -4), (-6, -6), (-4, -6), (-4, -2), (-5, -2), (-6, -2), (-5, -4), (-5, -6)],
    ("d", 1): [(6, 9), (7, 7), (7, 9), (8, 9), (6, -1)],
    ("d", 0): [(6, 6), (6, 8), (8, 8), (7, 6), (7, 8)],
    ("e", 1): [(9, 9)],
    ("e", 0): [(-7, -7)],
}
SIZES = {name: len(SENT[name, 1]) for name in DISTANCES}
PARTS = {"early": "ac", "late": "bde"}
STAGED = {
    (part, parity): [
        (name, n, (k, j))
        for name in names
        for n, (k, j) in enumerate(SENT[name, parity])
        if k % 2 != j % 2 or (k, j) == (-7, -7)
    ]
    for part, names in PARTS.items()
    for parity in (0, 1)
}
STAGED_SIZE = {part: max(len(STAGED[part, parity]) for parity in (0, 1)) for part in PARTS}


def columns_of(parity):
    return [j for j in range(LOW, HIGH + 1) if j % 2 == parity]


def own_parity():
    return (lax.axis_index("row") + lax.axis_index("col")) % 2


def for_own_parity(body):
    parity = own_parity()
    for mine in (0, 1):
        pl.when(parity == mine)(functools.partial(body, mine))


def slot_position(rows_ref, cols_ref, slot, nblocks):
    panel = lax.axis_index("row")
    row = rows_ref[0, slot] - panel * BR
    band = cols_ref[0, slot] - rows_ref[0, slot] + HB
    band = jnp.where(band < 0, band + nblocks, band)
    band = jnp.where(band >= nblocks, band - nblocks, band)
    odd = panel % 2 == 1
    return row, jnp.where(odd, BR - 1 - row, row), jnp.where(odd, WIDTH - 1 - band, band)


def index_copies(hbm_refs, smem_refs, sems):
    return [pltpu.make_async_copy(a, b, sems.at[i]) for i, (a, b) in enumerate(zip(hbm_refs, smem_refs))]


def pack_kernel(nblocks, slots, rows_ref, cols_ref, values_ref, *rest):
    out_refs = dict(zip("abcd", rest[:4]))
    left_ref, held, table, *index, sems, value_sem = rest[4:]
    copies = index_copies((rows_ref, cols_ref), index, sems)
    load = pltpu.make_async_copy(values_ref.at[0], held.at[pl.ds(0, slots)], value_sem)
    for copy in (*copies, load):
        copy.start()
    held[slots] = jnp.zeros((BLK, BLK), held.dtype)
    for i in range(BR * WIDTH + 1):
        table[i] = slots
    for copy in copies:
        copy.wait()
    for m in reversed(range(slots)):
        real_row, row, band = slot_position(*index, m, nblocks)
        table[jnp.where(real_row >= 0, row * WIDTH + band, BR * WIDTH)] = m
    load.wait()

    @for_own_parity
    def _(mine):
        for name, ref in out_refs.items():
            distance = DISTANCES[name]
            for n, (k, j) in enumerate(SENT[name, (mine + distance) % 2]):
                at = (k - BR * distance) * WIDTH + j - k + HB
                if distance % 2 == 1:
                    at = BR * WIDTH - 1 - at
                ref[n] = held[table[at]]
        columns = columns_of(mine)
        for i in range(BR):
            for n in range(NCOL):
                rows, cols = pl.ds(i * BLK, BLK), pl.ds(n * BLK, BLK)
                if n < len(columns) and abs(columns[n] - i) <= HB:
                    left_ref[rows, cols] = held[table[i * WIDTH + columns[n] - i + HB]]
                else:
                    left_ref[rows, cols] = jnp.zeros((BLK, BLK), left_ref.dtype)


def find_block(parity, k, j):
    if abs(k - j) > HB:
        return None
    if 0 <= k < BR:
        return ("left", parity == j % 2), (k, columns_of(j % 2).index(j)), False
    if 0 <= j < BR:
        return ("left", parity == k % 2), (j, columns_of(k % 2).index(k)), True
    for a, b, flip in ((k, j, False), (j, k, True)):
        for name in DISTANCES:
            if (a, b) in SENT[name, parity]:
                return name, SENT[name, parity].index((a, b)), flip
        for part in PARTS:
            staged = [position for _, _, position in STAGED[part, 1 - parity]]
            if (a, b) in staged:
                return part, staged.index((a, b)), not flip
    raise AssertionError((k, j))


def columns_product(refs, right, parity, js, wanted):
    total = None
    for own in (True, False):
        kind = parity if own else 1 - parity
        found = {}
        for k in columns_of(kind):
            for j in js:
                place = find_block(parity, k, j)
                if place is not None and place[0] in wanted:
                    found[k, j] = place
        if not found:
            continue
        first, last = min(k for k, _ in found), max(k for k, _ in found)
        ks = [k for k in columns_of(kind) if first <= k <= last]
        side = right.at[0 if own else 1]
        for x, k in enumerate(ks):
            for y, j in enumerate(js):
                if (k, j) in found:
                    source, place, flip = found[k, j]
                    if isinstance(place, tuple):
                        block = refs[source][pl.ds(place[0] * BLK, BLK), pl.ds(place[1] * BLK, BLK)]
                    else:
                        block = refs[source][place]
                    block = block.T if flip else block
                else:
                    block = jnp.zeros((BLK, BLK), right.dtype)
                side[pl.ds(x * BLK, BLK), pl.ds(y * BLK, BLK)] = block
        start = columns_of(kind).index(first)
        part = jnp.dot(
            refs["left", own][:, pl.ds(start * BLK, len(ks) * BLK)],
            side[pl.ds(0, len(ks) * BLK), pl.ds(0, len(js) * BLK)],
            preferred_element_type=jnp.float32,
        )
        total = part if total is None else total + part
    return total


LEFT = (("left", True), ("left", False))


def block_of(total, i, y):
    return total[i * BLK : (i + 1) * BLK, y * BLK : (y + 1) * BLK]


def stored_places(parity):
    columns = columns_of(parity)
    return [i * NCOL + n for i in range(BR) for n, j in enumerate(columns) if abs(i - j) <= HB]


def inner_places(parity):
    return [i * NCOL + n for i in range(BR) for n, j in enumerate(columns_of(parity)) if 0 <= j < BR]


def store(made, table, out_ref, place, sem):
    source = made.at[table[0, SOURCES + place]]
    pltpu.make_async_copy(source, out_ref.at[0, table[0, place]], sem).start()


def wait_for(count, made, out_ref, sem):
    pltpu.make_async_copy(made.at[pl.ds(0, count)], out_ref.at[0, pl.ds(0, count)], sem).wait()


def outer_pairs(parity):
    outer = [j for j in columns_of(parity) if not 0 <= j < BR]
    return [outer[n : n + 2] for n in range(0, len(outer), 2)]


def inner_kernel(nblocks, slots, rows_ref, cols_ref, counts_ref, left_ref, left_other_ref, *rest):
    table_ref, out_ref, right, made, table, *index, sems, table_sem, out_sem = rest
    copies = index_copies((rows_ref, cols_ref), index, sems)
    for copy in copies:
        copy.start()
    refs = {("left", True): left_ref, ("left", False): left_other_ref}

    @for_own_parity
    def _(mine):
        js = [j for j in columns_of(mine) if 0 <= j < BR]
        total = columns_product(refs, right, mine, js, LEFT)
        for i in range(BR):
            for y in range(2):
                if y < len(js):
                    made[i * NCOL + columns_of(mine).index(js[y])] = block_of(total, i, y)
        made[BR * NCOL] = jnp.zeros((BLK, BLK), made.dtype)

    for copy in copies:
        copy.wait()
    for place in range(BR * NCOL + 1):
        table[0, place] = -1
    count = counts_ref[0, 0]
    for m in range(slots):
        _, row, band = slot_position(*index, m, nblocks)
        table[0, jnp.where(m < count, row * NCOL + (row + band) // 2, BR * NCOL)] = m

    @for_own_parity
    def _(mine):
        unused = count
        for place in stored_places(mine):
            slot = table[0, place]
            absent = slot < 0
            table[0, place] = jnp.where(absent, unused, slot)
            table[0, SOURCES + place] = jnp.where(absent, BR * NCOL, place)
            unused = jnp.where(absent, unused + 1, unused)
        table[0, BR * NCOL] = unused
        here = [place for place in stored_places(mine) if place in inner_places(mine)]
        for place in here:
            store(made, table, out_ref, place, out_sem)
        stored = len(here)
        if len(stored_places(mine)) < slots:
            pltpu.make_async_copy(made.at[BR * NCOL], out_ref.at[0, unused], out_sem).start()
            stored += 1
        wait_for(stored, made, out_ref, out_sem)

    copy = pltpu.make_async_copy(table, table_ref, table_sem)
    copy.start()
    copy.wait()


def pack_e_kernel(left_ref, left_other_ref, e_ref):
    @for_own_parity
    def _(mine):
        i = 2 if mine == 0 else 0
        n = columns_of(0).index(i)
        e_ref[0] = (left_ref if mine == 0 else left_other_ref)[pl.ds(i * BLK, BLK), pl.ds(n * BLK, BLK)]


def stage_kernel(part, *refs):
    got = dict(zip(PARTS[part], refs))
    out_ref = refs[-1]

    @for_own_parity
    def _(mine):
        staged = STAGED[part, mine]
        for n, (name, place, _) in enumerate(staged):
            out_ref[n] = got[name][place].T
        for n in range(len(staged), STAGED_SIZE[part]):
            out_ref[n] = jnp.zeros((BLK, BLK), out_ref.dtype)


def add_columns(refs, wanted, old_ref, new_ref, right, mine):
    for pair, js in enumerate(outer_pairs(mine)):
        total = columns_product(refs, right.at[pair], mine, js, wanted)
        for i in range(BR):
            for y, j in enumerate(js):
                if abs(i - j) <= HB:
                    place = i * NCOL + columns_of(mine).index(j)
                    terms = [] if old_ref is None else [old_ref[place]]
                    terms += [] if total is None else [block_of(total, i, y)]
                    new_ref[place] = functools.reduce(jnp.add, terms)


def early_kernel(left_ref, left_other_ref, a_ref, c_ref, out_ref, right):
    refs = {("left", True): left_ref, ("left", False): left_other_ref, "a": a_ref, "c": c_ref}
    for_own_parity(functools.partial(add_columns, refs, (*LEFT, "a", "c"), None, out_ref, right))


def late_kernel(left_ref, left_other_ref, b_ref, d_ref, e_ref, old_ref, out_ref, right):
    refs = {("left", True): left_ref, ("left", False): left_other_ref, "b": b_ref, "d": d_ref, "e": e_ref}
    for_own_parity(functools.partial(add_columns, refs, ("b", "d", "e"), old_ref, out_ref, right))


def multiply_kernel(left_ref, left_other_ref, early_ref, late_ref, old_ref, table_ref, _, out_ref, *rest):
    right, made, table, table_sem, out_sem = rest
    refs = {("left", True): left_ref, ("left", False): left_other_ref, "early": early_ref, "late": late_ref}
    load = pltpu.make_async_copy(table_ref, table, table_sem)
    load.start()
    made[BR * NCOL] = jnp.zeros((BLK, BLK), made.dtype)

    @for_own_parity
    def _(mine):
        add_columns(refs, tuple(PARTS), old_ref, made, right, mine)
        load.wait()
        here = [place for place in stored_places(mine) if place not in inner_places(mine)]
        for place in here:
            store(made, table, out_ref, place, out_sem)
        wait_for(len(here), made, out_ref, out_sem)


def local(values, block_rows, block_cols, counts):
    slots = values.shape[1]
    row_count, col_count = lax.axis_size("row"), lax.axis_size("col")
    nblocks = BR * row_count
    smem = pl.BlockSpec(memory_space=pltpu.SMEM)
    vmem = pl.BlockSpec(memory_space=pltpu.VMEM)
    hbm = pl.BlockSpec(memory_space=pltpu.HBM)
    params = pltpu.CompilerParams(vmem_limit_bytes=VMEM_LIMIT)
    values, *places = (pltpu.with_memory_space_constraint(x, pltpu.HBM) for x in (values, block_rows, block_cols))
    index_scratch = [
        pltpu.SMEM((1, slots), jnp.int32),
        pltpu.SMEM((1, slots), jnp.int32),
        pltpu.SemaphoreType.DMA((2,)),
    ]
    table_shape = (1, BLK)

    def blocks(count, dtype=values.dtype):
        return jax.ShapeDtypeStruct((count, BLK, BLK), dtype)

    def cost(products, nbytes):
        return pl.CostEstimate(flops=2 * products * BLK**3, bytes_accessed=nbytes, transcendentals=0)

    def right_scratch(pairs):
        return pltpu.VMEM((pairs, 2, NCOL * BLK, 2 * BLK), values.dtype)

    *packed, left = pl.pallas_call(
        functools.partial(pack_kernel, nblocks, slots),
        out_shape=[blocks(SIZES[name]) for name in "abcd"]
        + [jax.ShapeDtypeStruct((BR * BLK, NCOL * BLK), values.dtype)],
        in_specs=[hbm] * 3,
        out_specs=[vmem] * 5,
        scratch_shapes=[
            pltpu.VMEM((slots + 1, BLK, BLK), values.dtype),
            pltpu.SMEM((BR * WIDTH + 1,), jnp.int32),
            *index_scratch,
            pltpu.SemaphoreType.DMA,
        ],
        compiler_params=params,
        name="pack",
    )(*places, values)

    def towards(name, message):
        pairs = []
        for r in range(row_count):
            for c in range(col_count):
                distance = DISTANCES[name] or (3 if (r + c) % 2 == 1 else -3)
                source = (r - distance if r % 2 == 1 else r + distance) % row_count
                pairs.append((source * col_count + c, r * col_count + c))
        return lax.ppermute(message, ("row", "col"), pairs)

    def swapped(block):
        return lax.ppermute(block, "col", [(0, 1), (1, 0)])

    left_other = swapped(left)
    got = [towards(name, message) for name, message in zip("abcd", packed)]
    message = pl.pallas_call(
        pack_e_kernel,
        out_shape=blocks(SIZES["e"]),
        in_specs=[vmem] * 2,
        out_specs=vmem,
        compiler_params=params,
        name="pack_e",
    )(left, left_other)
    got.append(towards("e", message))
    table, out = pl.pallas_call(
        functools.partial(inner_kernel, nblocks, slots),
        out_shape=[jax.ShapeDtypeStruct(table_shape, jnp.int32), jax.ShapeDtypeStruct(values.shape, jnp.float32)],
        in_specs=[hbm] * 2 + [smem] + [vmem] * 2,
        out_specs=[vmem, hbm],
        scratch_shapes=[
            pltpu.VMEM((2, NCOL * BLK, 2 * BLK), values.dtype),
            pltpu.VMEM((BR * NCOL + 1, BLK, BLK), jnp.float32),
            pltpu.SMEM(table_shape, jnp.int32),
            *index_scratch,
            pltpu.SemaphoreType.DMA,
            pltpu.SemaphoreType.DMA,
        ],
        compiler_params=params,
        cost_estimate=cost(3 * 2 * 17, 4 * values.size),
        name="inner",
    )(*places, counts, left, left_other)
    a, b, c, d, e = got

    def staged(part, arrays):
        return swapped(
            pl.pallas_call(
                functools.partial(stage_kernel, part),
                out_shape=blocks(STAGED_SIZE[part]),
                in_specs=[vmem] * len(arrays),
                out_specs=vmem,
                compiler_params=params,
                name="stage_" + part,
            )(*arrays)
        )

    def added(kernel, name, products, arrays):
        return pl.pallas_call(
            kernel,
            out_shape=blocks(BR * NCOL, jnp.float32),
            in_specs=[vmem] * len(arrays),
            out_specs=vmem,
            scratch_shapes=[right_scratch(4)],
            compiler_params=params,
            cost_estimate=cost(products, 0),
            name=name,
        )(*arrays)

    a, c, table = lax.optimization_barrier((a, c, table))
    staged_early = staged("early", (a, c))
    total = added(early_kernel, "early", EARLY_COST, (left, left_other, a, c))
    b, d, e, total = lax.optimization_barrier((b, d, e, total))
    staged_late = staged("late", (b, d, e))
    total = added(late_kernel, "late", LATE_COST, (left, left_other, b, d, e, total))
    return pl.pallas_call(
        multiply_kernel,
        out_shape=jax.ShapeDtypeStruct(values.shape, jnp.float32),
        in_specs=[vmem] * 6 + [hbm],
        out_specs=hbm,
        scratch_shapes=[
            right_scratch(4),
            pltpu.VMEM((BR * NCOL + 1, BLK, BLK), jnp.float32),
            pltpu.SMEM(table_shape, jnp.int32),
            pltpu.SemaphoreType.DMA,
            pltpu.SemaphoreType.DMA,
        ],
        input_output_aliases={6: 0},
        compiler_params=params,
        name="multiply",
    )(left, left_other, staged_early, staged_late, total, table, out)


def solution(mesh):
    return jax.shard_map(
        local,
        mesh=mesh,
        in_specs=(
            P(("parts", "row"), "col", None, None),
            P(("parts", "row"), "col"),
            P(("parts", "row"), "col"),
            P(("parts", "row"), "col"),
        ),
        out_specs=P(("parts", "row"), "col", None, None),
        check_vma=False,
    )
```

```python
import functools

import jax
import jax.numpy as jnp
from jax import lax
from jax.experimental import pallas as pl
from jax.experimental.pallas import tpu as pltpu
from jax.sharding import PartitionSpec as P

BLK = 128
BR = 3
HB = 7
WIDTH = 2 * HB + 1
LOW, HIGH = -HB, BR - 1 + HB
NCOL = 9
SOURCES = 32
EARLY_COST = 1
LATE_COST = 4000
VMEM_LIMIT = 12 * 2**20

DISTANCES = {"a": 1, "b": -1, "c": -2, "d": 2, "e": None}
SENT = {
    ("a", 1): [(3, 3), (5, 5), (3, 5), (3, 7), (4, 7), (5, 7), (3, 9), (4, 9), (5, 9), (3, -3), (3, -1), (4, -3), (5, -1)],
    ("a", 0): [(4, 4), (3, 4), (5, 4), (3, 6), (4, 6), (5, 6), (3, 8), (4, 8), (5, 8), (3, -2), (4, -2), (5, -2), (3, -4)],
    ("b", 1): [(-1, -1), (-3, -3), (-1, -3), (-1, -7), (-2, -7), (-3, -7)],
    ("b", 0): [(-2, -2), (-1, -2), (-3, -2), (-1, 4), (-1, -4), (-1, -6)],
    ("c", 1): [(-5, -5), (-4, -7), (-5, -7), (-6, -7), (-4, -3), (-5, -1), (-5, -3), (-6, -3)],
    ("c", 0): [(-4, -4), (-6, -6), (-4, -6), (-4, -2), (-5, -2), (-6, -2), (-5, -4), (-5, -6)],
    ("d", 1): [(6, 9), (7, 7), (7, 9), (8, 9), (6, -1)],
    ("d", 0): [(6, 6), (6, 8), (8, 8), (7, 6), (7, 8)],
    ("e", 1): [(9, 9)],
    ("e", 0): [(-7, -7)],
}
SIZES = {name: len(SENT[name, 1]) for name in DISTANCES}
PARTS = {"early": "ac", "late": "bde"}
STAGED = {
    (part, parity): [
        (name, n, (k, j))
        for name in names
        for n, (k, j) in enumerate(SENT[name, parity])
        if k % 2 != j % 2 or (k, j) == (-7, -7)
    ]
    for part, names in PARTS.items()
    for parity in (0, 1)
}
STAGED_SIZE = {part: max(len(STAGED[part, parity]) for parity in (0, 1)) for part in PARTS}


def columns_of(parity):
    return [j for j in range(LOW, HIGH + 1) if j % 2 == parity]


def own_parity():
    return (lax.axis_index("row") + lax.axis_index("col")) % 2


def for_own_parity(body):
    parity = own_parity()
    for mine in (0, 1):
        pl.when(parity == mine)(functools.partial(body, mine))


def slot_position(rows_ref, cols_ref, slot, nblocks):
    panel = lax.axis_index("row")
    row = rows_ref[0, slot] - panel * BR
    band = cols_ref[0, slot] - rows_ref[0, slot] + HB
    band = jnp.where(band < 0, band + nblocks, band)
    band = jnp.where(band >= nblocks, band - nblocks, band)
    odd = panel % 2 == 1
    return row, jnp.where(odd, BR - 1 - row, row), jnp.where(odd, WIDTH - 1 - band, band)


def index_copies(hbm_refs, smem_refs, sems):
    return [pltpu.make_async_copy(a, b, sems.at[i]) for i, (a, b) in enumerate(zip(hbm_refs, smem_refs))]


def pack_kernel(nblocks, slots, rows_ref, cols_ref, values_ref, *rest):
    out_refs = dict(zip("abcd", rest[:4]))
    left_ref, held, table, *index, sems, value_sem = rest[4:]
    copies = index_copies((rows_ref, cols_ref), index, sems)
    load = pltpu.make_async_copy(values_ref.at[0], held.at[pl.ds(0, slots)], value_sem)
    for copy in (*copies, load):
        copy.start()
    held[slots] = jnp.zeros((BLK, BLK), held.dtype)
    for i in range(BR * WIDTH + 1):
        table[i] = slots
    for copy in copies:
        copy.wait()
    for m in reversed(range(slots)):
        real_row, row, band = slot_position(*index, m, nblocks)
        table[jnp.where(real_row >= 0, row * WIDTH + band, BR * WIDTH)] = m
    load.wait()

    @for_own_parity
    def _(mine):
        for name, ref in out_refs.items():
            distance = DISTANCES[name]
            for n, (k, j) in enumerate(SENT[name, (mine + distance) % 2]):
                at = (k - BR * distance) * WIDTH + j - k + HB
                if distance % 2 == 1:
                    at = BR * WIDTH - 1 - at
                ref[n] = held[table[at]]
        columns = columns_of(mine)
        for i in range(BR):
            for n in range(NCOL):
                rows, cols = pl.ds(i * BLK, BLK), pl.ds(n * BLK, BLK)
                if n < len(columns) and abs(columns[n] - i) <= HB:
                    left_ref[rows, cols] = held[table[i * WIDTH + columns[n] - i + HB]]
                else:
                    left_ref[rows, cols] = jnp.zeros((BLK, BLK), left_ref.dtype)


def find_block(parity, k, j):
    if abs(k - j) > HB:
        return None
    if 0 <= k < BR:
        return ("left", parity == j % 2), (k, columns_of(j % 2).index(j)), False
    if 0 <= j < BR:
        return ("left", parity == k % 2), (j, columns_of(k % 2).index(k)), True
    for a, b, flip in ((k, j, False), (j, k, True)):
        for name in DISTANCES:
            if (a, b) in SENT[name, parity]:
                return name, SENT[name, parity].index((a, b)), flip
        for part in PARTS:
            staged = [position for _, _, position in STAGED[part, 1 - parity]]
            if (a, b) in staged:
                return part, staged.index((a, b)), not flip
    raise AssertionError((k, j))


def columns_product(refs, right, parity, js, wanted):
    total = None
    for own in (True, False):
        kind = parity if own else 1 - parity
        found = {}
        for k in columns_of(kind):
            for j in js:
                place = find_block(parity, k, j)
                if place is not None and place[0] in wanted:
                    found[k, j] = place
        if not found:
            continue
        first, last = min(k for k, _ in found), max(k for k, _ in found)
        ks = [k for k in columns_of(kind) if first <= k <= last]
        side = right.at[0 if own else 1]
        for x, k in enumerate(ks):
            for y, j in enumerate(js):
                if (k, j) in found:
                    source, place, flip = found[k, j]
                    if isinstance(place, tuple):
                        block = refs[source][pl.ds(place[0] * BLK, BLK), pl.ds(place[1] * BLK, BLK)]
                    else:
                        block = refs[source][place]
                    block = block.T if flip else block
                else:
                    block = jnp.zeros((BLK, BLK), right.dtype)
                side[pl.ds(x * BLK, BLK), pl.ds(y * BLK, BLK)] = block
        start = columns_of(kind).index(first)
        part = jnp.dot(
            refs["left", own][:, pl.ds(start * BLK, len(ks) * BLK)],
            side[pl.ds(0, len(ks) * BLK), pl.ds(0, len(js) * BLK)],
            preferred_element_type=jnp.float32,
        )
        total = part if total is None else total + part
    return total


LEFT = (("left", True), ("left", False))


def block_of(total, i, y):
    return total[i * BLK : (i + 1) * BLK, y * BLK : (y + 1) * BLK]


def stored_places(parity):
    columns = columns_of(parity)
    return [i * NCOL + n for i in range(BR) for n, j in enumerate(columns) if abs(i - j) <= HB]


def inner_places(parity):
    return [i * NCOL + n for i in range(BR) for n, j in enumerate(columns_of(parity)) if 0 <= j < BR]


def store(made, table, out_ref, place, sem):
    source = made.at[table[0, SOURCES + place]]
    pltpu.make_async_copy(source, out_ref.at[0, table[0, place]], sem).start()


def wait_for(count, made, out_ref, sem):
    pltpu.make_async_copy(made.at[pl.ds(0, count)], out_ref.at[0, pl.ds(0, count)], sem).wait()


def outer_pairs(parity):
    outer = [j for j in columns_of(parity) if not 0 <= j < BR]
    return [outer[n : n + 2] for n in range(0, len(outer), 2)]


def inner_kernel(nblocks, slots, rows_ref, cols_ref, counts_ref, left_ref, left_other_ref, *rest):
    table_ref, out_ref, right, made, table, *index, sems, table_sem, out_sem = rest
    copies = index_copies((rows_ref, cols_ref), index, sems)
    for copy in copies:
        copy.start()
    refs = {("left", True): left_ref, ("left", False): left_other_ref}

    @for_own_parity
    def _(mine):
        js = [j for j in columns_of(mine) if 0 <= j < BR]
        total = columns_product(refs, right, mine, js, LEFT)
        for i in range(BR):
            for y in range(2):
                if y < len(js):
                    made[i * NCOL + columns_of(mine).index(js[y])] = block_of(total, i, y)
        made[BR * NCOL] = jnp.zeros((BLK, BLK), made.dtype)

    for copy in copies:
        copy.wait()
    for place in range(BR * NCOL + 1):
        table[0, place] = -1
    count = counts_ref[0, 0]
    for m in range(slots):
        _, row, band = slot_position(*index, m, nblocks)
        table[0, jnp.where(m < count, row * NCOL + (row + band) // 2, BR * NCOL)] = m

    @for_own_parity
    def _(mine):
        unused = count
        for place in stored_places(mine):
            slot = table[0, place]
            absent = slot < 0
            table[0, place] = jnp.where(absent, unused, slot)
            table[0, SOURCES + place] = jnp.where(absent, BR * NCOL, place)
            unused = jnp.where(absent, unused + 1, unused)
        table[0, BR * NCOL] = unused
        here = [place for place in stored_places(mine) if place in inner_places(mine)]
        for place in here:
            store(made, table, out_ref, place, out_sem)
        stored = len(here)
        if len(stored_places(mine)) < slots:
            pltpu.make_async_copy(made.at[BR * NCOL], out_ref.at[0, unused], out_sem).start()
            stored += 1
        wait_for(stored, made, out_ref, out_sem)

    copy = pltpu.make_async_copy(table, table_ref, table_sem)
    copy.start()
    copy.wait()


def pack_e_kernel(left_ref, left_other_ref, e_ref):
    @for_own_parity
    def _(mine):
        i = 2 if mine == 0 else 0
        n = columns_of(0).index(i)
        e_ref[0] = (left_ref if mine == 0 else left_other_ref)[pl.ds(i * BLK, BLK), pl.ds(n * BLK, BLK)]


def stage_kernel(part, *refs):
    got = dict(zip(PARTS[part], refs))
    out_ref = refs[-1]

    @for_own_parity
    def _(mine):
        staged = STAGED[part, mine]
        for n, (name, place, _) in enumerate(staged):
            out_ref[n] = got[name][place].T
        for n in range(len(staged), STAGED_SIZE[part]):
            out_ref[n] = jnp.zeros((BLK, BLK), out_ref.dtype)


def add_columns(refs, wanted, old_ref, new_ref, right, mine):
    for pair, js in enumerate(outer_pairs(mine)):
        total = columns_product(refs, right.at[pair], mine, js, wanted)
        for i in range(BR):
            for y, j in enumerate(js):
                if abs(i - j) <= HB:
                    place = i * NCOL + columns_of(mine).index(j)
                    terms = [] if old_ref is None else [old_ref[place]]
                    terms += [] if total is None else [block_of(total, i, y)]
                    new_ref[place] = functools.reduce(jnp.add, terms)


def early_kernel(left_ref, left_other_ref, a_ref, c_ref, out_ref, right):
    refs = {("left", True): left_ref, ("left", False): left_other_ref, "a": a_ref, "c": c_ref}
    for_own_parity(functools.partial(add_columns, refs, (*LEFT, "a", "c"), None, out_ref, right))


def late_kernel(left_ref, left_other_ref, b_ref, d_ref, e_ref, old_ref, out_ref, right):
    refs = {("left", True): left_ref, ("left", False): left_other_ref, "b": b_ref, "d": d_ref, "e": e_ref}
    for_own_parity(functools.partial(add_columns, refs, ("b", "d", "e"), old_ref, out_ref, right))


def staged_early_kernel(left_ref, left_other_ref, staged_ref, old_ref, out_ref, right):
    refs = {("left", True): left_ref, ("left", False): left_other_ref, "early": staged_ref}
    for_own_parity(functools.partial(add_columns, refs, ("early",), old_ref, out_ref, right))


def multiply_kernel(left_ref, left_other_ref, staged_ref, old_ref, table_ref, _, out_ref, *rest):
    right, made, table, table_sem, out_sem = rest
    refs = {("left", True): left_ref, ("left", False): left_other_ref, "late": staged_ref}
    load = pltpu.make_async_copy(table_ref, table, table_sem)
    load.start()
    made[BR * NCOL] = jnp.zeros((BLK, BLK), made.dtype)

    @for_own_parity
    def _(mine):
        add_columns(refs, ("late",), old_ref, made, right, mine)
        load.wait()
        here = [place for place in stored_places(mine) if place not in inner_places(mine)]
        for place in here:
            store(made, table, out_ref, place, out_sem)
        wait_for(len(here), made, out_ref, out_sem)


def local(values, block_rows, block_cols, counts):
    slots = values.shape[1]
    row_count, col_count = lax.axis_size("row"), lax.axis_size("col")
    nblocks = BR * row_count
    smem = pl.BlockSpec(memory_space=pltpu.SMEM)
    vmem = pl.BlockSpec(memory_space=pltpu.VMEM)
    hbm = pl.BlockSpec(memory_space=pltpu.HBM)
    params = pltpu.CompilerParams(vmem_limit_bytes=VMEM_LIMIT)
    values, *places = (pltpu.with_memory_space_constraint(x, pltpu.HBM) for x in (values, block_rows, block_cols))
    index_scratch = [
        pltpu.SMEM((1, slots), jnp.int32),
        pltpu.SMEM((1, slots), jnp.int32),
        pltpu.SemaphoreType.DMA((2,)),
    ]
    table_shape = (1, BLK)

    def blocks(count, dtype=values.dtype):
        return jax.ShapeDtypeStruct((count, BLK, BLK), dtype)

    def cost(products, nbytes):
        return pl.CostEstimate(flops=2 * products * BLK**3, bytes_accessed=nbytes, transcendentals=0)

    def right_scratch(pairs):
        return pltpu.VMEM((pairs, 2, NCOL * BLK, 2 * BLK), values.dtype)

    *packed, left = pl.pallas_call(
        functools.partial(pack_kernel, nblocks, slots),
        out_shape=[blocks(SIZES[name]) for name in "abcd"]
        + [jax.ShapeDtypeStruct((BR * BLK, NCOL * BLK), values.dtype)],
        in_specs=[hbm] * 3,
        out_specs=[vmem] * 5,
        scratch_shapes=[
            pltpu.VMEM((slots + 1, BLK, BLK), values.dtype),
            pltpu.SMEM((BR * WIDTH + 1,), jnp.int32),
            *index_scratch,
            pltpu.SemaphoreType.DMA,
        ],
        compiler_params=params,
        name="pack",
    )(*places, values)

    def towards(name, message):
        pairs = []
        for r in range(row_count):
            for c in range(col_count):
                distance = DISTANCES[name] or (3 if (r + c) % 2 == 1 else -3)
                source = (r - distance if r % 2 == 1 else r + distance) % row_count
                pairs.append((source * col_count + c, r * col_count + c))
        return lax.ppermute(message, ("row", "col"), pairs)

    def swapped(block):
        return lax.ppermute(block, "col", [(0, 1), (1, 0)])

    left_other = swapped(left)
    got = [towards(name, message) for name, message in zip("abcd", packed)]
    message = pl.pallas_call(
        pack_e_kernel,
        out_shape=blocks(SIZES["e"]),
        in_specs=[vmem] * 2,
        out_specs=vmem,
        compiler_params=params,
        name="pack_e",
    )(left, left_other)
    got.append(towards("e", message))
    table, out = pl.pallas_call(
        functools.partial(inner_kernel, nblocks, slots),
        out_shape=[jax.ShapeDtypeStruct(table_shape, jnp.int32), jax.ShapeDtypeStruct(values.shape, jnp.float32)],
        in_specs=[hbm] * 2 + [smem] + [vmem] * 2,
        out_specs=[vmem, hbm],
        scratch_shapes=[
            pltpu.VMEM((2, NCOL * BLK, 2 * BLK), values.dtype),
            pltpu.VMEM((BR * NCOL + 1, BLK, BLK), jnp.float32),
            pltpu.SMEM(table_shape, jnp.int32),
            *index_scratch,
            pltpu.SemaphoreType.DMA,
            pltpu.SemaphoreType.DMA,
        ],
        compiler_params=params,
        cost_estimate=cost(3 * 2 * 17, 4 * values.size),
        name="inner",
    )(*places, counts, left, left_other)
    a, b, c, d, e = got

    def staged(part, arrays):
        return swapped(
            pl.pallas_call(
                functools.partial(stage_kernel, part),
                out_shape=blocks(STAGED_SIZE[part]),
                in_specs=[vmem] * len(arrays),
                out_specs=vmem,
                compiler_params=params,
                name="stage_" + part,
            )(*arrays)
        )

    def added(kernel, name, products, arrays):
        return pl.pallas_call(
            kernel,
            out_shape=blocks(BR * NCOL, jnp.float32),
            in_specs=[vmem] * len(arrays),
            out_specs=vmem,
            scratch_shapes=[right_scratch(4)],
            compiler_params=params,
            cost_estimate=cost(products, 0),
            name=name,
        )(*arrays)

    a, c, table = lax.optimization_barrier((a, c, table))
    staged_early = staged("early", (a, c))
    total = added(early_kernel, "early", EARLY_COST, (left, left_other, a, c))
    b, d, e, total = lax.optimization_barrier((b, d, e, total))
    staged_late = staged("late", (b, d, e))
    total = added(late_kernel, "late", LATE_COST, (left, left_other, b, d, e, total))
    total = added(staged_early_kernel, "staged_early", EARLY_COST, (left, left_other, staged_early, total))
    return pl.pallas_call(
        multiply_kernel,
        out_shape=jax.ShapeDtypeStruct(values.shape, jnp.float32),
        in_specs=[vmem] * 5 + [hbm],
        out_specs=hbm,
        scratch_shapes=[
            right_scratch(4),
            pltpu.VMEM((BR * NCOL + 1, BLK, BLK), jnp.float32),
            pltpu.SMEM(table_shape, jnp.int32),
            pltpu.SemaphoreType.DMA,
            pltpu.SemaphoreType.DMA,
        ],
        input_output_aliases={5: 0},
        compiler_params=params,
        name="multiply",
    )(left, left_other, staged_late, total, table, out)


def solution(mesh):
    return jax.shard_map(
        local,
        mesh=mesh,
        in_specs=(
            P(("parts", "row"), "col", None, None),
            P(("parts", "row"), "col"),
            P(("parts", "row"), "col"),
            P(("parts", "row"), "col"),
        ),
        out_specs=P(("parts", "row"), "col", None, None),
        check_vma=False,
    )
```

```python
import functools

import jax
import jax.numpy as jnp
from jax import lax
from jax.experimental import pallas as pl
from jax.experimental.pallas import tpu as pltpu
from jax.sharding import PartitionSpec as P

BLK = 128
BR = 3
HB = 7
WIDTH = 2 * HB + 1
LOW, HIGH = -HB, BR - 1 + HB
NCOL = 9
SOURCES = 32
EARLY_COST = 1
LATE_COST = 4000
VMEM_LIMIT = 12 * 2**20

DISTANCES = {"a": 1, "b": -1, "c": -2, "d": 2, "e": None}
SENT = {
    ("a", 1): [(3, 3), (5, 5), (3, 5), (3, 7), (4, 7), (5, 7), (3, 9), (4, 9), (5, 9), (3, -3), (3, -1), (4, -3), (5, -1)],
    ("a", 0): [(4, 4), (3, 4), (5, 4), (3, 6), (4, 6), (5, 6), (3, 8), (4, 8), (5, 8), (3, -2), (4, -2), (5, -2), (3, -4)],
    ("b", 1): [(-1, -1), (-3, -3), (-1, -3), (-1, -7), (-2, -7), (-3, -7)],
    ("b", 0): [(-2, -2), (-1, -2), (-3, -2), (-1, 4), (-1, -4), (-1, -6)],
    ("c", 1): [(-5, -5), (-4, -7), (-5, -7), (-6, -7), (-4, -3), (-5, -1), (-5, -3), (-6, -3)],
    ("c", 0): [(-4, -4), (-6, -6), (-4, -6), (-4, -2), (-5, -2), (-6, -2), (-5, -4), (-5, -6)],
    ("d", 1): [(6, 9), (7, 7), (7, 9), (8, 9), (6, -1)],
    ("d", 0): [(6, 6), (6, 8), (8, 8), (7, 6), (7, 8)],
    ("e", 1): [(9, 9)],
    ("e", 0): [(-7, -7)],
}
SIZES = {name: len(SENT[name, 1]) for name in DISTANCES}
PARTS = {"early": "ac", "late": "bde"}
STAGED = {
    (part, parity): [
        (name, n, (k, j))
        for name in names
        for n, (k, j) in enumerate(SENT[name, parity])
        if k % 2 != j % 2 or (k, j) == (-7, -7)
    ]
    for part, names in PARTS.items()
    for parity in (0, 1)
}
STAGED_SIZE = {part: max(len(STAGED[part, parity]) for parity in (0, 1)) for part in PARTS}


def columns_of(parity):
    return [j for j in range(LOW, HIGH + 1) if j % 2 == parity]


def own_parity():
    return (lax.axis_index("row") + lax.axis_index("col")) % 2


def for_own_parity(body):
    parity = own_parity()
    for mine in (0, 1):
        pl.when(parity == mine)(functools.partial(body, mine))


def slot_position(rows_ref, cols_ref, slot, nblocks):
    panel = lax.axis_index("row")
    row = rows_ref[0, slot] - panel * BR
    band = cols_ref[0, slot] - rows_ref[0, slot] + HB
    band = jnp.where(band < 0, band + nblocks, band)
    band = jnp.where(band >= nblocks, band - nblocks, band)
    odd = panel % 2 == 1
    return row, jnp.where(odd, BR - 1 - row, row), jnp.where(odd, WIDTH - 1 - band, band)


def index_copies(hbm_refs, smem_refs, sems):
    return [pltpu.make_async_copy(a, b, sems.at[i]) for i, (a, b) in enumerate(zip(hbm_refs, smem_refs))]


def pack_kernel(nblocks, slots, rows_ref, cols_ref, values_ref, *rest):
    out_refs = dict(zip("abcd", rest[:4]))
    left_ref, held, table, *index, sems, value_sem = rest[4:]
    copies = index_copies((rows_ref, cols_ref), index, sems)
    load = pltpu.make_async_copy(values_ref.at[0], held.at[pl.ds(0, slots)], value_sem)
    for copy in (*copies, load):
        copy.start()
    held[slots] = jnp.zeros((BLK, BLK), held.dtype)
    for i in range(BR * WIDTH + 1):
        table[i] = slots
    for copy in copies:
        copy.wait()
    for m in reversed(range(slots)):
        real_row, row, band = slot_position(*index, m, nblocks)
        table[jnp.where(real_row >= 0, row * WIDTH + band, BR * WIDTH)] = m
    load.wait()

    @for_own_parity
    def _(mine):
        for name, ref in out_refs.items():
            distance = DISTANCES[name]
            for n, (k, j) in enumerate(SENT[name, (mine + distance) % 2]):
                at = (k - BR * distance) * WIDTH + j - k + HB
                if distance % 2 == 1:
                    at = BR * WIDTH - 1 - at
                ref[n] = held[table[at]]
        columns = columns_of(mine)
        for i in range(BR):
            for n in range(NCOL):
                rows, cols = pl.ds(i * BLK, BLK), pl.ds(n * BLK, BLK)
                if n < len(columns) and abs(columns[n] - i) <= HB:
                    left_ref[rows, cols] = held[table[i * WIDTH + columns[n] - i + HB]]
                else:
                    left_ref[rows, cols] = jnp.zeros((BLK, BLK), left_ref.dtype)


def find_block(parity, k, j):
    if abs(k - j) > HB:
        return None
    if 0 <= k < BR:
        return ("left", parity == j % 2), (k, columns_of(j % 2).index(j)), False
    if 0 <= j < BR:
        return ("left", parity == k % 2), (j, columns_of(k % 2).index(k)), True
    for a, b, flip in ((k, j, False), (j, k, True)):
        for name in DISTANCES:
            if (a, b) in SENT[name, parity]:
                return name, SENT[name, parity].index((a, b)), flip
        for part in PARTS:
            staged = [position for _, _, position in STAGED[part, 1 - parity]]
            if (a, b) in staged:
                return part, staged.index((a, b)), not flip
    raise AssertionError((k, j))


def columns_product(refs, right, parity, js, wanted):
    total = None
    for own in (True, False):
        kind = parity if own else 1 - parity
        found = {}
        for k in columns_of(kind):
            for j in js:
                place = find_block(parity, k, j)
                if place is not None and place[0] in wanted:
                    found[k, j] = place
        if not found:
            continue
        first, last = min(k for k, _ in found), max(k for k, _ in found)
        ks = [k for k in columns_of(kind) if first <= k <= last]
        side = right.at[0 if own else 1]
        for x, k in enumerate(ks):
            for y, j in enumerate(js):
                if (k, j) in found:
                    source, place, flip = found[k, j]
                    if isinstance(place, tuple):
                        block = refs[source][pl.ds(place[0] * BLK, BLK), pl.ds(place[1] * BLK, BLK)]
                    else:
                        block = refs[source][place]
                    block = block.T if flip else block
                else:
                    block = jnp.zeros((BLK, BLK), right.dtype)
                side[pl.ds(x * BLK, BLK), pl.ds(y * BLK, BLK)] = block
        start = columns_of(kind).index(first)
        part = jnp.dot(
            refs["left", own][:, pl.ds(start * BLK, len(ks) * BLK)],
            side[pl.ds(0, len(ks) * BLK), pl.ds(0, len(js) * BLK)],
            preferred_element_type=jnp.float32,
        )
        total = part if total is None else total + part
    return total


LEFT = (("left", True), ("left", False))


def block_of(total, i, y):
    return total[i * BLK : (i + 1) * BLK, y * BLK : (y + 1) * BLK]


def stored_places(parity):
    columns = columns_of(parity)
    return [i * NCOL + n for i in range(BR) for n, j in enumerate(columns) if abs(i - j) <= HB]


def inner_places(parity):
    return [i * NCOL + n for i in range(BR) for n, j in enumerate(columns_of(parity)) if 0 <= j < BR]


def store(made, table, out_ref, place, sem):
    source = made.at[table[0, SOURCES + place]]
    pltpu.make_async_copy(source, out_ref.at[0, table[0, place]], sem).start()


def wait_for(count, made, out_ref, sem):
    pltpu.make_async_copy(made.at[pl.ds(0, count)], out_ref.at[0, pl.ds(0, count)], sem).wait()


def outer_pairs(parity):
    outer = [j for j in columns_of(parity) if not 0 <= j < BR]
    return [outer[n : n + 2] for n in range(0, len(outer), 2)]


def inner_kernel(nblocks, slots, rows_ref, cols_ref, counts_ref, left_ref, left_other_ref, *rest):
    table_ref, out_ref, right, made, table, *index, sems, table_sem, out_sem = rest
    copies = index_copies((rows_ref, cols_ref), index, sems)
    for copy in copies:
        copy.start()
    refs = {("left", True): left_ref, ("left", False): left_other_ref}

    @for_own_parity
    def _(mine):
        js = [j for j in columns_of(mine) if 0 <= j < BR]
        total = columns_product(refs, right, mine, js, LEFT)
        for i in range(BR):
            for y in range(2):
                if y < len(js):
                    made[i * NCOL + columns_of(mine).index(js[y])] = block_of(total, i, y)
        made[BR * NCOL] = jnp.zeros((BLK, BLK), made.dtype)

    for copy in copies:
        copy.wait()
    for place in range(BR * NCOL + 1):
        table[0, place] = -1
    count = counts_ref[0, 0]
    for m in range(slots):
        _, row, band = slot_position(*index, m, nblocks)
        table[0, jnp.where(m < count, row * NCOL + (row + band) // 2, BR * NCOL)] = m

    @for_own_parity
    def _(mine):
        unused = count
        for place in stored_places(mine):
            slot = table[0, place]
            absent = slot < 0
            table[0, place] = jnp.where(absent, unused, slot)
            table[0, SOURCES + place] = jnp.where(absent, BR * NCOL, place)
            unused = jnp.where(absent, unused + 1, unused)
        table[0, BR * NCOL] = unused
        here = [place for place in stored_places(mine) if place in inner_places(mine)]
        for place in here:
            store(made, table, out_ref, place, out_sem)
        stored = len(here)
        if len(stored_places(mine)) < slots:
            pltpu.make_async_copy(made.at[BR * NCOL], out_ref.at[0, unused], out_sem).start()
            stored += 1
        wait_for(stored, made, out_ref, out_sem)

    copy = pltpu.make_async_copy(table, table_ref, table_sem)
    copy.start()
    copy.wait()


def pack_e_kernel(left_ref, left_other_ref, e_ref):
    @for_own_parity
    def _(mine):
        i = 2 if mine == 0 else 0
        n = columns_of(0).index(i)
        e_ref[0] = (left_ref if mine == 0 else left_other_ref)[pl.ds(i * BLK, BLK), pl.ds(n * BLK, BLK)]


def stage_kernel(part, *refs):
    got = dict(zip(PARTS[part], refs))
    out_ref = refs[-1]

    @for_own_parity
    def _(mine):
        staged = STAGED[part, mine]
        for n, (name, place, _) in enumerate(staged):
            out_ref[n] = got[name][place].T
        for n in range(len(staged), STAGED_SIZE[part]):
            out_ref[n] = jnp.zeros((BLK, BLK), out_ref.dtype)


def late_columns(parity):
    found = [[find_block(parity, k, j) for k in range(LOW, HIGH + 1)] for j in columns_of(parity)]
    return [j for j, blocks in zip(columns_of(parity), found) if any(b is not None and b[0] == "late" for b in blocks)]


def late_pairs(parity):
    near = [j for j in late_columns(parity) if -BR <= j < 0]
    rest = [j for j in late_columns(parity) if j not in near]
    return [js[n : n + 2] for js in (near, rest) for n in range(0, len(js), 2)]


def add_columns(refs, wanted, old_ref, new_ref, right, mine, pairs=outer_pairs):
    for pair, js in enumerate(pairs(mine)):
        total = columns_product(refs, right.at[pair], mine, js, wanted)
        for i in range(BR):
            for y, j in enumerate(js):
                if abs(i - j) <= HB:
                    place = i * NCOL + columns_of(mine).index(j)
                    terms = [] if old_ref is None else [old_ref[place]]
                    terms += [] if total is None else [block_of(total, i, y)]
                    new_ref[place] = functools.reduce(jnp.add, terms)


def early_kernel(left_ref, left_other_ref, a_ref, c_ref, out_ref, right):
    refs = {("left", True): left_ref, ("left", False): left_other_ref, "a": a_ref, "c": c_ref}
    for_own_parity(functools.partial(add_columns, refs, (*LEFT, "a", "c"), None, out_ref, right))


def late_kernel(left_ref, left_other_ref, b_ref, d_ref, e_ref, old_ref, out_ref, right):
    refs = {("left", True): left_ref, ("left", False): left_other_ref, "b": b_ref, "d": d_ref, "e": e_ref}
    for_own_parity(functools.partial(add_columns, refs, ("b", "d", "e"), old_ref, out_ref, right))


def staged_early_kernel(left_ref, left_other_ref, staged_ref, old_ref, out_ref, right):
    refs = {("left", True): left_ref, ("left", False): left_other_ref, "early": staged_ref}
    for_own_parity(functools.partial(add_columns, refs, ("early",), old_ref, out_ref, right))
    out_ref[BR * NCOL] = jnp.zeros((BLK, BLK), out_ref.dtype)


def multiply_kernel(left_ref, left_other_ref, staged_ref, old_ref, table_ref, _, out_ref, *rest):
    right, made, table, table_sem, out_sem = rest
    refs = {("left", True): left_ref, ("left", False): left_other_ref, "late": staged_ref}
    load = pltpu.make_async_copy(table_ref, table, table_sem)
    load.start()
    made[BR * NCOL] = jnp.zeros((BLK, BLK), made.dtype)

    @for_own_parity
    def _(mine):
        add_columns(refs, ("late",), old_ref, made, right, mine, late_pairs)
        load.wait()
        here = [place for place in stored_places(mine) if place not in inner_places(mine)]
        late = [columns_of(mine).index(j) for j in late_columns(mine)]
        for place in here:
            store(made if place % NCOL in late else old_ref, table, out_ref, place, out_sem)
        wait_for(len(here), made, out_ref, out_sem)


def local(values, block_rows, block_cols, counts):
    slots = values.shape[1]
    row_count, col_count = lax.axis_size("row"), lax.axis_size("col")
    nblocks = BR * row_count
    smem = pl.BlockSpec(memory_space=pltpu.SMEM)
    vmem = pl.BlockSpec(memory_space=pltpu.VMEM)
    hbm = pl.BlockSpec(memory_space=pltpu.HBM)
    params = pltpu.CompilerParams(vmem_limit_bytes=VMEM_LIMIT)
    values, *places = (pltpu.with_memory_space_constraint(x, pltpu.HBM) for x in (values, block_rows, block_cols))
    index_scratch = [
        pltpu.SMEM((1, slots), jnp.int32),
        pltpu.SMEM((1, slots), jnp.int32),
        pltpu.SemaphoreType.DMA((2,)),
    ]
    table_shape = (1, BLK)

    def blocks(count, dtype=values.dtype):
        return jax.ShapeDtypeStruct((count, BLK, BLK), dtype)

    def cost(products, nbytes):
        return pl.CostEstimate(flops=2 * products * BLK**3, bytes_accessed=nbytes, transcendentals=0)

    def right_scratch(pairs):
        return pltpu.VMEM((pairs, 2, NCOL * BLK, 2 * BLK), values.dtype)

    *packed, left = pl.pallas_call(
        functools.partial(pack_kernel, nblocks, slots),
        out_shape=[blocks(SIZES[name]) for name in "abcd"]
        + [jax.ShapeDtypeStruct((BR * BLK, NCOL * BLK), values.dtype)],
        in_specs=[hbm] * 3,
        out_specs=[vmem] * 5,
        scratch_shapes=[
            pltpu.VMEM((slots + 1, BLK, BLK), values.dtype),
            pltpu.SMEM((BR * WIDTH + 1,), jnp.int32),
            *index_scratch,
            pltpu.SemaphoreType.DMA,
        ],
        compiler_params=params,
        name="pack",
    )(*places, values)

    def towards(name, message):
        pairs = []
        for r in range(row_count):
            for c in range(col_count):
                distance = DISTANCES[name] or (3 if (r + c) % 2 == 1 else -3)
                source = (r - distance if r % 2 == 1 else r + distance) % row_count
                pairs.append((source * col_count + c, r * col_count + c))
        return lax.ppermute(message, ("row", "col"), pairs)

    def swapped(block):
        return lax.ppermute(block, "col", [(0, 1), (1, 0)])

    left_other = swapped(left)
    got = [towards(name, message) for name, message in zip("abcd", packed)]
    message = pl.pallas_call(
        pack_e_kernel,
        out_shape=blocks(SIZES["e"]),
        in_specs=[vmem] * 2,
        out_specs=vmem,
        compiler_params=params,
        name="pack_e",
    )(left, left_other)
    got.append(towards("e", message))
    table, out = pl.pallas_call(
        functools.partial(inner_kernel, nblocks, slots),
        out_shape=[jax.ShapeDtypeStruct(table_shape, jnp.int32), jax.ShapeDtypeStruct(values.shape, jnp.float32)],
        in_specs=[hbm] * 2 + [smem] + [vmem] * 2,
        out_specs=[vmem, hbm],
        scratch_shapes=[
            pltpu.VMEM((2, NCOL * BLK, 2 * BLK), values.dtype),
            pltpu.VMEM((BR * NCOL + 1, BLK, BLK), jnp.float32),
            pltpu.SMEM(table_shape, jnp.int32),
            *index_scratch,
            pltpu.SemaphoreType.DMA,
            pltpu.SemaphoreType.DMA,
        ],
        compiler_params=params,
        cost_estimate=cost(3 * 2 * 17, 4 * values.size),
        name="inner",
    )(*places, counts, left, left_other)
    a, b, c, d, e = got

    def staged(part, arrays):
        return swapped(
            pl.pallas_call(
                functools.partial(stage_kernel, part),
                out_shape=blocks(STAGED_SIZE[part]),
                in_specs=[vmem] * len(arrays),
                out_specs=vmem,
                compiler_params=params,
                name="stage_" + part,
            )(*arrays)
        )

    def added(kernel, name, products, arrays):
        return pl.pallas_call(
            kernel,
            out_shape=blocks(BR * NCOL + 1, jnp.float32),
            in_specs=[vmem] * len(arrays),
            out_specs=vmem,
            scratch_shapes=[right_scratch(4)],
            compiler_params=params,
            cost_estimate=cost(products, 0),
            name=name,
        )(*arrays)

    a, c, table = lax.optimization_barrier((a, c, table))
    staged_early = staged("early", (a, c))
    total = added(early_kernel, "early", EARLY_COST, (left, left_other, a, c))
    b, d, e, total = lax.optimization_barrier((b, d, e, total))
    staged_late = staged("late", (b, d, e))
    total = added(late_kernel, "late", LATE_COST, (left, left_other, b, d, e, total))
    total = added(staged_early_kernel, "staged_early", EARLY_COST, (left, left_other, staged_early, total))
    return pl.pallas_call(
        multiply_kernel,
        out_shape=jax.ShapeDtypeStruct(values.shape, jnp.float32),
        in_specs=[vmem] * 5 + [hbm],
        out_specs=hbm,
        scratch_shapes=[
            right_scratch(4),
            pltpu.VMEM((BR * NCOL + 1, BLK, BLK), jnp.float32),
            pltpu.SMEM(table_shape, jnp.int32),
            pltpu.SemaphoreType.DMA,
            pltpu.SemaphoreType.DMA,
        ],
        input_output_aliases={5: 0},
        compiler_params=params,
        name="multiply",
    )(left, left_other, staged_late, total, table, out)


def solution(mesh):
    return jax.shard_map(
        local,
        mesh=mesh,
        in_specs=(
            P(("parts", "row"), "col", None, None),
            P(("parts", "row"), "col"),
            P(("parts", "row"), "col"),
            P(("parts", "row"), "col"),
        ),
        out_specs=P(("parts", "row"), "col", None, None),
        check_vma=False,
    )
```

```python
import functools

import jax
import jax.numpy as jnp
from jax import lax
from jax.experimental import pallas as pl
from jax.experimental.pallas import tpu as pltpu
from jax.sharding import PartitionSpec as P

BLK = 128
BR = 3
HB = 7
WIDTH = 2 * HB + 1
LOW, HIGH = -HB, BR - 1 + HB
NCOL = 9
SOURCES = 32
EARLY_COST = 1
LATE_COST = 4000
VMEM_LIMIT = 12 * 2**20

DISTANCES = {"a": 1, "b": -1, "c": -2, "d": 2, "e": None}
SENT = {
    ("a", 1): [(3, 3), (5, 5), (3, 5), (3, 7), (4, 7), (5, 7), (3, 9), (4, 9), (5, 9), (3, -3), (3, -1), (4, -3), (5, -1)],
    ("a", 0): [(4, 4), (3, 4), (5, 4), (3, 6), (4, 6), (5, 6), (3, 8), (4, 8), (5, 8), (3, -2), (4, -2), (5, -2), (3, -4)],
    ("b", 1): [(-1, -1), (-3, -3), (-1, -3), (-1, -7), (-2, -7), (-3, -7)],
    ("b", 0): [(-2, -2), (-1, -2), (-3, -2), (-1, 4), (-1, -4), (-1, -6)],
    ("c", 1): [(-5, -5), (-4, -7), (-5, -7), (-6, -7), (-4, -3), (-5, -1), (-5, -3), (-6, -3)],
    ("c", 0): [(-4, -4), (-6, -6), (-4, -6), (-4, -2), (-5, -2), (-6, -2), (-5, -4), (-5, -6)],
    ("d", 1): [(6, 9), (7, 7), (7, 9), (8, 9), (6, -1)],
    ("d", 0): [(6, 6), (6, 8), (8, 8), (7, 6), (7, 8)],
    ("e", 1): [(9, 9)],
    ("e", 0): [(-7, -7)],
}
SIZES = {name: len(SENT[name, 1]) for name in DISTANCES}
PARTS = {"early": "ac", "late": "bde"}
STAGED = {
    (part, parity): [
        (name, n, (k, j))
        for name in names
        for n, (k, j) in enumerate(SENT[name, parity])
        if k % 2 != j % 2 or (k, j) == (-7, -7)
    ]
    for part, names in PARTS.items()
    for parity in (0, 1)
}
STAGED_SIZE = {part: max(len(STAGED[part, parity]) for parity in (0, 1)) for part in PARTS}


def columns_of(parity):
    return [j for j in range(LOW, HIGH + 1) if j % 2 == parity]


def own_parity():
    return (lax.axis_index("row") + lax.axis_index("col")) % 2


def for_own_parity(body):
    parity = own_parity()
    for mine in (0, 1):
        pl.when(parity == mine)(functools.partial(body, mine))


def slot_position(rows_ref, cols_ref, slot, nblocks):
    panel = lax.axis_index("row")
    row = rows_ref[0, slot] - panel * BR
    band = cols_ref[0, slot] - rows_ref[0, slot] + HB
    band = jnp.where(band < 0, band + nblocks, band)
    band = jnp.where(band >= nblocks, band - nblocks, band)
    odd = panel % 2 == 1
    return row, jnp.where(odd, BR - 1 - row, row), jnp.where(odd, WIDTH - 1 - band, band)


def index_copies(hbm_refs, smem_refs, sems):
    return [pltpu.make_async_copy(a, b, sems.at[i]) for i, (a, b) in enumerate(zip(hbm_refs, smem_refs))]


def pack_kernel(nblocks, slots, rows_ref, cols_ref, values_ref, *rest):
    out_refs = dict(zip("abcd", rest[:4]))
    left_ref, held, table, *index, sems, value_sem = rest[4:]
    copies = index_copies((rows_ref, cols_ref), index, sems)
    load = pltpu.make_async_copy(values_ref.at[0], held.at[pl.ds(0, slots)], value_sem)
    for copy in (*copies, load):
        copy.start()
    held[slots] = jnp.zeros((BLK, BLK), held.dtype)
    for i in range(BR * WIDTH + 1):
        table[i] = slots
    for copy in copies:
        copy.wait()
    for m in reversed(range(slots)):
        real_row, row, band = slot_position(*index, m, nblocks)
        table[jnp.where(real_row >= 0, row * WIDTH + band, BR * WIDTH)] = m
    load.wait()

    @for_own_parity
    def _(mine):
        for name, ref in out_refs.items():
            distance = DISTANCES[name]
            for n, (k, j) in enumerate(SENT[name, (mine + distance) % 2]):
                at = (k - BR * distance) * WIDTH + j - k + HB
                if distance % 2 == 1:
                    at = BR * WIDTH - 1 - at
                ref[n] = held[table[at]]
        columns = columns_of(mine)
        for i in range(BR):
            for n in range(NCOL):
                rows, cols = pl.ds(i * BLK, BLK), pl.ds(n * BLK, BLK)
                if n < len(columns) and abs(columns[n] - i) <= HB:
                    left_ref[rows, cols] = held[table[i * WIDTH + columns[n] - i + HB]]
                else:
                    left_ref[rows, cols] = jnp.zeros((BLK, BLK), left_ref.dtype)


def find_block(parity, k, j):
    if abs(k - j) > HB:
        return None
    if 0 <= k < BR:
        return ("left", parity == j % 2), (k, columns_of(j % 2).index(j)), False
    if 0 <= j < BR:
        return ("left", parity == k % 2), (j, columns_of(k % 2).index(k)), True
    for a, b, flip in ((k, j, False), (j, k, True)):
        for name in DISTANCES:
            if (a, b) in SENT[name, parity]:
                return name, SENT[name, parity].index((a, b)), flip
        for part in PARTS:
            staged = [position for _, _, position in STAGED[part, 1 - parity]]
            if (a, b) in staged:
                return part, staged.index((a, b)), not flip
    raise AssertionError((k, j))


def columns_product(refs, right, parity, js, wanted):
    total = None
    for own in (True, False):
        kind = parity if own else 1 - parity
        found = {}
        for k in columns_of(kind):
            for j in js:
                place = find_block(parity, k, j)
                if place is not None and place[0] in wanted:
                    found[k, j] = place
        if not found:
            continue
        first, last = min(k for k, _ in found), max(k for k, _ in found)
        ks = [k for k in columns_of(kind) if first <= k <= last]
        side = right.at[0 if own else 1]
        for x, k in enumerate(ks):
            for y, j in enumerate(js):
                if (k, j) in found:
                    source, place, flip = found[k, j]
                    if isinstance(place, tuple):
                        block = refs[source][pl.ds(place[0] * BLK, BLK), pl.ds(place[1] * BLK, BLK)]
                    else:
                        block = refs[source][place]
                    block = block.T if flip else block
                else:
                    block = jnp.zeros((BLK, BLK), right.dtype)
                side[pl.ds(x * BLK, BLK), pl.ds(y * BLK, BLK)] = block
        start = columns_of(kind).index(first)
        part = jnp.dot(
            refs["left", own][:, pl.ds(start * BLK, len(ks) * BLK)],
            side[pl.ds(0, len(ks) * BLK), pl.ds(0, len(js) * BLK)],
            preferred_element_type=jnp.float32,
        )
        total = part if total is None else total + part
    return total


LEFT = (("left", True), ("left", False))


def block_of(total, i, y):
    return total[i * BLK : (i + 1) * BLK, y * BLK : (y + 1) * BLK]


def stored_places(parity):
    columns = columns_of(parity)
    return [i * NCOL + n for i in range(BR) for n, j in enumerate(columns) if abs(i - j) <= HB]


def inner_places(parity):
    return [i * NCOL + n for i in range(BR) for n, j in enumerate(columns_of(parity)) if 0 <= j < BR]


def store(made, table, out_ref, place, sem):
    source = made.at[table[0, SOURCES + place]]
    pltpu.make_async_copy(source, out_ref.at[0, table[0, place]], sem).start()


def wait_for(count, made, out_ref, sem):
    pltpu.make_async_copy(made.at[pl.ds(0, count)], out_ref.at[0, pl.ds(0, count)], sem).wait()


def outer_pairs(parity):
    outer = [j for j in columns_of(parity) if not 0 <= j < BR]
    return [outer[n : n + 2] for n in range(0, len(outer), 2)]


def inner_kernel(nblocks, slots, rows_ref, cols_ref, counts_ref, left_ref, left_other_ref, *rest):
    table, out_ref, right, made, *index, sems, out_sem = rest
    copies = index_copies((rows_ref, cols_ref), index, sems)
    for copy in copies:
        copy.start()
    refs = {("left", True): left_ref, ("left", False): left_other_ref}

    @for_own_parity
    def _(mine):
        js = [j for j in columns_of(mine) if 0 <= j < BR]
        total = columns_product(refs, right, mine, js, LEFT)
        for i in range(BR):
            for y in range(2):
                if y < len(js):
                    made[i * NCOL + columns_of(mine).index(js[y])] = block_of(total, i, y)
        made[BR * NCOL] = jnp.zeros((BLK, BLK), made.dtype)

    for copy in copies:
        copy.wait()
    for place in range(BR * NCOL + 1):
        table[0, place] = -1
    count = counts_ref[0, 0]
    for m in range(slots):
        _, row, band = slot_position(*index, m, nblocks)
        table[0, jnp.where(m < count, row * NCOL + (row + band) // 2, BR * NCOL)] = m

    @for_own_parity
    def _(mine):
        unused = count
        for place in stored_places(mine):
            slot = table[0, place]
            absent = slot < 0
            table[0, place] = jnp.where(absent, unused, slot)
            table[0, SOURCES + place] = jnp.where(absent, BR * NCOL, place)
            unused = jnp.where(absent, unused + 1, unused)
        table[0, BR * NCOL] = unused
        here = [place for place in stored_places(mine) if place in inner_places(mine)]
        for place in here:
            store(made, table, out_ref, place, out_sem)
        stored = len(here)
        if len(stored_places(mine)) < slots:
            pltpu.make_async_copy(made.at[BR * NCOL], out_ref.at[0, unused], out_sem).start()
            stored += 1
        wait_for(stored, made, out_ref, out_sem)


def pack_e_kernel(left_ref, left_other_ref, e_ref):
    @for_own_parity
    def _(mine):
        i = 2 if mine == 0 else 0
        n = columns_of(0).index(i)
        e_ref[0] = (left_ref if mine == 0 else left_other_ref)[pl.ds(i * BLK, BLK), pl.ds(n * BLK, BLK)]


def stage_kernel(part, *refs):
    got = dict(zip(PARTS[part], refs))
    out_ref = refs[-1]

    @for_own_parity
    def _(mine):
        staged = STAGED[part, mine]
        for n, (name, place, _) in enumerate(staged):
            out_ref[n] = got[name][place].T
        for n in range(len(staged), STAGED_SIZE[part]):
            out_ref[n] = jnp.zeros((BLK, BLK), out_ref.dtype)


def late_columns(parity):
    found = [[find_block(parity, k, j) for k in range(LOW, HIGH + 1)] for j in columns_of(parity)]
    return [j for j, blocks in zip(columns_of(parity), found) if any(b is not None and b[0] == "late" for b in blocks)]


def late_pairs(parity):
    near = [j for j in late_columns(parity) if -BR <= j < 0]
    rest = [j for j in late_columns(parity) if j not in near]
    return [js[n : n + 2] for js in (near, rest) for n in range(0, len(js), 2)]


def add_columns(refs, wanted, old_ref, new_ref, right, mine, pairs=outer_pairs):
    for pair, js in enumerate(pairs(mine)):
        total = columns_product(refs, right.at[pair], mine, js, wanted)
        for i in range(BR):
            for y, j in enumerate(js):
                if abs(i - j) <= HB:
                    place = i * NCOL + columns_of(mine).index(j)
                    terms = [] if old_ref is None else [old_ref[place]]
                    terms += [] if total is None else [block_of(total, i, y)]
                    new_ref[place] = functools.reduce(jnp.add, terms)


def early_kernel(left_ref, left_other_ref, a_ref, c_ref, out_ref, right):
    refs = {("left", True): left_ref, ("left", False): left_other_ref, "a": a_ref, "c": c_ref}
    for_own_parity(functools.partial(add_columns, refs, (*LEFT, "a", "c"), None, out_ref, right))


def late_kernel(left_ref, left_other_ref, b_ref, d_ref, e_ref, old_ref, out_ref, right):
    refs = {("left", True): left_ref, ("left", False): left_other_ref, "b": b_ref, "d": d_ref, "e": e_ref}
    for_own_parity(functools.partial(add_columns, refs, ("b", "d", "e"), old_ref, out_ref, right))


def staged_early_kernel(left_ref, left_other_ref, staged_ref, old_ref, out_ref, right):
    refs = {("left", True): left_ref, ("left", False): left_other_ref, "early": staged_ref}
    for_own_parity(functools.partial(add_columns, refs, ("early",), old_ref, out_ref, right))
    out_ref[BR * NCOL] = jnp.zeros((BLK, BLK), out_ref.dtype)


def multiply_kernel(left_ref, left_other_ref, staged_ref, old_ref, table, _, out_ref, *rest):
    right, made, out_sem = rest
    refs = {("left", True): left_ref, ("left", False): left_other_ref, "late": staged_ref}
    made[BR * NCOL] = jnp.zeros((BLK, BLK), made.dtype)

    @for_own_parity
    def _(mine):
        here = [place for place in stored_places(mine) if place not in inner_places(mine)]
        late = [columns_of(mine).index(j) for j in late_columns(mine)]
        for place in here:
            if place % NCOL not in late:
                store(old_ref, table, out_ref, place, out_sem)
        add_columns(refs, ("late",), old_ref, made, right, mine, late_pairs)
        for place in here:
            if place % NCOL in late:
                store(made, table, out_ref, place, out_sem)
        wait_for(len(here), made, out_ref, out_sem)


def local(values, block_rows, block_cols, counts):
    slots = values.shape[1]
    row_count, col_count = lax.axis_size("row"), lax.axis_size("col")
    nblocks = BR * row_count
    smem = pl.BlockSpec(memory_space=pltpu.SMEM)
    vmem = pl.BlockSpec(memory_space=pltpu.VMEM)
    hbm = pl.BlockSpec(memory_space=pltpu.HBM)
    params = pltpu.CompilerParams(vmem_limit_bytes=VMEM_LIMIT)
    values, *places = (pltpu.with_memory_space_constraint(x, pltpu.HBM) for x in (values, block_rows, block_cols))
    index_scratch = [
        pltpu.SMEM((1, slots), jnp.int32),
        pltpu.SMEM((1, slots), jnp.int32),
        pltpu.SemaphoreType.DMA((2,)),
    ]
    table_shape = (1, BLK)

    def blocks(count, dtype=values.dtype):
        return jax.ShapeDtypeStruct((count, BLK, BLK), dtype)

    def cost(products, nbytes):
        return pl.CostEstimate(flops=2 * products * BLK**3, bytes_accessed=nbytes, transcendentals=0)

    def right_scratch(pairs):
        return pltpu.VMEM((pairs, 2, NCOL * BLK, 2 * BLK), values.dtype)

    *packed, left = pl.pallas_call(
        functools.partial(pack_kernel, nblocks, slots),
        out_shape=[blocks(SIZES[name]) for name in "abcd"]
        + [jax.ShapeDtypeStruct((BR * BLK, NCOL * BLK), values.dtype)],
        in_specs=[hbm] * 3,
        out_specs=[vmem] * 5,
        scratch_shapes=[
            pltpu.VMEM((slots + 1, BLK, BLK), values.dtype),
            pltpu.SMEM((BR * WIDTH + 1,), jnp.int32),
            *index_scratch,
            pltpu.SemaphoreType.DMA,
        ],
        compiler_params=params,
        name="pack",
    )(*places, values)

    def towards(name, message):
        pairs = []
        for r in range(row_count):
            for c in range(col_count):
                distance = DISTANCES[name] or (3 if (r + c) % 2 == 1 else -3)
                source = (r - distance if r % 2 == 1 else r + distance) % row_count
                pairs.append((source * col_count + c, r * col_count + c))
        return lax.ppermute(message, ("row", "col"), pairs)

    def swapped(block):
        return lax.ppermute(block, "col", [(0, 1), (1, 0)])

    left_other = swapped(left)
    got = [towards(name, message) for name, message in zip("abcd", packed)]
    message = pl.pallas_call(
        pack_e_kernel,
        out_shape=blocks(SIZES["e"]),
        in_specs=[vmem] * 2,
        out_specs=vmem,
        compiler_params=params,
        name="pack_e",
    )(left, left_other)
    got.append(towards("e", message))
    table, out = pl.pallas_call(
        functools.partial(inner_kernel, nblocks, slots),
        out_shape=[pltpu.SMEM(table_shape, jnp.int32), jax.ShapeDtypeStruct(values.shape, jnp.float32)],
        in_specs=[hbm] * 2 + [smem] + [vmem] * 2,
        out_specs=[smem, hbm],
        scratch_shapes=[
            pltpu.VMEM((2, NCOL * BLK, 2 * BLK), values.dtype),
            pltpu.VMEM((BR * NCOL + 1, BLK, BLK), jnp.float32),
            *index_scratch,
            pltpu.SemaphoreType.DMA,
        ],
        compiler_params=params,
        cost_estimate=cost(3 * 2 * 17, 4 * values.size),
        name="inner",
    )(*places, counts, left, left_other)
    a, b, c, d, e = got

    def staged(part, arrays):
        return swapped(
            pl.pallas_call(
                functools.partial(stage_kernel, part),
                out_shape=blocks(STAGED_SIZE[part]),
                in_specs=[vmem] * len(arrays),
                out_specs=vmem,
                compiler_params=params,
                name="stage_" + part,
            )(*arrays)
        )

    def added(kernel, name, products, arrays):
        return pl.pallas_call(
            kernel,
            out_shape=blocks(BR * NCOL + 1, jnp.float32),
            in_specs=[vmem] * len(arrays),
            out_specs=vmem,
            scratch_shapes=[right_scratch(4)],
            compiler_params=params,
            cost_estimate=cost(products, 0),
            name=name,
        )(*arrays)

    a, c, table = lax.optimization_barrier((a, c, table))
    staged_early = staged("early", (a, c))
    total = added(early_kernel, "early", EARLY_COST, (left, left_other, a, c))
    b, d, e, total = lax.optimization_barrier((b, d, e, total))
    staged_late = staged("late", (b, d, e))
    total = added(late_kernel, "late", LATE_COST, (left, left_other, b, d, e, total))
    total = added(staged_early_kernel, "staged_early", EARLY_COST, (left, left_other, staged_early, total))
    return pl.pallas_call(
        multiply_kernel,
        out_shape=jax.ShapeDtypeStruct(values.shape, jnp.float32),
        in_specs=[vmem] * 4 + [smem, hbm],
        out_specs=hbm,
        scratch_shapes=[
            right_scratch(4),
            pltpu.VMEM((BR * NCOL + 1, BLK, BLK), jnp.float32),
            pltpu.SemaphoreType.DMA,
        ],
        input_output_aliases={5: 0},
        compiler_params=params,
        name="multiply",
    )(left, left_other, staged_late, total, pltpu.with_memory_space_constraint(table, pltpu.SMEM), out)


def solution(mesh):
    return jax.shard_map(
        local,
        mesh=mesh,
        in_specs=(
            P(("parts", "row"), "col", None, None),
            P(("parts", "row"), "col"),
            P(("parts", "row"), "col"),
            P(("parts", "row"), "col"),
        ),
        out_specs=P(("parts", "row"), "col", None, None),
        check_vma=False,
    )
```

```python
import functools

import jax
import jax.numpy as jnp
from jax import lax
from jax.experimental import pallas as pl
from jax.experimental.pallas import tpu as pltpu
from jax.sharding import PartitionSpec as P

BLK = 128
BR = 3
HB = 7
WIDTH = 2 * HB + 1
LOW, HIGH = -HB, BR - 1 + HB
NCOL = 9
SOURCES = 32
EARLY_COST = 1
LATE_COST = 4000
VMEM_LIMIT = 12 * 2**20

DISTANCES = {"a": 1, "b": -1, "c": -2, "d": 2, "e": None}
SENT = {
    ("a", 1): [(3, 3), (5, 5), (3, 5), (3, 7), (4, 7), (5, 7), (3, 9), (4, 9), (5, 9), (3, -3), (3, -1), (4, -3), (5, -1)],
    ("a", 0): [(4, 4), (3, 4), (5, 4), (3, 6), (4, 6), (5, 6), (3, 8), (4, 8), (5, 8), (3, -2), (4, -2), (5, -2), (3, -4)],
    ("b", 1): [(-1, -1), (-3, -3), (-1, -3), (-1, -7), (-2, -7), (-3, -7)],
    ("b", 0): [(-2, -2), (-1, -2), (-3, -2), (-1, 4), (-1, -4), (-1, -6)],
    ("c", 1): [(-5, -5), (-4, -7), (-5, -7), (-6, -7), (-4, -3), (-5, -1), (-5, -3), (-6, -3)],
    ("c", 0): [(-4, -4), (-6, -6), (-4, -6), (-4, -2), (-5, -2), (-6, -2), (-5, -4), (-5, -6)],
    ("d", 1): [(6, 9), (7, 7), (7, 9), (8, 9), (6, -1)],
    ("d", 0): [(6, 6), (6, 8), (8, 8), (7, 6), (7, 8)],
    ("e", 1): [(9, 9)],
    ("e", 0): [(-7, -7)],
}
SIZES = {name: len(SENT[name, 1]) for name in DISTANCES}
PARTS = {"early": "ac", "late": "bde"}
STAGED = {
    (part, parity): [
        (name, n, (k, j))
        for name in names
        for n, (k, j) in enumerate(SENT[name, parity])
        if k % 2 != j % 2 or (k, j) == (-7, -7)
    ]
    for part, names in PARTS.items()
    for parity in (0, 1)
}
STAGED_SIZE = {part: max(len(STAGED[part, parity]) for parity in (0, 1)) for part in PARTS}


def columns_of(parity):
    return [j for j in range(LOW, HIGH + 1) if j % 2 == parity]


def own_parity():
    return (lax.axis_index("row") + lax.axis_index("col")) % 2


def for_own_parity(body):
    parity = own_parity()
    for mine in (0, 1):
        pl.when(parity == mine)(functools.partial(body, mine))


def slot_position(rows_ref, cols_ref, slot, nblocks):
    panel = lax.axis_index("row")
    row = rows_ref[0, slot] - panel * BR
    band = cols_ref[0, slot] - rows_ref[0, slot] + HB
    band = jnp.where(band < 0, band + nblocks, band)
    band = jnp.where(band >= nblocks, band - nblocks, band)
    odd = panel % 2 == 1
    return row, jnp.where(odd, BR - 1 - row, row), jnp.where(odd, WIDTH - 1 - band, band)


def index_copies(hbm_refs, smem_refs, sems):
    return [pltpu.make_async_copy(a, b, sems.at[i]) for i, (a, b) in enumerate(zip(hbm_refs, smem_refs))]


def pack_kernel(nblocks, slots, rows_ref, cols_ref, values_ref, *rest):
    out_refs = dict(zip("abcd", rest[:4]))
    left_ref, held, table, *index, sems, value_sem = rest[4:]
    copies = index_copies((rows_ref, cols_ref), index, sems)
    load = pltpu.make_async_copy(values_ref.at[0], held.at[pl.ds(0, slots)], value_sem)
    for copy in (*copies, load):
        copy.start()
    held[slots] = jnp.zeros((BLK, BLK), held.dtype)
    for i in range(BR * WIDTH + 1):
        table[i] = slots
    for copy in copies:
        copy.wait()
    for m in reversed(range(slots)):
        real_row, row, band = slot_position(*index, m, nblocks)
        table[jnp.where(real_row >= 0, row * WIDTH + band, BR * WIDTH)] = m
    load.wait()

    @for_own_parity
    def _(mine):
        for name, ref in out_refs.items():
            distance = DISTANCES[name]
            for n, (k, j) in enumerate(SENT[name, (mine + distance) % 2]):
                at = (k - BR * distance) * WIDTH + j - k + HB
                if distance % 2 == 1:
                    at = BR * WIDTH - 1 - at
                ref[n] = held[table[at]]
        columns = columns_of(mine)
        for i in range(BR):
            for n in range(NCOL):
                rows, cols = pl.ds(i * BLK, BLK), pl.ds(n * BLK, BLK)
                if n < len(columns) and abs(columns[n] - i) <= HB:
                    left_ref[rows, cols] = held[table[i * WIDTH + columns[n] - i + HB]]
                else:
                    left_ref[rows, cols] = jnp.zeros((BLK, BLK), left_ref.dtype)


def find_block(parity, k, j):
    if abs(k - j) > HB:
        return None
    if 0 <= k < BR:
        return ("left", parity == j % 2), (k, columns_of(j % 2).index(j)), False
    if 0 <= j < BR:
        return ("left", parity == k % 2), (j, columns_of(k % 2).index(k)), True
    for a, b, flip in ((k, j, False), (j, k, True)):
        for name in DISTANCES:
            if (a, b) in SENT[name, parity]:
                return name, SENT[name, parity].index((a, b)), flip
        for part in PARTS:
            staged = [position for _, _, position in STAGED[part, 1 - parity]]
            if (a, b) in staged:
                return part, staged.index((a, b)), flip if part == "late" else not flip
    raise AssertionError((k, j))


def columns_product(refs, right, parity, js, wanted):
    total = None
    for own in (True, False):
        kind = parity if own else 1 - parity
        found = {}
        for k in columns_of(kind):
            for j in js:
                place = find_block(parity, k, j)
                if place is not None and place[0] in wanted:
                    found[k, j] = place
        if not found:
            continue
        first, last = min(k for k, _ in found), max(k for k, _ in found)
        ks = [k for k in columns_of(kind) if first <= k <= last]
        side = right.at[0 if own else 1]
        for x, k in enumerate(ks):
            for y, j in enumerate(js):
                if (k, j) in found:
                    source, place, flip = found[k, j]
                    if isinstance(place, tuple):
                        block = refs[source][pl.ds(place[0] * BLK, BLK), pl.ds(place[1] * BLK, BLK)]
                    else:
                        block = refs[source][place]
                    block = block.T if flip else block
                else:
                    block = jnp.zeros((BLK, BLK), right.dtype)
                side[pl.ds(x * BLK, BLK), pl.ds(y * BLK, BLK)] = block
        start = columns_of(kind).index(first)
        part = jnp.dot(
            refs["left", own][:, pl.ds(start * BLK, len(ks) * BLK)],
            side[pl.ds(0, len(ks) * BLK), pl.ds(0, len(js) * BLK)],
            preferred_element_type=jnp.float32,
        )
        total = part if total is None else total + part
    return total


LEFT = (("left", True), ("left", False))


def block_of(total, i, y):
    return total[i * BLK : (i + 1) * BLK, y * BLK : (y + 1) * BLK]


def stored_places(parity):
    columns = columns_of(parity)
    return [i * NCOL + n for i in range(BR) for n, j in enumerate(columns) if abs(i - j) <= HB]


def inner_places(parity):
    return [i * NCOL + n for i in range(BR) for n, j in enumerate(columns_of(parity)) if 0 <= j < BR]


def store(made, table, out_ref, place, sem):
    source = made.at[table[0, SOURCES + place]]
    pltpu.make_async_copy(source, out_ref.at[0, table[0, place]], sem).start()


def wait_for(count, made, out_ref, sem):
    pltpu.make_async_copy(made.at[pl.ds(0, count)], out_ref.at[0, pl.ds(0, count)], sem).wait()


def outer_pairs(parity):
    outer = [j for j in columns_of(parity) if not 0 <= j < BR]
    return [outer[n : n + 2] for n in range(0, len(outer), 2)]


def inner_kernel(nblocks, slots, rows_ref, cols_ref, counts_ref, left_ref, left_other_ref, *rest):
    table, out_ref, right, made, *index, sems, out_sem = rest
    copies = index_copies((rows_ref, cols_ref), index, sems)
    for copy in copies:
        copy.start()
    refs = {("left", True): left_ref, ("left", False): left_other_ref}

    @for_own_parity
    def _(mine):
        js = [j for j in columns_of(mine) if 0 <= j < BR]
        total = columns_product(refs, right, mine, js, LEFT)
        for i in range(BR):
            for y in range(2):
                if y < len(js):
                    made[i * NCOL + columns_of(mine).index(js[y])] = block_of(total, i, y)
        made[BR * NCOL] = jnp.zeros((BLK, BLK), made.dtype)

    for copy in copies:
        copy.wait()
    for place in range(BR * NCOL + 1):
        table[0, place] = -1
    count = counts_ref[0, 0]
    for m in range(slots):
        _, row, band = slot_position(*index, m, nblocks)
        table[0, jnp.where(m < count, row * NCOL + (row + band) // 2, BR * NCOL)] = m

    @for_own_parity
    def _(mine):
        unused = count
        for place in stored_places(mine):
            slot = table[0, place]
            absent = slot < 0
            table[0, place] = jnp.where(absent, unused, slot)
            table[0, SOURCES + place] = jnp.where(absent, BR * NCOL, place)
            unused = jnp.where(absent, unused + 1, unused)
        table[0, BR * NCOL] = unused
        here = [place for place in stored_places(mine) if place in inner_places(mine)]
        for place in here:
            store(made, table, out_ref, place, out_sem)
        stored = len(here)
        if len(stored_places(mine)) < slots:
            pltpu.make_async_copy(made.at[BR * NCOL], out_ref.at[0, unused], out_sem).start()
            stored += 1
        wait_for(stored, made, out_ref, out_sem)


def pack_e_kernel(left_ref, left_other_ref, e_ref):
    @for_own_parity
    def _(mine):
        i = 2 if mine == 0 else 0
        n = columns_of(0).index(i)
        e_ref[0] = (left_ref if mine == 0 else left_other_ref)[pl.ds(i * BLK, BLK), pl.ds(n * BLK, BLK)]


def stage_kernel(part, *refs):
    got = dict(zip(PARTS[part], refs))
    out_ref = refs[-1]

    @for_own_parity
    def _(mine):
        staged = STAGED[part, mine]
        for n, (name, place, _) in enumerate(staged):
            out_ref[n] = got[name][place] if part == "late" else got[name][place].T
        for n in range(len(staged), STAGED_SIZE[part]):
            out_ref[n] = jnp.zeros((BLK, BLK), out_ref.dtype)


def late_columns(parity):
    found = [[find_block(parity, k, j) for k in range(LOW, HIGH + 1)] for j in columns_of(parity)]
    return [j for j, blocks in zip(columns_of(parity), found) if any(b is not None and b[0] == "late" for b in blocks)]


def late_pairs(parity):
    near = [j for j in late_columns(parity) if -BR <= j < 0]
    rest = [j for j in late_columns(parity) if j not in near]
    return [js[n : n + 2] for js in (near, rest) for n in range(0, len(js), 2)]


def add_columns(refs, wanted, old_ref, new_ref, right, mine, pairs=outer_pairs):
    for pair, js in enumerate(pairs(mine)):
        total = columns_product(refs, right.at[pair], mine, js, wanted)
        for i in range(BR):
            for y, j in enumerate(js):
                if abs(i - j) <= HB:
                    place = i * NCOL + columns_of(mine).index(j)
                    terms = [] if old_ref is None else [old_ref[place]]
                    terms += [] if total is None else [block_of(total, i, y)]
                    new_ref[place] = functools.reduce(jnp.add, terms)


def early_kernel(left_ref, left_other_ref, a_ref, c_ref, out_ref, right):
    refs = {("left", True): left_ref, ("left", False): left_other_ref, "a": a_ref, "c": c_ref}
    for_own_parity(functools.partial(add_columns, refs, (*LEFT, "a", "c"), None, out_ref, right))


def late_kernel(left_ref, left_other_ref, b_ref, d_ref, e_ref, old_ref, out_ref, right):
    refs = {("left", True): left_ref, ("left", False): left_other_ref, "b": b_ref, "d": d_ref, "e": e_ref}
    for_own_parity(functools.partial(add_columns, refs, ("b", "d", "e"), old_ref, out_ref, right))


def staged_early_kernel(left_ref, left_other_ref, staged_ref, old_ref, out_ref, right):
    refs = {("left", True): left_ref, ("left", False): left_other_ref, "early": staged_ref}
    for_own_parity(functools.partial(add_columns, refs, ("early",), old_ref, out_ref, right))
    out_ref[BR * NCOL] = jnp.zeros((BLK, BLK), out_ref.dtype)


def multiply_kernel(left_ref, left_other_ref, staged_ref, old_ref, table, _, out_ref, *rest):
    right, made, out_sem = rest
    refs = {("left", True): left_ref, ("left", False): left_other_ref, "late": staged_ref}
    made[BR * NCOL] = jnp.zeros((BLK, BLK), made.dtype)

    @for_own_parity
    def _(mine):
        here = [place for place in stored_places(mine) if place not in inner_places(mine)]
        late = [columns_of(mine).index(j) for j in late_columns(mine)]
        for place in here:
            if place % NCOL not in late:
                store(old_ref, table, out_ref, place, out_sem)
        add_columns(refs, ("late",), old_ref, made, right, mine, late_pairs)
        for place in here:
            if place % NCOL in late:
                store(made, table, out_ref, place, out_sem)
        wait_for(len(here), made, out_ref, out_sem)


def local(values, block_rows, block_cols, counts):
    slots = values.shape[1]
    row_count, col_count = lax.axis_size("row"), lax.axis_size("col")
    nblocks = BR * row_count
    smem = pl.BlockSpec(memory_space=pltpu.SMEM)
    vmem = pl.BlockSpec(memory_space=pltpu.VMEM)
    hbm = pl.BlockSpec(memory_space=pltpu.HBM)
    params = pltpu.CompilerParams(vmem_limit_bytes=VMEM_LIMIT)
    values, *places = (pltpu.with_memory_space_constraint(x, pltpu.HBM) for x in (values, block_rows, block_cols))
    index_scratch = [
        pltpu.SMEM((1, slots), jnp.int32),
        pltpu.SMEM((1, slots), jnp.int32),
        pltpu.SemaphoreType.DMA((2,)),
    ]
    table_shape = (1, BLK)

    def blocks(count, dtype=values.dtype):
        return jax.ShapeDtypeStruct((count, BLK, BLK), dtype)

    def cost(products, nbytes):
        return pl.CostEstimate(flops=2 * products * BLK**3, bytes_accessed=nbytes, transcendentals=0)

    def right_scratch(pairs):
        return pltpu.VMEM((pairs, 2, NCOL * BLK, 2 * BLK), values.dtype)

    *packed, left = pl.pallas_call(
        functools.partial(pack_kernel, nblocks, slots),
        out_shape=[blocks(SIZES[name]) for name in "abcd"]
        + [jax.ShapeDtypeStruct((BR * BLK, NCOL * BLK), values.dtype)],
        in_specs=[hbm] * 3,
        out_specs=[vmem] * 5,
        scratch_shapes=[
            pltpu.VMEM((slots + 1, BLK, BLK), values.dtype),
            pltpu.SMEM((BR * WIDTH + 1,), jnp.int32),
            *index_scratch,
            pltpu.SemaphoreType.DMA,
        ],
        compiler_params=params,
        name="pack",
    )(*places, values)

    def towards(name, message):
        pairs = []
        for r in range(row_count):
            for c in range(col_count):
                distance = DISTANCES[name] or (3 if (r + c) % 2 == 1 else -3)
                source = (r - distance if r % 2 == 1 else r + distance) % row_count
                pairs.append((source * col_count + c, r * col_count + c))
        return lax.ppermute(message, ("row", "col"), pairs)

    def swapped(block):
        return lax.ppermute(block, "col", [(0, 1), (1, 0)])

    left_other = swapped(left)
    got = [towards(name, message) for name, message in zip("abcd", packed)]
    message = pl.pallas_call(
        pack_e_kernel,
        out_shape=blocks(SIZES["e"]),
        in_specs=[vmem] * 2,
        out_specs=vmem,
        compiler_params=params,
        name="pack_e",
    )(left, left_other)
    got.append(towards("e", message))
    table, out = pl.pallas_call(
        functools.partial(inner_kernel, nblocks, slots),
        out_shape=[pltpu.SMEM(table_shape, jnp.int32), jax.ShapeDtypeStruct(values.shape, jnp.float32)],
        in_specs=[hbm] * 2 + [smem] + [vmem] * 2,
        out_specs=[smem, hbm],
        scratch_shapes=[
            pltpu.VMEM((2, NCOL * BLK, 2 * BLK), values.dtype),
            pltpu.VMEM((BR * NCOL + 1, BLK, BLK), jnp.float32),
            *index_scratch,
            pltpu.SemaphoreType.DMA,
        ],
        compiler_params=params,
        cost_estimate=cost(3 * 2 * 17, 4 * values.size),
        name="inner",
    )(*places, counts, left, left_other)
    a, b, c, d, e = got

    def staged(part, arrays):
        return swapped(
            pl.pallas_call(
                functools.partial(stage_kernel, part),
                out_shape=blocks(STAGED_SIZE[part]),
                in_specs=[vmem] * len(arrays),
                out_specs=vmem,
                compiler_params=params,
                name="stage_" + part,
            )(*arrays)
        )

    def added(kernel, name, products, arrays):
        return pl.pallas_call(
            kernel,
            out_shape=blocks(BR * NCOL + 1, jnp.float32),
            in_specs=[vmem] * len(arrays),
            out_specs=vmem,
            scratch_shapes=[right_scratch(4)],
            compiler_params=params,
            cost_estimate=cost(products, 0),
            name=name,
        )(*arrays)

    a, c, table = lax.optimization_barrier((a, c, table))
    staged_early = staged("early", (a, c))
    total = added(early_kernel, "early", EARLY_COST, (left, left_other, a, c))
    b, d, e, total = lax.optimization_barrier((b, d, e, total))
    staged_late = staged("late", (b, d, e))
    total = added(late_kernel, "late", LATE_COST, (left, left_other, b, d, e, total))
    total = added(staged_early_kernel, "staged_early", EARLY_COST, (left, left_other, staged_early, total))
    return pl.pallas_call(
        multiply_kernel,
        out_shape=jax.ShapeDtypeStruct(values.shape, jnp.float32),
        in_specs=[vmem] * 4 + [smem, hbm],
        out_specs=hbm,
        scratch_shapes=[
            right_scratch(4),
            pltpu.VMEM((BR * NCOL + 1, BLK, BLK), jnp.float32),
            pltpu.SemaphoreType.DMA,
        ],
        input_output_aliases={5: 0},
        compiler_params=params,
        name="multiply",
    )(left, left_other, staged_late, total, pltpu.with_memory_space_constraint(table, pltpu.SMEM), out)


def solution(mesh):
    return jax.shard_map(
        local,
        mesh=mesh,
        in_specs=(
            P(("parts", "row"), "col", None, None),
            P(("parts", "row"), "col"),
            P(("parts", "row"), "col"),
            P(("parts", "row"), "col"),
        ),
        out_specs=P(("parts", "row"), "col", None, None),
        check_vma=False,
    )
```

```python
import functools

import jax
import jax.numpy as jnp
from jax import lax
from jax.experimental import pallas as pl
from jax.experimental.pallas import tpu as pltpu
from jax.sharding import PartitionSpec as P

BLK = 128
BR = 3
HB = 7
WIDTH = 2 * HB + 1
LOW, HIGH = -HB, BR - 1 + HB
NCOL = 9
SOURCES = 32
EARLY_COST = 1
LATE_COST = 4000
VMEM_LIMIT = 12 * 2**20

DISTANCES = {"a": 1, "b": -1, "c": -2, "d": 2, "e": None}
SENT = {
    ("a", 1): [(3, 3), (5, 5), (3, 5), (3, 7), (4, 7), (5, 7), (3, 9), (4, 9), (5, 9), (3, -3), (3, -1), (4, -3), (5, -1)],
    ("a", 0): [(4, 4), (3, 4), (5, 4), (3, 6), (4, 6), (5, 6), (3, 8), (4, 8), (5, 8), (3, -2), (4, -2), (5, -2), (3, -4)],
    ("b", 1): [(-1, -1), (-3, -3), (-1, -3), (-1, -7), (-2, -7), (-3, -7)],
    ("b", 0): [(-2, -2), (-1, -2), (-3, -2), (-1, 4), (-1, -4), (-1, -6)],
    ("c", 1): [(-5, -5), (-4, -7), (-5, -7), (-6, -7), (-4, -3), (-5, -1), (-5, -3), (-6, -3)],
    ("c", 0): [(-4, -4), (-6, -6), (-4, -6), (-4, -2), (-5, -2), (-6, -2), (-5, -4), (-5, -6)],
    ("d", 1): [(6, 9), (7, 7), (7, 9), (8, 9), (6, -1)],
    ("d", 0): [(6, 6), (6, 8), (8, 8), (7, 6), (7, 8)],
    ("e", 1): [(9, 9)],
    ("e", 0): [(-7, -7)],
}
SIZES = {name: len(SENT[name, 1]) for name in DISTANCES}
PARTS = {"early": "ac", "late": "bde"}
STAGED = {
    (part, parity): [
        (name, n, (k, j))
        for name in names
        for n, (k, j) in enumerate(SENT[name, parity])
        if k % 2 != j % 2 or (k, j) == (-7, -7)
    ]
    for part, names in PARTS.items()
    for parity in (0, 1)
}
STAGED_SIZE = {part: max(len(STAGED[part, parity]) for parity in (0, 1)) for part in PARTS}


BOTH_WAYS = min(len(STAGED["late", parity]) for parity in (0, 1))


def columns_of(parity):
    return [j for j in range(LOW, HIGH + 1) if j % 2 == parity]


def own_parity():
    return (lax.axis_index("row") + lax.axis_index("col")) % 2


def for_own_parity(body):
    parity = own_parity()
    for mine in (0, 1):
        pl.when(parity == mine)(functools.partial(body, mine))


def slot_position(rows_ref, cols_ref, slot, nblocks):
    panel = lax.axis_index("row")
    row = rows_ref[0, slot] - panel * BR
    band = cols_ref[0, slot] - rows_ref[0, slot] + HB
    band = jnp.where(band < 0, band + nblocks, band)
    band = jnp.where(band >= nblocks, band - nblocks, band)
    odd = panel % 2 == 1
    return row, jnp.where(odd, BR - 1 - row, row), jnp.where(odd, WIDTH - 1 - band, band)


def index_copies(hbm_refs, smem_refs, sems):
    return [pltpu.make_async_copy(a, b, sems.at[i]) for i, (a, b) in enumerate(zip(hbm_refs, smem_refs))]


def pack_kernel(nblocks, slots, rows_ref, cols_ref, values_ref, *rest):
    out_refs = dict(zip("abcd", rest[:4]))
    left_ref, held, table, *index, sems, value_sem = rest[4:]
    copies = index_copies((rows_ref, cols_ref), index, sems)
    load = pltpu.make_async_copy(values_ref.at[0], held.at[pl.ds(0, slots)], value_sem)
    for copy in (*copies, load):
        copy.start()
    held[slots] = jnp.zeros((BLK, BLK), held.dtype)
    for i in range(BR * WIDTH + 1):
        table[i] = slots
    for copy in copies:
        copy.wait()
    for m in reversed(range(slots)):
        real_row, row, band = slot_position(*index, m, nblocks)
        table[jnp.where(real_row >= 0, row * WIDTH + band, BR * WIDTH)] = m
    load.wait()

    @for_own_parity
    def _(mine):
        for name, ref in out_refs.items():
            distance = DISTANCES[name]
            for n, (k, j) in enumerate(SENT[name, (mine + distance) % 2]):
                at = (k - BR * distance) * WIDTH + j - k + HB
                if distance % 2 == 1:
                    at = BR * WIDTH - 1 - at
                ref[n] = held[table[at]]
        columns = columns_of(mine)
        for i in range(BR):
            for n in range(NCOL):
                rows, cols = pl.ds(i * BLK, BLK), pl.ds(n * BLK, BLK)
                if n < len(columns) and abs(columns[n] - i) <= HB:
                    left_ref[rows, cols] = held[table[i * WIDTH + columns[n] - i + HB]]
                else:
                    left_ref[rows, cols] = jnp.zeros((BLK, BLK), left_ref.dtype)


def find_block(parity, k, j):
    if abs(k - j) > HB:
        return None
    if 0 <= k < BR:
        return ("left", parity == j % 2), (k, columns_of(j % 2).index(j)), False
    if 0 <= j < BR:
        return ("left", parity == k % 2), (j, columns_of(k % 2).index(k)), True
    for a, b, flip in ((k, j, False), (j, k, True)):
        for name in DISTANCES:
            if (a, b) in SENT[name, parity]:
                return name, SENT[name, parity].index((a, b)), flip
        for part in PARTS:
            staged = [position for _, _, position in STAGED[part, 1 - parity]]
            if (a, b) in staged:
                n = staged.index((a, b))
                if part == "early":
                    return part, n, not flip
                return ("late", n, flip) if n < BOTH_WAYS else ("last", n - BOTH_WAYS, flip)
    raise AssertionError((k, j))


def columns_product(refs, right, parity, js, wanted):
    total = None
    for own in (True, False):
        kind = parity if own else 1 - parity
        found = {}
        for k in columns_of(kind):
            for j in js:
                place = find_block(parity, k, j)
                if place is not None and place[0] in wanted:
                    found[k, j] = place
        if not found:
            continue
        first, last = min(k for k, _ in found), max(k for k, _ in found)
        ks = [k for k in columns_of(kind) if first <= k <= last]
        side = right.at[0 if own else 1]
        for x, k in enumerate(ks):
            for y, j in enumerate(js):
                if (k, j) in found:
                    source, place, flip = found[k, j]
                    if isinstance(place, tuple):
                        block = refs[source][pl.ds(place[0] * BLK, BLK), pl.ds(place[1] * BLK, BLK)]
                    else:
                        block = refs[source][place]
                    block = block.T if flip else block
                else:
                    block = jnp.zeros((BLK, BLK), right.dtype)
                side[pl.ds(x * BLK, BLK), pl.ds(y * BLK, BLK)] = block
        start = columns_of(kind).index(first)
        part = jnp.dot(
            refs["left", own][:, pl.ds(start * BLK, len(ks) * BLK)],
            side[pl.ds(0, len(ks) * BLK), pl.ds(0, len(js) * BLK)],
            preferred_element_type=jnp.float32,
        )
        total = part if total is None else total + part
    return total


LEFT = (("left", True), ("left", False))


def block_of(total, i, y):
    return total[i * BLK : (i + 1) * BLK, y * BLK : (y + 1) * BLK]


def stored_places(parity):
    columns = columns_of(parity)
    return [i * NCOL + n for i in range(BR) for n, j in enumerate(columns) if abs(i - j) <= HB]


def inner_places(parity):
    return [i * NCOL + n for i in range(BR) for n, j in enumerate(columns_of(parity)) if 0 <= j < BR]


def store(made, table, out_ref, place, sem):
    source = made.at[table[0, SOURCES + place]]
    pltpu.make_async_copy(source, out_ref.at[0, table[0, place]], sem).start()


def wait_for(count, made, out_ref, sem):
    pltpu.make_async_copy(made.at[pl.ds(0, count)], out_ref.at[0, pl.ds(0, count)], sem).wait()


def outer_pairs(parity):
    outer = [j for j in columns_of(parity) if not 0 <= j < BR]
    return [outer[n : n + 2] for n in range(0, len(outer), 2)]


def inner_kernel(nblocks, slots, rows_ref, cols_ref, counts_ref, left_ref, left_other_ref, *rest):
    table, out_ref, right, made, *index, sems, out_sem = rest
    copies = index_copies((rows_ref, cols_ref), index, sems)
    for copy in copies:
        copy.start()
    refs = {("left", True): left_ref, ("left", False): left_other_ref}

    @for_own_parity
    def _(mine):
        js = [j for j in columns_of(mine) if 0 <= j < BR]
        total = columns_product(refs, right, mine, js, LEFT)
        for i in range(BR):
            for y in range(2):
                if y < len(js):
                    made[i * NCOL + columns_of(mine).index(js[y])] = block_of(total, i, y)
        made[BR * NCOL] = jnp.zeros((BLK, BLK), made.dtype)

    for copy in copies:
        copy.wait()
    for place in range(BR * NCOL + 1):
        table[0, place] = -1
    count = counts_ref[0, 0]
    for m in range(slots):
        _, row, band = slot_position(*index, m, nblocks)
        table[0, jnp.where(m < count, row * NCOL + (row + band) // 2, BR * NCOL)] = m

    @for_own_parity
    def _(mine):
        unused = count
        for place in stored_places(mine):
            slot = table[0, place]
            absent = slot < 0
            table[0, place] = jnp.where(absent, unused, slot)
            table[0, SOURCES + place] = jnp.where(absent, BR * NCOL, place)
            unused = jnp.where(absent, unused + 1, unused)
        table[0, BR * NCOL] = unused
        here = [place for place in stored_places(mine) if place in inner_places(mine)]
        for place in here:
            store(made, table, out_ref, place, out_sem)
        stored = len(here)
        if len(stored_places(mine)) < slots:
            pltpu.make_async_copy(made.at[BR * NCOL], out_ref.at[0, unused], out_sem).start()
            stored += 1
        wait_for(stored, made, out_ref, out_sem)


def pack_e_kernel(left_ref, left_other_ref, e_ref):
    @for_own_parity
    def _(mine):
        i = 2 if mine == 0 else 0
        n = columns_of(0).index(i)
        e_ref[0] = (left_ref if mine == 0 else left_other_ref)[pl.ds(i * BLK, BLK), pl.ds(n * BLK, BLK)]


def stage_kernel(part, *refs):
    got = dict(zip(PARTS[part], refs))
    out_ref = refs[-1]

    @for_own_parity
    def _(mine):
        staged = STAGED[part, mine]
        for n, (name, place, _) in enumerate(staged):
            out_ref[n] = got[name][place] if part == "late" else got[name][place].T
        for n in range(len(staged), STAGED_SIZE[part]):
            out_ref[n] = jnp.zeros((BLK, BLK), out_ref.dtype)


def late_columns(parity):
    found = [[find_block(parity, k, j) for k in range(LOW, HIGH + 1)] for j in columns_of(parity)]
    return [j for j, blocks in zip(columns_of(parity), found) if any(b is not None and b[0] in ("late", "last") for b in blocks)]


def late_pairs(parity):
    near = [j for j in late_columns(parity) if -BR <= j < 0]
    rest = [j for j in late_columns(parity) if j not in near]
    return [js[n : n + 2] for js in (near, rest) for n in range(0, len(js), 2)]


def stage_late_kernel(b_ref, d_ref, e_ref, out_ref, last_ref):
    got = {"b": b_ref, "d": d_ref, "e": e_ref}

    @for_own_parity
    def _(mine):
        staged = STAGED["late", mine]
        for n in range(STAGED_SIZE["late"]):
            ref, at = (out_ref, n) if n < BOTH_WAYS else (last_ref, n - BOTH_WAYS)
            ref[at] = got[staged[n][0]][staged[n][1]] if n < len(staged) else jnp.zeros((BLK, BLK), ref.dtype)


def add_columns(refs, wanted, old_ref, new_ref, right, mine, pairs=outer_pairs):
    for pair, js in enumerate(pairs(mine)):
        total = columns_product(refs, right.at[pair], mine, js, wanted)
        for i in range(BR):
            for y, j in enumerate(js):
                if abs(i - j) <= HB:
                    place = i * NCOL + columns_of(mine).index(j)
                    terms = [] if old_ref is None else [old_ref[place]]
                    terms += [] if total is None else [block_of(total, i, y)]
                    new_ref[place] = functools.reduce(jnp.add, terms)


def early_kernel(left_ref, left_other_ref, a_ref, c_ref, out_ref, right):
    refs = {("left", True): left_ref, ("left", False): left_other_ref, "a": a_ref, "c": c_ref}
    for_own_parity(functools.partial(add_columns, refs, (*LEFT, "a", "c"), None, out_ref, right))


def late_kernel(left_ref, left_other_ref, b_ref, d_ref, e_ref, old_ref, out_ref, right):
    refs = {("left", True): left_ref, ("left", False): left_other_ref, "b": b_ref, "d": d_ref, "e": e_ref}
    for_own_parity(functools.partial(add_columns, refs, ("b", "d", "e"), old_ref, out_ref, right))


def staged_early_kernel(left_ref, left_other_ref, staged_ref, old_ref, out_ref, right):
    refs = {("left", True): left_ref, ("left", False): left_other_ref, "early": staged_ref}
    for_own_parity(functools.partial(add_columns, refs, ("early",), old_ref, out_ref, right))
    out_ref[BR * NCOL] = jnp.zeros((BLK, BLK), out_ref.dtype)


def multiply_kernel(left_ref, left_other_ref, late_ref, last_ref, old_ref, table, _, out_ref, *rest):
    right, made, out_sem = rest
    refs = {("left", True): left_ref, ("left", False): left_other_ref, "late": late_ref, "last": last_ref}
    made[BR * NCOL] = jnp.zeros((BLK, BLK), made.dtype)

    @for_own_parity
    def _(mine):
        here = [place for place in stored_places(mine) if place not in inner_places(mine)]
        late = [columns_of(mine).index(j) for j in late_columns(mine)]
        for place in here:
            if place % NCOL not in late:
                store(old_ref, table, out_ref, place, out_sem)
        add_columns(refs, ("late", "last"), old_ref, made, right, mine, late_pairs)
        for place in here:
            if place % NCOL in late:
                store(made, table, out_ref, place, out_sem)
        wait_for(len(here), made, out_ref, out_sem)


def local(values, block_rows, block_cols, counts):
    slots = values.shape[1]
    row_count, col_count = lax.axis_size("row"), lax.axis_size("col")
    nblocks = BR * row_count
    smem = pl.BlockSpec(memory_space=pltpu.SMEM)
    vmem = pl.BlockSpec(memory_space=pltpu.VMEM)
    hbm = pl.BlockSpec(memory_space=pltpu.HBM)
    params = pltpu.CompilerParams(vmem_limit_bytes=VMEM_LIMIT)
    values, *places = (pltpu.with_memory_space_constraint(x, pltpu.HBM) for x in (values, block_rows, block_cols))
    index_scratch = [
        pltpu.SMEM((1, slots), jnp.int32),
        pltpu.SMEM((1, slots), jnp.int32),
        pltpu.SemaphoreType.DMA((2,)),
    ]
    table_shape = (1, BLK)

    def blocks(count, dtype=values.dtype):
        return jax.ShapeDtypeStruct((count, BLK, BLK), dtype)

    def cost(products, nbytes):
        return pl.CostEstimate(flops=2 * products * BLK**3, bytes_accessed=nbytes, transcendentals=0)

    def right_scratch(pairs):
        return pltpu.VMEM((pairs, 2, NCOL * BLK, 2 * BLK), values.dtype)

    *packed, left = pl.pallas_call(
        functools.partial(pack_kernel, nblocks, slots),
        out_shape=[blocks(SIZES[name]) for name in "abcd"]
        + [jax.ShapeDtypeStruct((BR * BLK, NCOL * BLK), values.dtype)],
        in_specs=[hbm] * 3,
        out_specs=[vmem] * 5,
        scratch_shapes=[
            pltpu.VMEM((slots + 1, BLK, BLK), values.dtype),
            pltpu.SMEM((BR * WIDTH + 1,), jnp.int32),
            *index_scratch,
            pltpu.SemaphoreType.DMA,
        ],
        compiler_params=params,
        name="pack",
    )(*places, values)

    def towards(name, message):
        pairs = []
        for r in range(row_count):
            for c in range(col_count):
                distance = DISTANCES[name] or (3 if (r + c) % 2 == 1 else -3)
                source = (r - distance if r % 2 == 1 else r + distance) % row_count
                pairs.append((source * col_count + c, r * col_count + c))
        return lax.ppermute(message, ("row", "col"), pairs)

    def swapped(block):
        return lax.ppermute(block, "col", [(0, 1), (1, 0)])

    left_other = swapped(left)
    got = [towards(name, message) for name, message in zip("abcd", packed)]
    message = pl.pallas_call(
        pack_e_kernel,
        out_shape=blocks(SIZES["e"]),
        in_specs=[vmem] * 2,
        out_specs=vmem,
        compiler_params=params,
        name="pack_e",
    )(left, left_other)
    got.append(towards("e", message))
    table, out = pl.pallas_call(
        functools.partial(inner_kernel, nblocks, slots),
        out_shape=[pltpu.SMEM(table_shape, jnp.int32), jax.ShapeDtypeStruct(values.shape, jnp.float32)],
        in_specs=[hbm] * 2 + [smem] + [vmem] * 2,
        out_specs=[smem, hbm],
        scratch_shapes=[
            pltpu.VMEM((2, NCOL * BLK, 2 * BLK), values.dtype),
            pltpu.VMEM((BR * NCOL + 1, BLK, BLK), jnp.float32),
            *index_scratch,
            pltpu.SemaphoreType.DMA,
        ],
        compiler_params=params,
        cost_estimate=cost(3 * 2 * 17, 4 * values.size),
        name="inner",
    )(*places, counts, left, left_other)
    a, b, c, d, e = got

    def staged(part, arrays):
        return swapped(
            pl.pallas_call(
                functools.partial(stage_kernel, part),
                out_shape=blocks(STAGED_SIZE[part]),
                in_specs=[vmem] * len(arrays),
                out_specs=vmem,
                compiler_params=params,
                name="stage_" + part,
            )(*arrays)
        )

    def added(kernel, name, products, arrays):
        return pl.pallas_call(
            kernel,
            out_shape=blocks(BR * NCOL + 1, jnp.float32),
            in_specs=[vmem] * len(arrays),
            out_specs=vmem,
            scratch_shapes=[right_scratch(4)],
            compiler_params=params,
            cost_estimate=cost(products, 0),
            name=name,
        )(*arrays)

    a, c, table = lax.optimization_barrier((a, c, table))
    staged_early = staged("early", (a, c))
    total = added(early_kernel, "early", EARLY_COST, (left, left_other, a, c))
    b, d, e, total = lax.optimization_barrier((b, d, e, total))
    staged_late, staged_last = pl.pallas_call(
        stage_late_kernel,
        out_shape=[blocks(BOTH_WAYS), blocks(STAGED_SIZE["late"] - BOTH_WAYS)],
        in_specs=[vmem] * 3,
        out_specs=[vmem] * 2,
        compiler_params=params,
        name="stage_late",
    )(b, d, e)
    one_way = [(r * col_count + r % 2, r * col_count + 1 - r % 2) for r in range(row_count)]
    staged_late = swapped(staged_late)
    staged_last = lax.ppermute(staged_last, ("row", "col"), one_way)
    total = added(late_kernel, "late", LATE_COST, (left, left_other, b, d, e, total))
    total = added(staged_early_kernel, "staged_early", EARLY_COST, (left, left_other, staged_early, total))
    return pl.pallas_call(
        multiply_kernel,
        out_shape=jax.ShapeDtypeStruct(values.shape, jnp.float32),
        in_specs=[vmem] * 5 + [smem, hbm],
        out_specs=hbm,
        scratch_shapes=[
            right_scratch(4),
            pltpu.VMEM((BR * NCOL + 1, BLK, BLK), jnp.float32),
            pltpu.SemaphoreType.DMA,
        ],
        input_output_aliases={6: 0},
        compiler_params=params,
        name="multiply",
    )(left, left_other, staged_late, staged_last, total, pltpu.with_memory_space_constraint(table, pltpu.SMEM), out)


def solution(mesh):
    return jax.shard_map(
        local,
        mesh=mesh,
        in_specs=(
            P(("parts", "row"), "col", None, None),
            P(("parts", "row"), "col"),
            P(("parts", "row"), "col"),
            P(("parts", "row"), "col"),
        ),
        out_specs=P(("parts", "row"), "col", None, None),
        check_vma=False,
    )
```

```python
import functools

import jax
import jax.numpy as jnp
from jax import lax
from jax.experimental import pallas as pl
from jax.experimental.pallas import tpu as pltpu
from jax.sharding import PartitionSpec as P

BLK = 128
BR = 3
HB = 7
WIDTH = 2 * HB + 1
LOW, HIGH = -HB, BR - 1 + HB
NCOL = 9
SOURCES = 32
EARLY_COST = 1
LATE_COST = 4000
VMEM_LIMIT = 12 * 2**20

DISTANCES = {"a": 1, "b": -1, "c": -2, "d": 2, "e": None}
SENT = {
    ("a", 1): [(3, 3), (5, 5), (3, 5), (3, 7), (4, 7), (5, 7), (3, 9), (4, 9), (5, 9), (3, -3), (3, -1), (4, -3), (5, -1)],
    ("a", 0): [(4, 4), (3, 4), (5, 4), (3, 6), (4, 6), (5, 6), (3, 8), (4, 8), (5, 8), (3, -2), (4, -2), (5, -2), (3, -4)],
    ("b", 1): [(-1, -1), (-3, -3), (-1, -3), (-1, -7), (-2, -7), (-3, -7)],
    ("b", 0): [(-2, -2), (-1, -2), (-3, -2), (-1, 4), (-1, -4), (-1, -6)],
    ("c", 1): [(-5, -5), (-4, -7), (-5, -7), (-6, -7), (-4, -3), (-5, -1), (-5, -3), (-6, -3)],
    ("c", 0): [(-4, -4), (-6, -6), (-4, -6), (-4, -2), (-5, -2), (-6, -2), (-5, -4), (-5, -6)],
    ("d", 1): [(6, 9), (7, 7), (7, 9), (8, 9), (6, -1)],
    ("d", 0): [(6, 6), (6, 8), (8, 8), (7, 6), (7, 8)],
    ("e", 1): [(9, 9)],
    ("e", 0): [(-7, -7)],
}
SIZES = {name: len(SENT[name, 1]) for name in DISTANCES}
PARTS = {"early": "ac", "late": "bde"}
STAGED = {
    (part, parity): [
        (name, n, (k, j))
        for name in names
        for n, (k, j) in enumerate(SENT[name, parity])
        if k % 2 != j % 2 or (k, j) == (-7, -7)
    ]
    for part, names in PARTS.items()
    for parity in (0, 1)
}
STAGED_SIZE = {part: max(len(STAGED[part, parity]) for parity in (0, 1)) for part in PARTS}


def columns_of(parity):
    return [j for j in range(LOW, HIGH + 1) if j % 2 == parity]


def own_parity():
    return (lax.axis_index("row") + lax.axis_index("col")) % 2


def for_own_parity(body):
    parity = own_parity()
    for mine in (0, 1):
        pl.when(parity == mine)(functools.partial(body, mine))


def slot_position(rows_ref, cols_ref, slot, nblocks):
    panel = lax.axis_index("row")
    row = rows_ref[0, slot] - panel * BR
    band = cols_ref[0, slot] - rows_ref[0, slot] + HB
    band = jnp.where(band < 0, band + nblocks, band)
    band = jnp.where(band >= nblocks, band - nblocks, band)
    odd = panel % 2 == 1
    return row, jnp.where(odd, BR - 1 - row, row), jnp.where(odd, WIDTH - 1 - band, band)


def index_copies(hbm_refs, smem_refs, sems):
    return [pltpu.make_async_copy(a, b, sems.at[i]) for i, (a, b) in enumerate(zip(hbm_refs, smem_refs))]


def pack_kernel(nblocks, slots, rows_ref, cols_ref, values_ref, *rest):
    out_refs = dict(zip("abcd", rest[:4]))
    left_ref, held, table, *index, sems, value_sem = rest[4:]
    copies = index_copies((rows_ref, cols_ref), index, sems)
    load = pltpu.make_async_copy(values_ref.at[0], held.at[pl.ds(0, slots)], value_sem)
    for copy in (*copies, load):
        copy.start()
    held[slots] = jnp.zeros((BLK, BLK), held.dtype)
    for i in range(BR * WIDTH + 1):
        table[i] = slots
    for copy in copies:
        copy.wait()
    for m in reversed(range(slots)):
        real_row, row, band = slot_position(*index, m, nblocks)
        table[jnp.where(real_row >= 0, row * WIDTH + band, BR * WIDTH)] = m
    load.wait()

    @for_own_parity
    def _(mine):
        for name, ref in out_refs.items():
            distance = DISTANCES[name]
            for n, (k, j) in enumerate(SENT[name, (mine + distance) % 2]):
                at = (k - BR * distance) * WIDTH + j - k + HB
                if distance % 2 == 1:
                    at = BR * WIDTH - 1 - at
                ref[n] = held[table[at]]
        columns = columns_of(mine)
        for i in range(BR):
            for n in range(NCOL):
                rows, cols = pl.ds(i * BLK, BLK), pl.ds(n * BLK, BLK)
                if n < len(columns) and abs(columns[n] - i) <= HB:
                    left_ref[rows, cols] = held[table[i * WIDTH + columns[n] - i + HB]]
                else:
                    left_ref[rows, cols] = jnp.zeros((BLK, BLK), left_ref.dtype)


def find_block(parity, k, j):
    if abs(k - j) > HB:
        return None
    if 0 <= k < BR:
        return ("left", parity == j % 2), (k, columns_of(j % 2).index(j)), False
    if 0 <= j < BR:
        return ("left", parity == k % 2), (j, columns_of(k % 2).index(k)), True
    for a, b, flip in ((k, j, False), (j, k, True)):
        for name in DISTANCES:
            if (a, b) in SENT[name, parity]:
                return name, SENT[name, parity].index((a, b)), flip
        for part in PARTS:
            staged = [position for _, _, position in STAGED[part, 1 - parity]]
            if (a, b) in staged:
                return part, staged.index((a, b)), flip if part == "late" else not flip
    raise AssertionError((k, j))


def columns_product(refs, right, parity, js, wanted):
    total = None
    for own in (True, False):
        kind = parity if own else 1 - parity
        found = {}
        for k in columns_of(kind):
            for j in js:
                place = find_block(parity, k, j)
                if place is not None and place[0] in wanted:
                    found[k, j] = place
        if not found:
            continue
        first, last = min(k for k, _ in found), max(k for k, _ in found)
        ks = [k for k in columns_of(kind) if first <= k <= last]
        side = right.at[0 if own else 1]
        for x, k in enumerate(ks):
            for y, j in enumerate(js):
                if (k, j) in found:
                    source, place, flip = found[k, j]
                    if isinstance(place, tuple):
                        block = refs[source][pl.ds(place[0] * BLK, BLK), pl.ds(place[1] * BLK, BLK)]
                    else:
                        block = refs[source][place]
                    block = block.T if flip else block
                else:
                    block = jnp.zeros((BLK, BLK), right.dtype)
                side[pl.ds(x * BLK, BLK), pl.ds(y * BLK, BLK)] = block
        start = columns_of(kind).index(first)
        part = jnp.dot(
            refs["left", own][:, pl.ds(start * BLK, len(ks) * BLK)],
            side[pl.ds(0, len(ks) * BLK), pl.ds(0, len(js) * BLK)],
            preferred_element_type=jnp.float32,
        )
        total = part if total is None else total + part
    return total


LEFT = (("left", True), ("left", False))


def block_of(total, i, y):
    return total[i * BLK : (i + 1) * BLK, y * BLK : (y + 1) * BLK]


def stored_places(parity):
    columns = columns_of(parity)
    return [i * NCOL + n for i in range(BR) for n, j in enumerate(columns) if abs(i - j) <= HB]


def inner_places(parity):
    return [i * NCOL + n for i in range(BR) for n, j in enumerate(columns_of(parity)) if 0 <= j < BR]


def store(made, table, out_ref, place, sem):
    source = made.at[table[0, SOURCES + place]]
    pltpu.make_async_copy(source, out_ref.at[0, table[0, place]], sem).start()


def wait_for(count, made, out_ref, sem):
    pltpu.make_async_copy(made.at[pl.ds(0, count)], out_ref.at[0, pl.ds(0, count)], sem).wait()


def outer_pairs(parity):
    outer = [j for j in columns_of(parity) if not 0 <= j < BR]
    return [outer[n : n + 2] for n in range(0, len(outer), 2)]


def inner_kernel(nblocks, slots, rows_ref, cols_ref, counts_ref, left_ref, left_other_ref, *rest):
    table, out_ref, right, made, *index, sems, out_sem = rest
    copies = index_copies((rows_ref, cols_ref), index, sems)
    for copy in copies:
        copy.start()
    refs = {("left", True): left_ref, ("left", False): left_other_ref}

    @for_own_parity
    def _(mine):
        js = [j for j in columns_of(mine) if 0 <= j < BR]
        total = columns_product(refs, right, mine, js, LEFT)
        for i in range(BR):
            for y in range(2):
                if y < len(js):
                    made[i * NCOL + columns_of(mine).index(js[y])] = block_of(total, i, y)
        made[BR * NCOL] = jnp.zeros((BLK, BLK), made.dtype)

    for copy in copies:
        copy.wait()
    for place in range(BR * NCOL + 1):
        table[0, place] = -1
    count = counts_ref[0, 0]
    for m in range(slots):
        _, row, band = slot_position(*index, m, nblocks)
        table[0, jnp.where(m < count, row * NCOL + (row + band) // 2, BR * NCOL)] = m

    @for_own_parity
    def _(mine):
        unused = count
        for place in stored_places(mine):
            slot = table[0, place]
            absent = slot < 0
            table[0, place] = jnp.where(absent, unused, slot)
            table[0, SOURCES + place] = jnp.where(absent, BR * NCOL, place)
            unused = jnp.where(absent, unused + 1, unused)
        table[0, BR * NCOL] = unused
        here = [place for place in stored_places(mine) if place in inner_places(mine)]
        for place in here:
            store(made, table, out_ref, place, out_sem)
        stored = len(here)
        if len(stored_places(mine)) < slots:
            pltpu.make_async_copy(made.at[BR * NCOL], out_ref.at[0, unused], out_sem).start()
            stored += 1
        wait_for(stored, made, out_ref, out_sem)


def pack_e_kernel(left_ref, left_other_ref, e_ref):
    @for_own_parity
    def _(mine):
        i = 2 if mine == 0 else 0
        n = columns_of(0).index(i)
        e_ref[0] = (left_ref if mine == 0 else left_other_ref)[pl.ds(i * BLK, BLK), pl.ds(n * BLK, BLK)]


def stage_kernel(part, *refs):
    got = dict(zip(PARTS[part], refs))
    out_ref = refs[-1]

    @for_own_parity
    def _(mine):
        staged = STAGED[part, mine]
        for n, (name, place, _) in enumerate(staged):
            out_ref[n] = got[name][place] if part == "late" else got[name][place].T
        for n in range(len(staged), STAGED_SIZE[part]):
            out_ref[n] = jnp.zeros((BLK, BLK), out_ref.dtype)


def late_columns(parity):
    found = [[find_block(parity, k, j) for k in range(LOW, HIGH + 1)] for j in columns_of(parity)]
    return [j for j, blocks in zip(columns_of(parity), found) if any(b is not None and b[0] == "late" for b in blocks)]


def late_pairs(parity):
    near = [j for j in late_columns(parity) if -BR <= j < 0]
    rest = [j for j in late_columns(parity) if j not in near]
    return [js[n : n + 2] for js in (near, rest) for n in range(0, len(js), 2)]


def add_columns(refs, wanted, old_ref, new_ref, right, mine, pairs=outer_pairs):
    for pair, js in enumerate(pairs(mine)):
        total = columns_product(refs, right.at[pair], mine, js, wanted)
        for i in range(BR):
            for y, j in enumerate(js):
                if abs(i - j) <= HB:
                    place = i * NCOL + columns_of(mine).index(j)
                    terms = [] if old_ref is None else [old_ref[place]]
                    terms += [] if total is None else [block_of(total, i, y)]
                    new_ref[place] = functools.reduce(jnp.add, terms)


def early_kernel(left_ref, left_other_ref, a_ref, c_ref, out_ref, right):
    refs = {("left", True): left_ref, ("left", False): left_other_ref, "a": a_ref, "c": c_ref}
    for_own_parity(functools.partial(add_columns, refs, (*LEFT, "a", "c"), None, out_ref, right))


def late_kernel(left_ref, left_other_ref, b_ref, d_ref, e_ref, old_ref, out_ref, right):
    refs = {("left", True): left_ref, ("left", False): left_other_ref, "b": b_ref, "d": d_ref, "e": e_ref}
    for_own_parity(functools.partial(add_columns, refs, ("b", "d", "e"), old_ref, out_ref, right))


def staged_early_kernel(left_ref, left_other_ref, staged_ref, old_ref, out_ref, right):
    refs = {("left", True): left_ref, ("left", False): left_other_ref, "early": staged_ref}
    for_own_parity(functools.partial(add_columns, refs, ("early",), old_ref, out_ref, right))
    out_ref[BR * NCOL] = jnp.zeros((BLK, BLK), out_ref.dtype)


def multiply_kernel(left_ref, left_other_ref, staged_ref, old_ref, table, _, out_ref, *rest):
    right, made, out_sem = rest
    refs = {("left", True): left_ref, ("left", False): left_other_ref, "late": staged_ref}
    made[BR * NCOL] = jnp.zeros((BLK, BLK), made.dtype)

    @for_own_parity
    def _(mine):
        here = [place for place in stored_places(mine) if place not in inner_places(mine)]
        late = [columns_of(mine).index(j) for j in late_columns(mine)]
        for place in here:
            if place % NCOL not in late:
                store(old_ref, table, out_ref, place, out_sem)
        for pair, js in enumerate(late_pairs(mine)):
            add_columns(refs, ("late",), old_ref, made, right.at[pl.ds(pair, 1)], mine, lambda parity, js=js: [js])
            for place in here:
                if place % NCOL in [columns_of(mine).index(j) for j in js]:
                    store(made, table, out_ref, place, out_sem)
        wait_for(len(here), made, out_ref, out_sem)


def local(values, block_rows, block_cols, counts):
    slots = values.shape[1]
    row_count, col_count = lax.axis_size("row"), lax.axis_size("col")
    nblocks = BR * row_count
    smem = pl.BlockSpec(memory_space=pltpu.SMEM)
    vmem = pl.BlockSpec(memory_space=pltpu.VMEM)
    hbm = pl.BlockSpec(memory_space=pltpu.HBM)
    params = pltpu.CompilerParams(vmem_limit_bytes=VMEM_LIMIT)
    values, *places = (pltpu.with_memory_space_constraint(x, pltpu.HBM) for x in (values, block_rows, block_cols))
    index_scratch = [
        pltpu.SMEM((1, slots), jnp.int32),
        pltpu.SMEM((1, slots), jnp.int32),
        pltpu.SemaphoreType.DMA((2,)),
    ]
    table_shape = (1, BLK)

    def blocks(count, dtype=values.dtype):
        return jax.ShapeDtypeStruct((count, BLK, BLK), dtype)

    def cost(products, nbytes):
        return pl.CostEstimate(flops=2 * products * BLK**3, bytes_accessed=nbytes, transcendentals=0)

    def right_scratch(pairs):
        return pltpu.VMEM((pairs, 2, NCOL * BLK, 2 * BLK), values.dtype)

    *packed, left = pl.pallas_call(
        functools.partial(pack_kernel, nblocks, slots),
        out_shape=[blocks(SIZES[name]) for name in "abcd"]
        + [jax.ShapeDtypeStruct((BR * BLK, NCOL * BLK), values.dtype)],
        in_specs=[hbm] * 3,
        out_specs=[vmem] * 5,
        scratch_shapes=[
            pltpu.VMEM((slots + 1, BLK, BLK), values.dtype),
            pltpu.SMEM((BR * WIDTH + 1,), jnp.int32),
            *index_scratch,
            pltpu.SemaphoreType.DMA,
        ],
        compiler_params=params,
        name="pack",
    )(*places, values)

    def towards(name, message):
        pairs = []
        for r in range(row_count):
            for c in range(col_count):
                distance = DISTANCES[name] or (3 if (r + c) % 2 == 1 else -3)
                source = (r - distance if r % 2 == 1 else r + distance) % row_count
                pairs.append((source * col_count + c, r * col_count + c))
        return lax.ppermute(message, ("row", "col"), pairs)

    def swapped(block):
        return lax.ppermute(block, "col", [(0, 1), (1, 0)])

    left_other = swapped(left)
    got = [towards(name, message) for name, message in zip("abcd", packed)]
    message = pl.pallas_call(
        pack_e_kernel,
        out_shape=blocks(SIZES["e"]),
        in_specs=[vmem] * 2,
        out_specs=vmem,
        compiler_params=params,
        name="pack_e",
    )(left, left_other)
    got.append(towards("e", message))
    table, out = pl.pallas_call(
        functools.partial(inner_kernel, nblocks, slots),
        out_shape=[pltpu.SMEM(table_shape, jnp.int32), jax.ShapeDtypeStruct(values.shape, jnp.float32)],
        in_specs=[hbm] * 2 + [smem] + [vmem] * 2,
        out_specs=[smem, hbm],
        scratch_shapes=[
            pltpu.VMEM((2, NCOL * BLK, 2 * BLK), values.dtype),
            pltpu.VMEM((BR * NCOL + 1, BLK, BLK), jnp.float32),
            *index_scratch,
            pltpu.SemaphoreType.DMA,
        ],
        compiler_params=params,
        cost_estimate=cost(3 * 2 * 17, 4 * values.size),
        name="inner",
    )(*places, counts, left, left_other)
    a, b, c, d, e = got

    def staged(part, arrays):
        return swapped(
            pl.pallas_call(
                functools.partial(stage_kernel, part),
                out_shape=blocks(STAGED_SIZE[part]),
                in_specs=[vmem] * len(arrays),
                out_specs=vmem,
                compiler_params=params,
                name="stage_" + part,
            )(*arrays)
        )

    def added(kernel, name, products, arrays):
        return pl.pallas_call(
            kernel,
            out_shape=blocks(BR * NCOL + 1, jnp.float32),
            in_specs=[vmem] * len(arrays),
            out_specs=vmem,
            scratch_shapes=[right_scratch(4)],
            compiler_params=params,
            cost_estimate=cost(products, 0),
            name=name,
        )(*arrays)

    a, c, table = lax.optimization_barrier((a, c, table))
    staged_early = staged("early", (a, c))
    total = added(early_kernel, "early", EARLY_COST, (left, left_other, a, c))
    b, d, e, total = lax.optimization_barrier((b, d, e, total))
    staged_late = staged("late", (b, d, e))
    total = added(late_kernel, "late", LATE_COST, (left, left_other, b, d, e, total))
    total = added(staged_early_kernel, "staged_early", EARLY_COST, (left, left_other, staged_early, total))
    return pl.pallas_call(
        multiply_kernel,
        out_shape=jax.ShapeDtypeStruct(values.shape, jnp.float32),
        in_specs=[vmem] * 4 + [smem, hbm],
        out_specs=hbm,
        scratch_shapes=[
            right_scratch(4),
            pltpu.VMEM((BR * NCOL + 1, BLK, BLK), jnp.float32),
            pltpu.SemaphoreType.DMA,
        ],
        input_output_aliases={5: 0},
        compiler_params=params,
        name="multiply",
    )(left, left_other, staged_late, total, pltpu.with_memory_space_constraint(table, pltpu.SMEM), out)


def solution(mesh):
    return jax.shard_map(
        local,
        mesh=mesh,
        in_specs=(
            P(("parts", "row"), "col", None, None),
            P(("parts", "row"), "col"),
            P(("parts", "row"), "col"),
            P(("parts", "row"), "col"),
        ),
        out_specs=P(("parts", "row"), "col", None, None),
        check_vma=False,
    )
```
